128 devices in a mesh: lat: 4 (over x_hi, core), lon: 32 (over y, x_lo, z).
Axes of the slice: x: 4 (x_hi: 2, x_lo: 2; x = x_hi * 2 + x_lo), y: 4, z: 4, core: 2. Of those that a mesh axis runs over, the one named last changes fastest.
Arguments:
- encoded: bfloat16 [2, 24, 512, 384], P(None, 'lat', 'lon'), may hold values from -6 to 6
- upstream: bfloat16 [2, 24, 384, 512], P(None, 'lat', 'lon'), may hold values from -6 to 6
- w_qkv: bfloat16 [2, 512, 1536], replicated, may hold values from -0.25 to 0.25
- w_proj: bfloat16 [2, 512, 512], replicated, may hold values from -0.25 to 0.25
- w_up: bfloat16 [2, 512, 2048], replicated, may hold values from -0.25 to 0.25
- w_down: bfloat16 [2, 2048, 512], replicated, may hold values from -0.125 to 0.125
Outputs:
- mixed: bfloat16 [2, 24, 384, 512], P(None, 'lat', 'lon')
- grad_tokens: bfloat16 [2, 24, 512, 384], P(None, 'lat', 'lon')
- grad_qkv: float32 [2, 512, 1536], P(None, None, ('lat', 'lon'))
- grad_proj: float32 [2, 512, 512], P(None, None, ('lat', 'lon'))
- grad_up: float32 [2, 512, 2048], P(None, None, ('lat', 'lon'))
- grad_down: float32 [2, 2048, 512], P(None, None, ('lat', 'lon'))
The draws below stay inside these ranges and needn't reach their ends.
All inputs are finite; a program needn't handle non-finite values.
Results may differ from the reference program's by a relative error of at most 0.024.
Values may be sent and summed in bfloat16 or wider, within the bound.
A program may use at most 192 MiB of HBM per device.

```python
import jax
import jax.numpy as jnp
from jax import lax

C = 512
HEADS = 16
FF = 2048
LEV = 2
WLAT = 6
WLON = 12
NLAT = 24
NLON = 384


def with_spikes(values, key, source, target, parts, factor):
    owner, partner = [(jnp.arange(values.shape[axis_at]) // (values.shape[axis_at] // parts)).reshape([-1 if axis == axis_at else 1 for axis in range(values.ndim)]) for axis_at in (source, target)]
    chosen = jax.random.permutation(key, parts)[partner]
    strong = (owner == chosen) | (owner == (partner + parts // 2) % parts)
    return jnp.where(strong, factor * values, values)


def steps_of(rng, dims, cuts, least, top_value):
    gain = 1.0
    for dim, blocks in cuts:
        steps = jax.random.uniform(jax.random.fold_in(jax.random.fold_in(rng, 6), dim), (blocks,), jnp.float32, least / len(cuts), top_value / len(cuts))
        gain = gain * jnp.repeat(jnp.exp(steps), dims[dim] // blocks).reshape((-1,) + (1,) * (len(dims) - 1 - dim))
    return gain


def scatter_about(key, shape, deviation, reach, pieces=(), held_as=jnp.bfloat16):
    array = jax.random.normal(key, shape, jnp.float32) * deviation
    if len(pieces) > 0:
        array = steps_of(key, shape, pieces, -0.22, 0.18) * array
    return jnp.clip(array, min=-reach, max=reach).astype(held_as)


def noise_with(rng, shape, deviation, limit, cuts, heavy, kind=jnp.bfloat16):
    values = deviation * jax.random.normal(rng, shape, jnp.float32)
    if cuts:
        values = values * steps_of(rng, shape, cuts, -0.22, 0.18)
    return jnp.clip(with_spikes(values, jax.random.fold_in(rng, 3), *heavy), -limit, limit).astype(kind)


def setup_inputs(seed: int = 0) -> dict:
    splits = jax.random.split(jax.random.key(seed), 7)
    return {
        "encoded": scatter_about(splits[0], (LEV, NLAT, C, NLON), 1.0, 6.0, ((1, 4), (2, 32))),
        "upstream": noise_with(splits[1], (LEV, NLAT, NLON, C), 1.0, 6.0, ((1, 4), (2, 32)), (2, 3, 32, 2.75)),
        "w_qkv": scatter_about(splits[2], (2, C, 3 * C), C ** -0.5, 0.25),
        "w_proj": scatter_about(splits[3], (2, C, C), C ** -0.5, 0.25),
        "w_up": scatter_about(splits[4], (2, C, FF), C ** -0.5, 0.25),
        "w_down": scatter_about(splits[5], (2, FF, C), FF ** -0.5, 0.125),
    }


NORM_EPS = 1e-05

def layer_norm(features):
    average = lax.optimization_barrier(jnp.mean(features, -1, keepdims=True))
    centred = features - average
    variance = lax.optimization_barrier(jnp.mean(centred * centred, -1, keepdims=True))
    return centred * lax.rsqrt(variance + NORM_EPS)

def product(pattern, former, latter):
    return jnp.einsum(pattern, former.astype(jnp.float32), latter.astype(jnp.float32), precision=lax.Precision.HIGHEST)

def window_block(tokens, extras, layer, pair_mask):
    w_qkv, w_proj, w_up, w_down = layer
    groups, window_len, channels = tokens.shape
    head_size = channels // HEADS
    normed = layer_norm(tokens).astype(jnp.bfloat16)
    projected = (product('gtc,cd->gtd', normed, w_qkv) + extras[0]).astype(jnp.bfloat16)
    queries = projected[..., :channels].reshape(groups, window_len, HEADS, head_size)
    key_vecs = projected[..., channels:2 * channels].reshape(groups, window_len, HEADS, head_size)
    value_vecs = projected[..., 2 * channels:].reshape(groups, window_len, HEADS, head_size)
    scores = product('gthd,gshd->ghts', queries, key_vecs) * head_size ** (-0.5)
    exped = jnp.exp(scores) * pair_mask[:, None]
    probabilities = (exped / lax.optimization_barrier(jnp.sum(exped, -1, keepdims=True))).astype(jnp.bfloat16)
    attended = product('ghts,gshd->gthd', probabilities, value_vecs)
    attended = attended.reshape(groups, window_len, channels).astype(jnp.bfloat16)
    middle = tokens + product('gtc,cd->gtd', attended, w_proj) + extras[1]
    normed_two = layer_norm(middle).astype(jnp.bfloat16)
    hidden = jax.nn.gelu(product('gtc,cf->gtf', normed_two, w_up) + extras[2], approximate=False).astype(jnp.bfloat16)
    result = middle + product('gtf,fc->gtc', hidden, w_down) + extras[3]
    return (result, (normed, attended, normed_two, hidden))

def make_extras(tokens, layer):
    groups, window_len, channels = tokens.shape
    hidden_units = layer[2].shape[1]
    return (jnp.zeros((groups, window_len, 3 * channels), jnp.float32), jnp.zeros((groups, window_len, channels), jnp.float32), jnp.zeros((groups, window_len, hidden_units), jnp.float32), jnp.zeros((groups, window_len, channels), jnp.float32))

def weight_grads(saved, extras_ct):
    return tuple((product('gtc,gtd->cd', saved[index], extras_ct[index].astype(jnp.bfloat16)) for index in range(4)))

def to_windows(grid):
    levels, rows, cols, depth = grid.shape
    split = grid.reshape(levels, rows // WLAT, WLAT, cols // WLON, WLON, depth)
    split = split.transpose(1, 3, 0, 2, 4, 5)
    return split.reshape(rows // WLAT * (cols // WLON), levels * WLAT * WLON, depth)

def from_windows(blocks, levels, rows, cols):
    depth = blocks.shape[-1]
    split = blocks.reshape(rows // WLAT, cols // WLON, levels, WLAT, WLON, depth)
    return split.transpose(2, 0, 3, 1, 4, 5).reshape(levels, rows, cols, depth)

def window_mask(row_ids, total_rows, levels, cols, shifted):
    if shifted:
        labels = jnp.where(row_ids < total_rows - WLAT, 0.0, jnp.where(row_ids < total_rows - WLAT // 2, 1.0, 2.0))
    else:
        labels = jnp.zeros(row_ids.shape, jnp.float32)
    label_grid = jnp.broadcast_to(labels.astype(jnp.float32)[None, :, None, None], (levels, row_ids.shape[0], cols, 1))
    flat = to_windows(label_grid)[..., 0]
    return (flat[:, :, None] == flat[:, None, :]).astype(jnp.float32)

def run_layer(grid, layer, masks):
    levels, rows, cols, channels = grid.shape
    blocks = to_windows(grid).reshape(rows // WLAT, cols // WLON, -1, channels)
    mask_rows = masks.reshape(rows // WLAT, cols // WLON, masks.shape[1], masks.shape[2])

    def one_row(item):
        return window_block(item[0], make_extras(item[0], layer), layer, item[1])[0]
    outputs = lax.map(one_row, (blocks, mask_rows))
    return from_windows(outputs.reshape(-1, outputs.shape[2], channels), levels, rows, cols)

def back_layer(grid, ct_grid, layer, masks):
    levels, rows, cols, channels = grid.shape
    blocks = to_windows(grid).reshape(rows // WLAT, cols // WLON, -1, channels)
    ct_blocks = to_windows(ct_grid).reshape(rows // WLAT, cols // WLON, -1, channels)
    mask_rows = masks.reshape(rows // WLAT, cols // WLON, masks.shape[1], masks.shape[2])

    def one_row(carry, item):
        tokens, cotangent, pair_mask = item

        def local(values_in, extras):
            return window_block(values_in, extras, layer, pair_mask)
        result, pullback, saved = jax.vjp(local, tokens, make_extras(tokens, layer), has_aux=True)
        d_tokens, extras_ct = pullback(cotangent)
        grads = weight_grads(saved, extras_ct)
        return (tuple((carry[index] + grads[index] for index in range(4))), d_tokens)
    start = tuple((jnp.zeros(matrix.shape, jnp.float32) for matrix in layer))
    totals, d_rows = lax.scan(one_row, start, (blocks, ct_blocks, mask_rows))
    return (from_windows(d_rows.reshape(-1, d_rows.shape[2], channels), levels, rows, cols), totals)

def reference(encoded, upstream, w_qkv, w_proj, w_up, w_down):
    grid = jnp.transpose(encoded, (0, 1, 3, 2))
    levels, rows, cols, channels = grid.shape
    row_ids = jnp.arange(rows, dtype=jnp.int32)
    plain_mask = window_mask(row_ids, rows, levels, cols, False)
    shift_mask = window_mask(row_ids, rows, levels, cols, True)
    layer_one = (w_qkv[0], w_proj[0], w_up[0], w_down[0])
    layer_two = (w_qkv[1], w_proj[1], w_up[1], w_down[1])
    half = (WLAT // 2, WLON // 2)
    first = run_layer(grid.astype(jnp.float32), layer_one, plain_mask).astype(jnp.bfloat16)
    rolled = jnp.roll(first, (-half[0], -half[1]), axis=(1, 2))
    second = run_layer(rolled.astype(jnp.float32), layer_two, shift_mask).astype(jnp.bfloat16)
    mixed = jnp.roll(second, half, axis=(1, 2))
    back = jnp.roll(upstream, (-half[0], -half[1]), axis=(1, 2)).astype(jnp.float32)
    d_second, grads_two = back_layer(rolled.astype(jnp.float32), back, layer_two, shift_mask)
    g_mid = jnp.roll(d_second.astype(jnp.bfloat16), half, axis=(1, 2)).astype(jnp.float32)
    d_first, grads_one = back_layer(grid.astype(jnp.float32), g_mid, layer_one, plain_mask)
    grad_tokens = jnp.transpose(d_first.astype(jnp.bfloat16), (0, 1, 3, 2))
    stacked = tuple((jnp.stack([grads_one[index], grads_two[index]]) for index in range(4)))
    return (mixed, grad_tokens, stacked[0], stacked[1], stacked[2], stacked[3])
```

```python
import functools

import jax
import jax.numpy as jnp
import numpy as np
from jax import lax
from jax.experimental import pallas as pl
from jax.experimental.pallas import tpu as pltpu
from jax.sharding import PartitionSpec as P

HEADS = 16
WLAT = 6
WLON = 12
LEV = 2
C = 512
FF = 2048
T = LEV * WLAT * WLON
QUAD = T // 4
SLOT = 48
NORM_EPS = 1e-05
MESH = pl.DeviceIdType.MESH
BF = jnp.bfloat16
F32 = jnp.float32


def quadrant_order():
    return [
        (l, 3 * a + r, 6 * b + c)
        for a in range(2)
        for b in range(2)
        for l in range(LEV)
        for r in range(3)
        for c in range(6)
    ]


def permutations():
    slots_of_natural = np.zeros((4 * SLOT, 12 * 16), np.float32)
    tokens_of_slots = np.zeros((T, 4 * SLOT), np.float32)
    for t, (l, r, c) in enumerate(quadrant_order()):
        slot = t // QUAD * SLOT + t % QUAD
        slots_of_natural[slot, (l * WLAT + r) * 16 + c] = 1
        tokens_of_slots[t, slot] = 1
    return slots_of_natural, tokens_of_slots


def nn(a, b):
    return lax.dot_general(a, b, (((1,), (0,)), ((), ())), preferred_element_type=F32)


def nt(a, b):
    return lax.dot_general(a, b, (((1,), (1,)), ((), ())), preferred_element_type=F32)


def tn(a, b):
    return lax.dot_general(a, b, (((0,), (0,)), ((), ())), preferred_element_type=F32)


def norm(x):
    centred = x - jnp.mean(x, -1, keepdims=True)
    rstd = lax.rsqrt(jnp.mean(centred * centred, -1, keepdims=True) + NORM_EPS)
    return centred * rstd, rstd


def norm_back(dn, nhat, rstd):
    return rstd * (
        dn - jnp.mean(dn, -1, keepdims=True) - nhat * jnp.mean(dn * nhat, -1, keepdims=True)
    )


def layers_kernel(
    grid_ref, up_ref, son_ref, tos_ref, wqkv_hbm, wproj_hbm, wup_hbm, wdown_hbm,
    mixed_ref, dgrid_ref, gqkv_hbm, gproj_hbm, gup_hbm, gdown_hbm,
    wqkv, wproj, wup, wdown, wsem,
    nat, send, recv, send_sem, recv_sem,
    xs, n1h, n1, r1, us, ps, att, n2h, n2, r2, gp, hs, acc, eq, ep, eu, ed, dab,
    gqkv, gproj, gup, gdown, gsem,
):
    i, j = lax.axis_index("lat"), lax.axis_index("lon")
    nlat, nlon = lax.axis_size("lat"), lax.axis_size("lon")

    def device(di, dj):
        return (lax.rem(i + di + nlat, nlat), lax.rem(j + dj + nlon, nlon))

    weights = ((wqkv_hbm, wqkv), (wproj_hbm, wproj), (wup_hbm, wup), (wdown_hbm, wdown))
    fetches = []
    for k in range(2):
        for w, (src, dst) in enumerate(weights):
            fetch = pltpu.make_async_copy(src.at[k], dst.at[k], wsem.at[k, w])
            fetch.start()
            fetches.append(fetch)

    barrier = pltpu.get_barrier_semaphore()
    offsets = ((0, 1), (1, 0), (1, 1), (0, -1), (-1, 0), (-1, -1))
    for di, dj in offsets:
        pl.semaphore_signal(barrier, inc=1, device_id=device(di, dj), device_id_type=MESH)
    pl.semaphore_wait(barrier, len(offsets))

    def exchange(event, forward):
        copies = []
        for q in range(4):
            a, b = q // 2, q % 2
            di, dj = (a - 1, b - 1) if forward else (a, b)
            if (di, dj) == (0, 0):
                recv[event, 3 - q] = send[event, q]
            else:
                copy = pltpu.make_async_remote_copy(
                    src_ref=send.at[event, q], dst_ref=recv.at[event, 3 - q],
                    send_sem=send_sem.at[event, q], recv_sem=recv_sem.at[event, 3 - q],
                    device_id=device(di, dj), device_id_type=MESH,
                )
                copy.start()
                copies.append(copy)
        return copies

    def finish(copies):
        for copy in copies:
            copy.wait()

    def put(event, tokens):
        send[event] = tn(tos_ref[...], tokens).astype(BF).reshape(4, SLOT, C)

    def got(event):
        return nn(tos_ref[...], recv[event].reshape(4 * SLOT, C))

    nat[...] = jnp.zeros_like(nat)
    nat[:, 0:WLON, :] = up_ref[...]
    send[0] = nn(son_ref[...], nat[...].reshape(12 * 16, C)).astype(BF).reshape(4, SLOT, C)
    up_copies = exchange(0, True)

    lane = lax.broadcasted_iota(jnp.int32, (1, 128), 1)
    head_mask = [((lane >= 32 * s) & (lane < 32 * s + 32)).astype(BF) for s in range(4)]
    half_t = lax.broadcasted_iota(jnp.int32, (T, T), 0) < T // 2
    half_s = lax.broadcasted_iota(jnp.int32, (T, T), 1) < T // 2
    apart = jnp.where(half_t == half_s, 0.0, 1.0).astype(F32)
    last = jnp.where(i == nlat - 1, 1.0, 0.0).astype(F32)

    def forward(k, x):
        xs[k] = x
        nhat, rstd = norm(x)
        n1h[k] = nhat
        r1[k] = jnp.broadcast_to(rstd, (T, 128))
        n1[k] = nhat.astype(BF)
        fetches[4 * k].wait()

        @pl.loop(0, 3)
        def _(s):
            cols = pl.ds(pl.multiple_of(s * C, C), C)
            us[k, :, cols] = nn(n1[k], wqkv[k, :, cols]).astype(BF)

        @pl.loop(0, 4)
        def _(g):
            def part(w):
                return us[k, :, pl.ds(pl.multiple_of(w * C + g * 128, 128), 128)]

            q, key, v = part(0), part(1), part(2)
            total = jnp.zeros((T, 128), F32)
            for s in range(4):
                e = jnp.exp(nt(q * head_mask[s], key) * (32**-0.5))
                if k == 1:
                    e = e * (1.0 - last * apart)
                p = (e / jnp.sum(e, -1, keepdims=True)).astype(BF)
                ps[k, g * 4 + s] = p
                total += nn(p, v * head_mask[s])
            att[k, :, pl.ds(pl.multiple_of(g * 128, 128), 128)] = total.astype(BF)

        fetches[4 * k + 1].wait()
        m = xs[k] + nn(att[k], wproj[k])
        acc[...] = m
        nhat, rstd = norm(m)
        n2h[k] = nhat
        r2[k] = jnp.broadcast_to(rstd, (T, 128))
        n2[k] = nhat.astype(BF)
        fetches[4 * k + 2].wait()
        fetches[4 * k + 3].wait()

        @pl.loop(0, 4)
        def _(s):
            cols = pl.ds(pl.multiple_of(s * C, C), C)
            z = nn(n2[k], wup[k, :, cols])
            cdf = 0.5 * (1.0 + lax.erf(z * (2.0**-0.5)))
            gp[k, :, cols] = cdf + z * (jnp.exp(-0.5 * z * z) * ((2.0 * np.pi) ** -0.5))
            h = (z * cdf).astype(BF)
            hs[k, :, cols] = h
            acc[...] += nn(h, wdown[k, cols, :])

        return acc[...]

    def backward(k, ct):
        acc[...] = ct
        ed[...] = ct.astype(BF)

        @pl.loop(0, 4)
        def _(s):
            cols = pl.ds(pl.multiple_of(s * C, C), C)
            dh = nt(ed[...], wdown[k, cols, :]).astype(BF).astype(F32)
            eu[:, cols] = (dh * gp[k, :, cols]).astype(BF)

        dn2 = nt(eu[...], wup[k]).astype(BF).astype(F32)
        dm = acc[...] + norm_back(dn2, n2h[k], r2[k][:, 0:1])
        acc[...] = dm
        ep[...] = dm.astype(BF)
        dab[...] = nt(ep[...], wproj[k]).astype(BF)

        @pl.loop(0, 4)
        def _(g):
            def at(w):
                return pl.ds(pl.multiple_of(w * C + g * 128, 128), 128)

            q, key, v = us[k, :, at(0)], us[k, :, at(1)], us[k, :, at(2)]
            da = dab[:, at(0)]
            dq = jnp.zeros((T, 128), F32)
            dk = jnp.zeros((T, 128), F32)
            dv = jnp.zeros((T, 128), F32)
            for s in range(4):
                p = ps[k, g * 4 + s]
                dah = da * head_mask[s]
                dp = nt(dah, v).astype(BF).astype(F32)
                dv += tn(p, dah)
                pf = p.astype(F32)
                ds = pf * (dp - jnp.sum(dp * pf, -1, keepdims=True))
                ds = (ds * (32**-0.5)).astype(BF)
                dq += nn(ds, key * head_mask[s])
                dk += tn(ds, q * head_mask[s])
            eq[:, at(0)] = dq.astype(BF)
            eq[:, at(1)] = dk.astype(BF)
            eq[:, at(2)] = dv.astype(BF)

        dn1 = nt(eq[...], wqkv[k]).astype(BF).astype(F32)
        return acc[...] + norm_back(dn1, n1h[k], r1[k][:, 0:1])

    def weight_grads(k):
        @pl.loop(0, 3)
        def _(s):
            cols = pl.ds(pl.multiple_of(s * C, C), C)
            gqkv[k, cols, :] = tn(eq[:, cols], n1[k]).astype(BF)

        gproj[k] = tn(ep[...], att[k]).astype(BF)

        @pl.loop(0, 4)
        def _(s):
            cols = pl.ds(pl.multiple_of(s * C, C), C)
            gup[k, cols, :] = tn(eu[:, cols], n2[k]).astype(BF)
            gdown[k, :, cols] = tn(ed[...], hs[k, :, cols]).astype(BF)

        stores = []
        for w, (src, dst) in enumerate(
            ((gqkv, gqkv_hbm), (gproj, gproj_hbm), (gup, gup_hbm), (gdown, gdown_hbm))
        ):
            store = pltpu.make_async_copy(src.at[k], dst.at[k], gsem.at[k, w])
            store.start()
            stores.append(store)
        return stores

    first = forward(0, jnp.transpose(grid_ref[...].astype(F32)))
    put(1, first.astype(BF))
    finish(exchange(1, True))
    second = forward(1, got(1))
    put(2, second.astype(BF))
    mixed_copies = exchange(2, False)
    finish(up_copies)
    d_second = backward(1, got(0))
    put(3, d_second.astype(BF))
    mid_copies = exchange(3, False)
    stores = weight_grads(1)
    finish(mid_copies)
    d_first = backward(0, got(3))
    dgrid_ref[...] = jnp.transpose(d_first).astype(BF)
    stores += weight_grads(0)
    finish(mixed_copies)
    natural = tn(son_ref[...], recv[2].reshape(4 * SLOT, C)).astype(BF)
    mixed_ref[...] = natural.reshape(12, 16, C)[:, 0:WLON, :]
    finish(stores)


def layers(grid, upstream, w_qkv, w_proj, w_up, w_down):
    son, tos = permutations()
    vmem = pl.BlockSpec(memory_space=pltpu.VMEM)
    hbm = pl.BlockSpec(memory_space=pl.ANY)
    dma = pltpu.SemaphoreType.DMA
    V = pltpu.VMEM
    return pl.pallas_call(
        layers_kernel,
        out_shape=(
            jax.ShapeDtypeStruct((12, WLON, C), BF),
            jax.ShapeDtypeStruct((C, T), BF),
            jax.ShapeDtypeStruct((2, 3 * C, C), BF),
            jax.ShapeDtypeStruct((2, C, C), BF),
            jax.ShapeDtypeStruct((2, FF, C), BF),
            jax.ShapeDtypeStruct((2, C, FF), BF),
        ),
        in_specs=[vmem] * 4 + [hbm] * 4,
        out_specs=(vmem, vmem, hbm, hbm, hbm, hbm),
        scratch_shapes=[
            V((2, C, 3 * C), BF), V((2, C, C), BF), V((2, C, FF), BF), V((2, FF, C), BF),
            dma((2, 4)),
            V((12, 16, C), BF), V((4, 4, SLOT, C), BF), V((4, 4, SLOT, C), BF),
            dma((4, 4)), dma((4, 4)),
            V((2, T, C), F32), V((2, T, C), F32), V((2, T, C), BF), V((2, T, 128), F32),
            V((2, T, 3 * C), BF), V((2, HEADS, T, T), BF), V((2, T, C), BF),
            V((2, T, C), F32), V((2, T, C), BF), V((2, T, 128), F32),
            V((2, T, FF), F32), V((2, T, FF), BF), V((T, C), F32),
            V((T, 3 * C), BF), V((T, C), BF), V((T, FF), BF), V((T, C), BF), V((T, C), BF),
            V((2, 3 * C, C), BF), V((2, C, C), BF), V((2, FF, C), BF), V((2, C, FF), BF),
            dma((2, 4)),
        ],
        compiler_params=pltpu.CompilerParams(
            collective_id=0, has_side_effects=True, vmem_limit_bytes=60 * 2**20
        ),
    )(grid, upstream, jnp.asarray(son, BF), jnp.asarray(tos, BF), w_qkv, w_proj, w_up, w_down)


def on_device(encoded, upstream, w_qkv, w_proj, w_up, w_down):
    levels, rows, width, cols = encoded.shape
    nlon = cols // WLON
    pieces = encoded.reshape(levels, 2, 3, width, nlon, 2, 6)
    pieces = pieces.transpose(4, 3, 1, 5, 0, 2, 6).reshape(nlon * width, T)
    grid = lax.all_to_all(pieces, "lon", split_axis=0, concat_axis=0, tiled=True)
    up = upstream.reshape(levels * rows, WLON, C)
    mixed, dgrid, *grads = layers(grid, up, w_qkv, w_proj, w_up, w_down)
    leaving = lax.all_to_all(dgrid, "lon", split_axis=0, concat_axis=0, tiled=True)
    leaving = leaving.reshape(nlon, width, 2, 2, levels, 3, 6).transpose(4, 2, 5, 1, 0, 3, 6)
    shares = [
        lax.psum_scatter(g, ("lat", "lon"), scatter_dimension=1, tiled=True).astype(F32)
        for g in grads
    ]
    return (
        mixed.reshape(upstream.shape),
        leaving.reshape(encoded.shape),
        *[jnp.swapaxes(s, 1, 2) for s in shares],
    )


def solution(mesh):
    return jax.shard_map(
        on_device,
        mesh=mesh,
        in_specs=(P(None, "lat", "lon", None), P(None, "lat", "lon", None), P(), P(), P(), P()),
        out_specs=(
            P(None, "lat", "lon", None),
            P(None, "lat", "lon", None),
            P(None, None, ("lat", "lon")),
            P(None, None, ("lat", "lon")),
            P(None, None, ("lat", "lon")),
            P(None, None, ("lat", "lon")),
        ),
        check_vma=False,
    )
```

```python
import functools

import jax
import jax.numpy as jnp
import numpy as np
from jax import lax
from jax.experimental import pallas as pl
from jax.experimental.pallas import tpu as pltpu
from jax.sharding import PartitionSpec as P

HEADS = 16
WLAT = 6
WLON = 12
LEV = 2
C = 512
FF = 2048
T = LEV * WLAT * WLON
QUAD = T // 4
SLOT = 48
NORM_EPS = 1e-05
MESH = pl.DeviceIdType.MESH
BF = jnp.bfloat16
F32 = jnp.float32


def quadrant_order():
    return [
        (l, 3 * a + r, 6 * b + c)
        for a in range(2)
        for b in range(2)
        for l in range(LEV)
        for r in range(3)
        for c in range(6)
    ]


def permutations():
    slots_of_natural = np.zeros((4 * SLOT, 12 * 16), np.float32)
    tokens_of_slots = np.zeros((T, 4 * SLOT), np.float32)
    for t, (l, r, c) in enumerate(quadrant_order()):
        slot = t // QUAD * SLOT + t % QUAD
        slots_of_natural[slot, (l * WLAT + r) * 16 + c] = 1
        tokens_of_slots[t, slot] = 1
    return slots_of_natural, tokens_of_slots


def nn(a, b):
    return lax.dot_general(a, b, (((1,), (0,)), ((), ())), preferred_element_type=F32)


def nt(a, b):
    return lax.dot_general(a, b, (((1,), (1,)), ((), ())), preferred_element_type=F32)


def tn(a, b):
    return lax.dot_general(a, b, (((0,), (0,)), ((), ())), preferred_element_type=F32)


def norm(x):
    centred = x - jnp.mean(x, -1, keepdims=True)
    rstd = lax.rsqrt(jnp.mean(centred * centred, -1, keepdims=True) + NORM_EPS)
    return centred * rstd, rstd


def norm_back(dn, nhat, rstd):
    return rstd * (
        dn - jnp.mean(dn, -1, keepdims=True) - nhat * jnp.mean(dn * nhat, -1, keepdims=True)
    )


def layers_kernel(
    grid_ref, up_ref, son_ref, tos_ref, wqkv_hbm, wproj_hbm, wup_hbm, wdown_hbm,
    mixed_ref, dgrid_ref, grads_ref,
    wqkv, wproj, wup, wdown, wsem,
    nat, send, recv, send_sem, recv_sem,
    xs, n1h, n1, r1, us, ps, att, n2h, n2, r2, gp, hs, acc, eq, ep, eu, ed, dab,
    pn1, patt, pn2, phs, peq, pep, peu, ped, pair_send, pair_recv,
    part, fwd, fsum, side, part2, fwd2, fsum2, side2, part3, side3, ring_send, ring_recv,
):
    i, j = lax.axis_index("lat"), lax.axis_index("lon")
    nlat, nlon = lax.axis_size("lat"), lax.axis_size("lon")

    def device(di, dj):
        return (lax.rem(i + di + nlat, nlat), lax.rem(j + dj + nlon, nlon))

    core, z, y = lax.rem(i, 2), lax.rem(j, 4), j // 8
    x = i // 2 * 2 + lax.rem(j // 4, 2)

    def along(axis, steps):
        at = {"x": x, "y": y, "z": z}
        at[axis] = lax.rem(at[axis] + steps + 4, 4)
        return (at["x"] // 2 * 2 + core, at["y"] * 8 + lax.rem(at["x"], 2) * 4 + at["z"])

    partner = (i + 1 - 2 * core, j)

    weights = ((wqkv_hbm, wqkv), (wproj_hbm, wproj), (wup_hbm, wup), (wdown_hbm, wdown))
    fetches = []
    for k in range(2):
        for w, (src, dst) in enumerate(weights):
            fetch = pltpu.make_async_copy(src.at[k], dst.at[k], wsem.at[k, w])
            fetch.start()
            fetches.append(fetch)

    barrier = pltpu.get_barrier_semaphore()
    offsets = ((0, 1), (1, 0), (1, 1), (0, -1), (-1, 0), (-1, -1))
    greeted = [device(di, dj) for di, dj in offsets]
    greeted += [along(axis, steps) for axis in "xyz" for steps in (1, 2, 3)] + [partner]
    for other in greeted:
        pl.semaphore_signal(barrier, inc=1, device_id=other, device_id_type=MESH)
    pl.semaphore_wait(barrier, len(greeted))

    def remote(src, dst, sems, index, to):
        copy = pltpu.make_async_remote_copy(
            src_ref=src, dst_ref=dst, send_sem=sems[0].at[index], recv_sem=sems[1].at[index],
            device_id=to, device_id_type=MESH,
        )
        copy.start()
        sent.append(copy)
        return copy

    sent = []
    pairs = {}
    wide = {"eq": 384, "ep": 128, "eu": 512, "ed": 128}
    whole = {"n1": (n1, pn1), "att": (att, patt), "n2": (n2, pn2), "hs": (hs, phs)}
    cut = {"eq": (eq, peq), "ep": (ep, pep), "eu": (eu, peu), "ed": (ed, ped)}

    def columns(name, hi, owner):
        width = wide[name]
        return pl.ds(pl.multiple_of((2 * hi + owner) * width, width), width)

    def give(k, name):
        sems = (pair_send, pair_recv)
        if name in whole:
            src, dst = whole[name]
            index = list(whole).index(name)
            pairs[k, name] = [remote(src.at[k], dst.at[k], sems, (k, index), partner)]
        else:
            src, dst = cut[name]
            index = 4 + 2 * list(cut).index(name)
            pairs[k, name] = [
                remote(src.at[k, :, columns(name, hi, 1 - core)], dst.at[k, hi], sems, (k, index + hi), partner)
                for hi in range(2)
            ]

    def take(k, name):
        for copy in pairs[k, name]:
            copy.wait_recv()

    orders = ("xyz", "zyx", "yxz")
    rings = {}

    def chunk(k, p, phase, t, half):
        t = lax.rem(t + 4, 4)
        if phase == 0:
            return part.at[k, p, t, pl.ds(2 * half, 2)]
        return part2.at[k, p, t, pl.ds(32 * half, 32)]

    def ring_bufs(k, p, phase):
        if phase == 0:
            halves = [[side.at[k, p, s, pl.ds(2 * h, 2)] for h in range(2)] for s in range(2)]
            return [fwd.at[k, p, s] for s in range(2)], [fsum.at[k, p, s] for s in range(2)], halves
        halves = [[side2.at[k, p, s, pl.ds(32 * h, 32)] for h in range(2)] for s in range(2)]
        return [fwd2.at[k, p, s] for s in range(2)], [fsum2.at[k, p, s] for s in range(2)], halves

    def f32(ref):
        return ref[...].astype(F32)

    def ring_start(k, p, phase):
        axis = orders[p][phase]
        t = {"x": x, "y": y, "z": z}[axis]
        after, before = along(axis, 1), along(axis, -1)
        f, _, halves = ring_bufs(k, p, phase)
        sems = (ring_send, ring_recv)
        o = 6 * phase
        rings[k, p, phase] = [
            remote(chunk(k, p, phase, t + 2, 0), f[0], sems, (k, p, o), after),
            remote(chunk(k, p, phase, t + 2, 1), f[1], sems, (k, p, o + 1), before),
            remote(chunk(k, p, phase, t + 1, 1), halves[0][1], sems, (k, p, o + 2), after),
            remote(chunk(k, p, phase, t - 1, 0), halves[1][0], sems, (k, p, o + 3), before),
        ]

    def ring_mid(k, p, phase):
        axis = orders[p][phase]
        t = {"x": x, "y": y, "z": z}[axis]
        after, before = along(axis, 1), along(axis, -1)
        f, fs, halves = ring_bufs(k, p, phase)
        copies = rings[k, p, phase]
        sems = (ring_send, ring_recv)
        o = 6 * phase
        copies[0].wait_recv()
        fs[0][...] = (f32(f[0]) + f32(chunk(k, p, phase, t + 1, 0))).astype(BF)
        copies.append(remote(fs[0], halves[0][0], sems, (k, p, o + 4), after))
        copies[1].wait_recv()
        fs[1][...] = (f32(f[1]) + f32(chunk(k, p, phase, t - 1, 1))).astype(BF)
        copies.append(remote(fs[1], halves[1][1], sems, (k, p, o + 5), before))

    def ring_end(k, p, phase):
        axis = orders[p][phase]
        t = {"x": x, "y": y, "z": z}[axis]
        for copy in rings[k, p, phase][2:]:
            copy.wait_recv()
        if phase == 0:
            total = f32(part.at[k, p, t]) + f32(side.at[k, p, 0]) + f32(side.at[k, p, 1])
            part2[k, p] = total.astype(BF)
            ring_start(k, p, 1)
            return
        total = f32(part2.at[k, p, t]) + f32(side2.at[k, p, 0]) + f32(side2.at[k, p, 1])
        for s in range(4):
            if p == 0:
                rows = (total[12 * s : 12 * s + 12], total[48 + 4 * s : 52 + 4 * s])
                rows = jnp.concatenate(rows, 0)
            elif p == 1:
                rows = total[16 * s : 16 * s + 16]
            else:
                rows = [total[16 * hb + 4 * s : 16 * hb + 4 * s + 4] for hb in range(4)]
                rows = jnp.concatenate(rows, 0)
            part3[k, p, s] = rows
        axis = orders[p][2]
        t = {"x": x, "y": y, "z": z}[axis]
        rings[k, p, 2] = [
            remote(
                part3.at[k, p, lax.rem(t + s, 4)], side3.at[k, p, s - 1], (ring_send, ring_recv),
                (k, p, 11 + s), along(axis, s),
            )
            for s in (1, 2, 3)
        ]

    def ring_last(k, p):
        t = {"x": x, "y": y, "z": z}[orders[p][2]]
        for copy in rings[k, p, 2]:
            copy.wait_recv()
        grads_ref[k, p] = part3[k, p, t] + side3[k, p, 0] + side3[k, p, 1] + side3[k, p, 2]

    def both(k, name, hi, own, theirs):
        src, dst = cut[name]
        return tn(src[k, :, columns(name, hi, core)], own) + tn(dst[k, hi], theirs)

    def grads_a(k):
        for name in ("n1", "att", "ep", "eq"):
            take(k, name)
        for hi in range(2):
            g = both(k, "eq", hi, n1[k], pn1[k]).astype(BF)
            for at in range(8):
                part[k, 0, 2 * hi + at % 2, at // 2, 0:48, :] = g[48 * at : 48 * at + 48]
            g = both(k, "ep", hi, att[k], patt[k]).astype(BF)
            for at in range(8):
                part[k, 0, 2 * hi + at % 2, at // 2, 48:64, :] = g[16 * at : 16 * at + 16]
        ring_start(k, 0, 0)

    def grads_b(k):
        for name in ("n2", "eu"):
            take(k, name)
        for hi in range(2):
            g = both(k, "eu", hi, n2[k], pn2[k]).astype(BF)
            for at in range(32):
                row = (2 * hi + at // 4 % 2) * 16
                part[k, 1, at % 4, at // 8, row : row + 16, :] = g[16 * at : 16 * at + 16]
        ring_start(k, 1, 0)

    def grads_c(k):
        for name in ("hs", "ed"):
            take(k, name)
        for hi in range(2):
            for hb in range(4):
                cols = slice(hb * C, hb * C + C)
                g = both(k, "ed", hi, hs[k, :, cols], phs[k, :, cols]).astype(BF)
                for at in range(8):
                    row = 16 * hb
                    part[k, 2, at // 2, 2 * hi + at % 2, row : row + 16, :] = g[16 * at : 16 * at + 16]
        ring_start(k, 2, 0)

    def exchange(event, forward):
        copies = []
        for q in range(4):
            a, b = q // 2, q % 2
            di, dj = (a - 1, b - 1) if forward else (a, b)
            if (di, dj) == (0, 0):
                recv[event, 3 - q] = send[event, q]
            else:
                copy = pltpu.make_async_remote_copy(
                    src_ref=send.at[event, q], dst_ref=recv.at[event, 3 - q],
                    send_sem=send_sem.at[event, q], recv_sem=recv_sem.at[event, 3 - q],
                    device_id=device(di, dj), device_id_type=MESH,
                )
                copy.start()
                copies.append(copy)
        return copies

    def finish(copies):
        for copy in copies:
            copy.wait()

    def put(event, tokens):
        send[event] = tn(tos_ref[...], tokens).astype(BF).reshape(4, SLOT, C)

    def got(event):
        return nn(tos_ref[...], recv[event].reshape(4 * SLOT, C))

    nat[...] = jnp.zeros_like(nat)
    nat[:, 0:WLON, :] = up_ref[...]
    send[0] = nn(son_ref[...], nat[...].reshape(12 * 16, C)).astype(BF).reshape(4, SLOT, C)
    up_copies = exchange(0, True)

    lane = lax.broadcasted_iota(jnp.int32, (1, 128), 1)
    head_mask = [((lane >= 32 * s) & (lane < 32 * s + 32)).astype(BF) for s in range(4)]
    half_t = lax.broadcasted_iota(jnp.int32, (T, T), 0) < T // 2
    half_s = lax.broadcasted_iota(jnp.int32, (T, T), 1) < T // 2
    apart = jnp.where(half_t == half_s, 0.0, 1.0).astype(F32)
    last = jnp.where(i == nlat - 1, 1.0, 0.0).astype(F32)

    def forward(k, x):
        xs[k] = x
        nhat, rstd = norm(x)
        n1h[k] = nhat
        r1[k] = jnp.broadcast_to(rstd, (T, 128))
        n1[k] = nhat.astype(BF)
        give(k, "n1")
        fetches[4 * k].wait()

        @pl.loop(0, 3)
        def _(s):
            cols = pl.ds(pl.multiple_of(s * C, C), C)
            us[k, :, cols] = nn(n1[k], wqkv[k, :, cols]).astype(BF)

        @pl.loop(0, 4)
        def _(g):
            def part(w):
                return us[k, :, pl.ds(pl.multiple_of(w * C + g * 128, 128), 128)]

            q, key, v = part(0), part(1), part(2)
            total = jnp.zeros((T, 128), F32)
            for s in range(4):
                e = jnp.exp(nt(q * head_mask[s], key) * (32**-0.5))
                if k == 1:
                    e = e * (1.0 - last * apart)
                p = (e / jnp.sum(e, -1, keepdims=True)).astype(BF)
                ps[k, g * 4 + s] = p
                total += nn(p, v * head_mask[s])
            att[k, :, pl.ds(pl.multiple_of(g * 128, 128), 128)] = total.astype(BF)

        give(k, "att")
        fetches[4 * k + 1].wait()
        m = xs[k] + nn(att[k], wproj[k])
        acc[...] = m
        nhat, rstd = norm(m)
        n2h[k] = nhat
        r2[k] = jnp.broadcast_to(rstd, (T, 128))
        n2[k] = nhat.astype(BF)
        give(k, "n2")
        fetches[4 * k + 2].wait()
        fetches[4 * k + 3].wait()

        @pl.loop(0, 4)
        def _(s):
            cols = pl.ds(pl.multiple_of(s * C, C), C)
            z = nn(n2[k], wup[k, :, cols])
            cdf = 0.5 * (1.0 + lax.erf(z * (2.0**-0.5)))
            gp[k, :, cols] = cdf + z * (jnp.exp(-0.5 * z * z) * ((2.0 * np.pi) ** -0.5))
            h = (z * cdf).astype(BF)
            hs[k, :, cols] = h
            acc[...] += nn(h, wdown[k, cols, :])

        give(k, "hs")
        return acc[...]

    def backward(k, ct, after_up, after_proj, amid):
        acc[...] = ct
        ed[k] = ct.astype(BF)
        give(k, "ed")

        @pl.loop(0, 4)
        def _(s):
            cols = pl.ds(pl.multiple_of(s * C, C), C)
            dh = nt(ed[k], wdown[k, cols, :]).astype(BF).astype(F32)
            eu[k, :, cols] = (dh * gp[k, :, cols]).astype(BF)

        give(k, "eu")
        after_up()
        dn2 = nt(eu[k], wup[k]).astype(BF).astype(F32)
        dm = acc[...] + norm_back(dn2, n2h[k], r2[k][:, 0:1])
        acc[...] = dm
        ep[k] = dm.astype(BF)
        give(k, "ep")
        grads_c(k)
        dab[...] = nt(ep[k], wproj[k]).astype(BF)
        grads_b(k)
        after_proj()

        def heads(g):
            def at(w):
                return pl.ds(pl.multiple_of(w * C + g * 128, 128), 128)

            q, key, v = us[k, :, at(0)], us[k, :, at(1)], us[k, :, at(2)]
            da = dab[:, at(0)]
            dq = jnp.zeros((T, 128), F32)
            dk = jnp.zeros((T, 128), F32)
            dv = jnp.zeros((T, 128), F32)
            for s in range(4):
                p = ps[k, g * 4 + s]
                dah = da * head_mask[s]
                dp = nt(dah, v).astype(BF).astype(F32)
                dv += tn(p, dah)
                pf = p.astype(F32)
                ds = pf * (dp - jnp.sum(dp * pf, -1, keepdims=True))
                ds = (ds * (32**-0.5)).astype(BF)
                dq += nn(ds, key * head_mask[s])
                dk += tn(ds, q * head_mask[s])
            eq[k, :, at(0)] = dq.astype(BF)
            eq[k, :, at(1)] = dk.astype(BF)
            eq[k, :, at(2)] = dv.astype(BF)

        pl.loop(0, 2)(heads)
        amid()
        pl.loop(2, 4)(heads)
        give(k, "eq")

    def backward_end(k):
        dn1 = nt(eq[k], wqkv[k]).astype(BF).astype(F32)
        return acc[...] + norm_back(dn1, n1h[k], r1[k][:, 0:1])

    def nothing():
        pass

    first = forward(0, jnp.transpose(grid_ref[...].astype(F32)))
    put(1, first.astype(BF))
    finish(exchange(1, True))
    second = forward(1, got(1))
    put(2, second.astype(BF))
    mixed_copies = exchange(2, False)
    finish(up_copies)

    def amid_one():
        ring_mid(1, 2, 0)

    backward(1, got(0), nothing, nothing, amid_one)
    ring_mid(1, 1, 0)
    d_second = backward_end(1)
    put(3, d_second.astype(BF))
    mid_copies = exchange(3, False)
    ring_end(1, 2, 0)
    grads_a(1)
    ring_end(1, 1, 0)
    ring_mid(1, 2, 1)
    finish(mid_copies)

    def up_zero():
        ring_mid(1, 0, 0)
        ring_mid(1, 1, 1)
        ring_end(1, 2, 1)

    def proj_zero():
        ring_end(1, 0, 0)
        ring_end(1, 1, 1)
        ring_last(1, 2)

    def amid_zero():
        ring_mid(1, 0, 1)
        ring_mid(0, 2, 0)
        ring_mid(0, 1, 0)
        ring_last(1, 1)

    backward(0, got(3), up_zero, proj_zero, amid_zero)
    grads_a(0)
    ring_end(1, 0, 1)
    ring_end(0, 2, 0)
    ring_end(0, 1, 0)
    d_first = backward_end(0)
    dgrid_ref[...] = jnp.transpose(d_first).astype(BF)
    ring_mid(0, 0, 0)
    ring_mid(0, 2, 1)
    ring_mid(0, 1, 1)
    ring_last(1, 0)
    finish(mixed_copies)
    natural = tn(son_ref[...], recv[2].reshape(4 * SLOT, C)).astype(BF)
    mixed_ref[...] = natural.reshape(12, 16, C)[:, 0:WLON, :]
    ring_end(0, 0, 0)
    ring_end(0, 2, 1)
    ring_end(0, 1, 1)
    ring_mid(0, 0, 1)
    ring_last(0, 2)
    ring_last(0, 1)
    ring_end(0, 0, 1)
    ring_last(0, 0)
    for copy in sent:
        copy.wait_send()


def layers(grid, upstream, w_qkv, w_proj, w_up, w_down):
    son, tos = permutations()
    vmem = pl.BlockSpec(memory_space=pltpu.VMEM)
    hbm = pl.BlockSpec(memory_space=pl.ANY)
    dma = pltpu.SemaphoreType.DMA
    V = pltpu.VMEM
    return pl.pallas_call(
        layers_kernel,
        out_shape=(
            jax.ShapeDtypeStruct((12, WLON, C), BF),
            jax.ShapeDtypeStruct((C, T), BF),
            jax.ShapeDtypeStruct((2, 3, 16, C), F32),
        ),
        in_specs=[vmem] * 4 + [hbm] * 4,
        out_specs=(vmem, vmem, vmem),
        scratch_shapes=[
            V((2, C, 3 * C), BF), V((2, C, C), BF), V((2, C, FF), BF), V((2, FF, C), BF),
            dma((2, 4)),
            V((12, 16, C), BF), V((4, 4, SLOT, C), BF), V((4, 4, SLOT, C), BF),
            dma((4, 4)), dma((4, 4)),
            V((2, T, C), F32), V((2, T, C), F32), V((2, T, C), BF), V((2, T, 128), F32),
            V((2, T, 3 * C), BF), V((2, HEADS, T, T), BF), V((2, T, C), BF),
            V((2, T, C), F32), V((2, T, C), BF), V((2, T, 128), F32),
            V((2, T, FF), F32), V((2, T, FF), BF), V((T, C), F32),
            V((2, T, 3 * C), BF), V((2, T, C), BF), V((2, T, FF), BF), V((2, T, C), BF), V((T, C), BF),
            V((2, T, C), BF), V((2, T, C), BF), V((2, T, C), BF), V((2, T, FF), BF),
            V((2, 2, T, 384), BF), V((2, 2, T, 128), BF), V((2, 2, T, 512), BF), V((2, 2, T, 128), BF),
            dma((2, 12)), dma((2, 12)),
            V((2, 3, 4, 4, 64, C), BF), V((2, 3, 2, 2, 64, C), BF), V((2, 3, 2, 2, 64, C), BF),
            V((2, 3, 2, 4, 64, C), BF),
            V((2, 3, 4, 64, C), BF), V((2, 3, 2, 32, C), BF), V((2, 3, 2, 32, C), BF),
            V((2, 3, 2, 64, C), BF),
            V((2, 3, 4, 16, C), F32), V((2, 3, 3, 16, C), F32),
            dma((2, 3, 15)), dma((2, 3, 15)),
        ],
        compiler_params=pltpu.CompilerParams(
            collective_id=0, has_side_effects=True, vmem_limit_bytes=60 * 2**20
        ),
    )(grid, upstream, jnp.asarray(son, BF), jnp.asarray(tos, BF), w_qkv, w_proj, w_up, w_down)


def on_device(encoded, upstream, w_qkv, w_proj, w_up, w_down):
    levels, rows, width, cols = encoded.shape
    nlon = cols // WLON
    pieces = encoded.reshape(levels, 2, 3, width, nlon, 2, 6)
    pieces = pieces.transpose(4, 3, 1, 5, 0, 2, 6).reshape(nlon * width, T)
    grid = lax.all_to_all(pieces, "lon", split_axis=0, concat_axis=0, tiled=True)
    up = upstream.reshape(levels * rows, WLON, C)
    mixed, dgrid, grads = layers(grid, up, w_qkv, w_proj, w_up, w_down)
    leaving = lax.all_to_all(dgrid, "lon", split_axis=0, concat_axis=0, tiled=True)
    leaving = leaving.reshape(nlon, width, 2, 2, levels, 3, 6).transpose(4, 2, 5, 1, 0, 3, 6)
    down = grads[:, 2].reshape(2, 4, 4, C).transpose(0, 1, 3, 2).reshape(2, FF, 4)
    return (
        mixed.reshape(upstream.shape),
        leaving.reshape(encoded.shape),
        jnp.swapaxes(grads[:, 0, 0:12], 1, 2),
        jnp.swapaxes(grads[:, 0, 12:16], 1, 2),
        jnp.swapaxes(grads[:, 1], 1, 2),
        down,
    )


def solution(mesh):
    return jax.shard_map(
        on_device,
        mesh=mesh,
        in_specs=(P(None, "lat", "lon", None), P(None, "lat", "lon", None), P(), P(), P(), P()),
        out_specs=(
            P(None, "lat", "lon", None),
            P(None, "lat", "lon", None),
            P(None, None, ("lat", "lon")),
            P(None, None, ("lat", "lon")),
            P(None, None, ("lat", "lon")),
            P(None, None, ("lat", "lon")),
        ),
        check_vma=False,
    )
```

```python
import functools

import jax
import jax.numpy as jnp
import numpy as np
from jax import lax
from jax.experimental import pallas as pl
from jax.experimental.pallas import tpu as pltpu
from jax.sharding import PartitionSpec as P

HEADS = 16
WLAT = 6
WLON = 12
LEV = 2
C = 512
FF = 2048
T = LEV * WLAT * WLON
QUAD = T // 4
SLOT = 48
NORM_EPS = 1e-05
MESH = pl.DeviceIdType.MESH
BF = jnp.bfloat16
F32 = jnp.float32


def quadrant_order():
    return [
        (l, 3 * a + r, 6 * b + c)
        for a in range(2)
        for b in range(2)
        for l in range(LEV)
        for r in range(3)
        for c in range(6)
    ]


def permutations():
    slots_of_natural = np.zeros((4 * SLOT, 12 * 16), np.float32)
    tokens_of_slots = np.zeros((T, 4 * SLOT), np.float32)
    for t, (l, r, c) in enumerate(quadrant_order()):
        slot = t // QUAD * SLOT + t % QUAD
        slots_of_natural[slot, (l * WLAT + r) * 16 + c] = 1
        tokens_of_slots[t, slot] = 1
    tokens_of_natural = tokens_of_slots @ slots_of_natural
    spread = np.zeros((32 * 16, 32 * WLON), np.float32)
    for col in range(32 * WLON):
        spread[col // WLON * 16 + col % WLON, col] = 1
    swap = np.eye(1024, dtype=np.float32).reshape(8, 8, 16, 1024).swapaxes(0, 1).reshape(1024, 1024)
    matrices = (slots_of_natural, tokens_of_slots, tokens_of_natural, spread, swap)
    return [jnp.asarray(m, BF) for m in matrices]


def nn(a, b):
    return lax.dot_general(a, b, (((1,), (0,)), ((), ())), preferred_element_type=F32)


def nt(a, b):
    return lax.dot_general(a, b, (((1,), (1,)), ((), ())), preferred_element_type=F32)


def tn(a, b):
    return lax.dot_general(a, b, (((0,), (0,)), ((), ())), preferred_element_type=F32)


def norm(x):
    centred = x - jnp.mean(x, -1, keepdims=True)
    rstd = lax.rsqrt(jnp.mean(centred * centred, -1, keepdims=True) + NORM_EPS)
    return centred * rstd, rstd


def norm_back(dn, nhat, rstd):
    return rstd * (
        dn - jnp.mean(dn, -1, keepdims=True) - nhat * jnp.mean(dn * nhat, -1, keepdims=True)
    )


def layers_kernel(
    enc_ref, up_ref, son_ref, tos_ref, ton_ref, spread_ref, swap_hbm,
    wqkv_hbm, wproj_hbm, wup_hbm, wdown_hbm,
    mixed_ref, denc_ref, oqkv_ref, oproj_ref, oup_ref, odown_ref,
    wqkv, wproj, wup, wdown, wsem,
    swap, swap_sem, leave, came, leave2, came2, lane_send, lane_recv, own_sem, nat2, turned, nat, send, recv, send_sem, recv_sem,
    xs, n1h, n1, r1, us, ps, att, n2h, n2, r2, gp, hs, acc, eq, ep, eu, ed, dab,
    pn1, patt, pn2, phs, peq, pep, peu, ped, pair_send, pair_recv,
    part, fwd, fsum, side, part2, fwd2, fsum2, side2, part3, side3, ring_send, ring_recv,
):
    i, j = lax.axis_index("lat"), lax.axis_index("lon")
    nlat, nlon = lax.axis_size("lat"), lax.axis_size("lon")

    def device(di, dj):
        return (lax.rem(i + di + nlat, nlat), lax.rem(j + dj + nlon, nlon))

    core, z, y = lax.rem(i, 2), lax.rem(j, 4), j // 8
    x = i // 2 * 2 + lax.rem(j // 4, 2)

    def along(axis, steps):
        at = {"x": x, "y": y, "z": z}
        at[axis] = lax.rem(at[axis] + steps + 4, 4)
        return (at["x"] // 2 * 2 + core, at["y"] * 8 + lax.rem(at["x"], 2) * 4 + at["z"])

    partner = (i + 1 - 2 * core, j)

    weights = ((wqkv_hbm, wqkv), (wproj_hbm, wproj), (wup_hbm, wup), (wdown_hbm, wdown))
    swap_fetch = pltpu.make_async_copy(swap_hbm, swap, swap_sem)
    swap_fetch.start()
    fetches = []
    for k in range(2):
        for w, (src, dst) in enumerate(weights):
            fetch = pltpu.make_async_copy(src.at[k], dst.at[k], wsem.at[k, w])
            fetch.start()
            fetches.append(fetch)

    barrier = pltpu.get_barrier_semaphore()
    offsets = ((0, 1), (1, 0), (1, 1), (0, -1), (-1, 0), (-1, -1))
    greeted = [device(di, dj) for di, dj in offsets]
    greeted += [along(axis, steps) for axis in "xyz" for steps in (1, 2, 3)] + [partner]
    for other in greeted:
        pl.semaphore_signal(barrier, inc=1, device_id=other, device_id_type=MESH)

    @pl.loop(1, nlon)
    def _(step):
        pl.semaphore_signal(barrier, inc=1, device_id=device(0, step), device_id_type=MESH)

    columns_first = nt(spread_ref[...], enc_ref[...].reshape(12 * 16, 32 * WLON)).astype(BF)
    leave[:, 0] = columns_first[:, 0:128].reshape(32, 16, 128)
    leave[:, 1, :, 0:64] = columns_first[:, 128:192].reshape(32, 16, 64)
    leave[:, 1, :, 64:128] = jnp.zeros((32, 16, 64), BF)
    pl.semaphore_wait(barrier, len(greeted) + nlon - 1)
    mine = pl.ds(pl.multiple_of(lax.rem(j, 8) * 128, 128), 128)

    def lane_copy(step, event):
        to = lax.rem(j + step, nlon)
        if event == 0:
            src, dst = leave.at[to], came.at[:, j // 8, :, mine]
        else:
            src, dst = leave2.at[to], came2.at[j]
        return pltpu.make_async_remote_copy(
            src_ref=src, dst_ref=dst, send_sem=lane_send.at[event, step], recv_sem=lane_recv.at[event, step],
            device_id=(i, to), device_id_type=MESH,
        )

    def lane_start(event):
        @pl.loop(1, nlon)
        def _(step):
            lane_copy(step, event).start()

        if event == 0:
            src, dst = leave.at[j], came.at[:, j // 8, :, mine]
        else:
            src, dst = leave2.at[j], came2.at[j]
        own = pltpu.make_async_copy(src, dst, own_sem.at[event])
        own.start()
        return own

    def lane_finish(event, own):
        own.wait()

        @pl.loop(1, nlon)
        def _(step):
            lane_copy(step, event).wait()

    own = lane_start(0)

    def remote(src, dst, sems, index, to):
        copy = pltpu.make_async_remote_copy(
            src_ref=src, dst_ref=dst, send_sem=sems[0].at[index], recv_sem=sems[1].at[index],
            device_id=to, device_id_type=MESH,
        )
        copy.start()
        sent.append(copy)
        return copy

    sent = []
    pairs = {}
    wide = {"eq": 384, "ep": 128, "eu": 512, "ed": 128}
    whole = {"n1": (n1, pn1), "att": (att, patt), "n2": (n2, pn2), "hs": (hs, phs)}
    cut = {"eq": (eq, peq), "ep": (ep, pep), "eu": (eu, peu), "ed": (ed, ped)}

    def columns(name, hi, owner):
        width = wide[name]
        return pl.ds(pl.multiple_of((2 * hi + owner) * width, width), width)

    def give(k, name):
        sems = (pair_send, pair_recv)
        if name in whole:
            src, dst = whole[name]
            index = list(whole).index(name)
            pairs[k, name] = [remote(src.at[k], dst.at[k], sems, (k, index), partner)]
        else:
            src, dst = cut[name]
            index = 4 + 2 * list(cut).index(name)
            pairs[k, name] = [
                remote(src.at[k, :, columns(name, hi, 1 - core)], dst.at[k, hi], sems, (k, index + hi), partner)
                for hi in range(2)
            ]

    def take(k, name):
        for copy in pairs[k, name]:
            copy.wait_recv()

    orders = ("xyz", "zyx", "yxz")
    rings = {}

    def chunk(k, p, phase, t, half):
        t = lax.rem(t + 4, 4)
        if phase == 0:
            return part.at[k, p, t, pl.ds(2 * half, 2)]
        return part2.at[k, p, t, pl.ds(32 * half, 32)]

    def ring_bufs(k, p, phase):
        if phase == 0:
            halves = [[side.at[k, p, s, pl.ds(2 * h, 2)] for h in range(2)] for s in range(2)]
            return [fwd.at[k, p, s] for s in range(2)], [fsum.at[k, p, s] for s in range(2)], halves
        halves = [[side2.at[k, p, s, pl.ds(32 * h, 32)] for h in range(2)] for s in range(2)]
        return [fwd2.at[k, p, s] for s in range(2)], [fsum2.at[k, p, s] for s in range(2)], halves

    def f32(ref):
        return ref[...].astype(F32)

    def ring_start(k, p, phase):
        axis = orders[p][phase]
        t = {"x": x, "y": y, "z": z}[axis]
        after, before = along(axis, 1), along(axis, -1)
        f, _, halves = ring_bufs(k, p, phase)
        sems = (ring_send, ring_recv)
        o = 6 * phase
        rings[k, p, phase] = [
            remote(chunk(k, p, phase, t + 2, 0), f[0], sems, (k, p, o), after),
            remote(chunk(k, p, phase, t + 2, 1), f[1], sems, (k, p, o + 1), before),
            remote(chunk(k, p, phase, t + 1, 1), halves[0][1], sems, (k, p, o + 2), after),
            remote(chunk(k, p, phase, t - 1, 0), halves[1][0], sems, (k, p, o + 3), before),
        ]

    def ring_mid(k, p, phase):
        axis = orders[p][phase]
        t = {"x": x, "y": y, "z": z}[axis]
        after, before = along(axis, 1), along(axis, -1)
        f, fs, halves = ring_bufs(k, p, phase)
        copies = rings[k, p, phase]
        sems = (ring_send, ring_recv)
        o = 6 * phase
        copies[0].wait_recv()
        fs[0][...] = (f32(f[0]) + f32(chunk(k, p, phase, t + 1, 0))).astype(BF)
        copies.append(remote(fs[0], halves[0][0], sems, (k, p, o + 4), after))
        copies[1].wait_recv()
        fs[1][...] = (f32(f[1]) + f32(chunk(k, p, phase, t - 1, 1))).astype(BF)
        copies.append(remote(fs[1], halves[1][1], sems, (k, p, o + 5), before))

    def ring_end(k, p, phase):
        axis = orders[p][phase]
        t = {"x": x, "y": y, "z": z}[axis]
        for copy in rings[k, p, phase][2:]:
            copy.wait_recv()
        if phase == 0:
            total = f32(part.at[k, p, t]) + f32(side.at[k, p, 0]) + f32(side.at[k, p, 1])
            part2[k, p] = total.astype(BF)
            ring_start(k, p, 1)
            return
        total = f32(part2.at[k, p, t]) + f32(side2.at[k, p, 0]) + f32(side2.at[k, p, 1])
        for s in range(4):
            if p == 0:
                rows = (total[12 * s : 12 * s + 12], total[48 + 4 * s : 52 + 4 * s])
                rows = jnp.concatenate(rows, 0)
            elif p == 1:
                rows = total[16 * s : 16 * s + 16]
            else:
                rows = [total[16 * hb + 4 * s : 16 * hb + 4 * s + 4] for hb in range(4)]
                rows = jnp.concatenate(rows, 0)
            part3[k, p, s] = rows
        axis = orders[p][2]
        t = {"x": x, "y": y, "z": z}[axis]
        rings[k, p, 2] = [
            remote(
                part3.at[k, p, lax.rem(t + s, 4)], side3.at[k, p, s - 1], (ring_send, ring_recv),
                (k, p, 11 + s), along(axis, s),
            )
            for s in (1, 2, 3)
        ]

    def ring_last(k, p):
        t = {"x": x, "y": y, "z": z}[orders[p][2]]
        for copy in rings[k, p, 2]:
            copy.wait_recv()
        total = part3[k, p, t] + side3[k, p, 0] + side3[k, p, 1] + side3[k, p, 2]
        if p == 0:
            oqkv_ref[:, k, :] = total[0:12]
            oproj_ref[k] = total[12:16]
        elif p == 1:
            oup_ref[k] = total
        else:
            for hb in range(4):
                odown_ref[k, :, hb * C : hb * C + C] = total[4 * hb : 4 * hb + 4]

    def both(k, name, hi, own, theirs):
        src, dst = cut[name]
        return tn(src[k, :, columns(name, hi, core)], own) + tn(dst[k, hi], theirs)

    def grads_a(k):
        for name in ("n1", "att", "ep", "eq"):
            take(k, name)
        for hi in range(2):
            g = both(k, "eq", hi, n1[k], pn1[k]).astype(BF)
            for at in range(8):
                part[k, 0, 2 * hi + at % 2, at // 2, 0:48, :] = g[48 * at : 48 * at + 48]
            g = both(k, "ep", hi, att[k], patt[k]).astype(BF)
            for at in range(8):
                part[k, 0, 2 * hi + at % 2, at // 2, 48:64, :] = g[16 * at : 16 * at + 16]
        ring_start(k, 0, 0)

    def grads_b(k):
        for name in ("n2", "eu"):
            take(k, name)
        for hi in range(2):
            g = both(k, "eu", hi, n2[k], pn2[k]).astype(BF)
            for at in range(32):
                row = (2 * hi + at // 4 % 2) * 16
                part[k, 1, at % 4, at // 8, row : row + 16, :] = g[16 * at : 16 * at + 16]
        ring_start(k, 1, 0)

    def grads_c(k):
        for name in ("hs", "ed"):
            take(k, name)
        for hi in range(2):
            for hb in range(4):
                cols = slice(hb * C, hb * C + C)
                g = both(k, "ed", hi, hs[k, :, cols], phs[k, :, cols]).astype(BF)
                for at in range(8):
                    row = 16 * hb
                    part[k, 2, at // 2, 2 * hi + at % 2, row : row + 16, :] = g[16 * at : 16 * at + 16]
        ring_start(k, 2, 0)

    def exchange(event, forward):
        copies = []
        for q in range(4):
            a, b = q // 2, q % 2
            di, dj = (a - 1, b - 1) if forward else (a, b)
            if (di, dj) == (0, 0):
                recv[event, 3 - q] = send[event, q]
            else:
                copy = pltpu.make_async_remote_copy(
                    src_ref=send.at[event, q], dst_ref=recv.at[event, 3 - q],
                    send_sem=send_sem.at[event, q], recv_sem=recv_sem.at[event, 3 - q],
                    device_id=device(di, dj), device_id_type=MESH,
                )
                copy.start()
                copies.append(copy)
        return copies

    def finish(copies):
        for copy in copies:
            copy.wait()

    def put(event, tokens):
        send[event] = tn(tos_ref[...], tokens).astype(BF).reshape(4, SLOT, C)

    def got(event):
        return nn(tos_ref[...], recv[event].reshape(4 * SLOT, C))

    nat[...] = jnp.zeros_like(nat)
    nat[:, 0:WLON, :] = up_ref[...]
    send[0] = nn(son_ref[...], nat[...].reshape(12 * 16, C)).astype(BF).reshape(4, SLOT, C)
    up_copies = exchange(0, True)

    lane = lax.broadcasted_iota(jnp.int32, (1, 128), 1)
    head_mask = [((lane >= 32 * s) & (lane < 32 * s + 32)).astype(BF) for s in range(4)]
    half_t = lax.broadcasted_iota(jnp.int32, (T, T), 0) < T // 2
    half_s = lax.broadcasted_iota(jnp.int32, (T, T), 1) < T // 2
    apart = jnp.where(half_t == half_s, 0.0, 1.0).astype(F32)
    last = jnp.where(i == nlat - 1, 1.0, 0.0).astype(F32)

    def forward(k, x):
        xs[k] = x
        nhat, rstd = norm(x)
        n1h[k] = nhat
        r1[k] = jnp.broadcast_to(rstd, (T, 128))
        n1[k] = nhat.astype(BF)
        give(k, "n1")
        fetches[4 * k].wait()

        @pl.loop(0, 3)
        def _(s):
            cols = pl.ds(pl.multiple_of(s * C, C), C)
            us[k, :, cols] = nn(n1[k], wqkv[k, :, cols]).astype(BF)

        @pl.loop(0, 4)
        def _(g):
            def part(w):
                return us[k, :, pl.ds(pl.multiple_of(w * C + g * 128, 128), 128)]

            q, key, v = part(0), part(1), part(2)
            total = jnp.zeros((T, 128), F32)
            for s in range(4):
                e = jnp.exp(nt(q * head_mask[s], key) * (32**-0.5))
                if k == 1:
                    e = e * (1.0 - last * apart)
                p = (e / jnp.sum(e, -1, keepdims=True)).astype(BF)
                ps[k, g * 4 + s] = p
                total += nn(p, v * head_mask[s])
            att[k, :, pl.ds(pl.multiple_of(g * 128, 128), 128)] = total.astype(BF)

        give(k, "att")
        fetches[4 * k + 1].wait()
        m = xs[k] + nn(att[k], wproj[k])
        acc[...] = m
        nhat, rstd = norm(m)
        n2h[k] = nhat
        r2[k] = jnp.broadcast_to(rstd, (T, 128))
        n2[k] = nhat.astype(BF)
        give(k, "n2")
        fetches[4 * k + 2].wait()
        fetches[4 * k + 3].wait()

        @pl.loop(0, 4)
        def _(s):
            cols = pl.ds(pl.multiple_of(s * C, C), C)
            z = nn(n2[k], wup[k, :, cols])
            cdf = 0.5 * (1.0 + lax.erf(z * (2.0**-0.5)))
            gp[k, :, cols] = cdf + z * (jnp.exp(-0.5 * z * z) * ((2.0 * np.pi) ** -0.5))
            h = (z * cdf).astype(BF)
            hs[k, :, cols] = h
            acc[...] += nn(h, wdown[k, cols, :])

        give(k, "hs")
        return acc[...]

    def backward(k, ct, after_up, after_proj, amid):
        acc[...] = ct
        ed[k] = ct.astype(BF)
        give(k, "ed")

        @pl.loop(0, 4)
        def _(s):
            cols = pl.ds(pl.multiple_of(s * C, C), C)
            dh = nt(ed[k], wdown[k, cols, :]).astype(BF).astype(F32)
            eu[k, :, cols] = (dh * gp[k, :, cols]).astype(BF)

        give(k, "eu")
        after_up()
        dn2 = nt(eu[k], wup[k]).astype(BF).astype(F32)
        dm = acc[...] + norm_back(dn2, n2h[k], r2[k][:, 0:1])
        acc[...] = dm
        ep[k] = dm.astype(BF)
        give(k, "ep")
        grads_c(k)
        dab[...] = nt(ep[k], wproj[k]).astype(BF)
        grads_b(k)
        after_proj()

        def heads(g):
            def at(w):
                return pl.ds(pl.multiple_of(w * C + g * 128, 128), 128)

            q, key, v = us[k, :, at(0)], us[k, :, at(1)], us[k, :, at(2)]
            da = dab[:, at(0)]
            dq = jnp.zeros((T, 128), F32)
            dk = jnp.zeros((T, 128), F32)
            dv = jnp.zeros((T, 128), F32)
            for s in range(4):
                p = ps[k, g * 4 + s]
                dah = da * head_mask[s]
                dp = nt(dah, v).astype(BF).astype(F32)
                dv += tn(p, dah)
                pf = p.astype(F32)
                ds = pf * (dp - jnp.sum(dp * pf, -1, keepdims=True))
                ds = (ds * (32**-0.5)).astype(BF)
                dq += nn(ds, key * head_mask[s])
                dk += tn(ds, q * head_mask[s])
            eq[k, :, at(0)] = dq.astype(BF)
            eq[k, :, at(1)] = dk.astype(BF)
            eq[k, :, at(2)] = dv.astype(BF)

        pl.loop(0, 2)(heads)
        amid()
        pl.loop(2, 4)(heads)
        give(k, "eq")

    def backward_end(k):
        dn1 = nt(eq[k], wqkv[k]).astype(BF).astype(F32)
        return acc[...] + norm_back(dn1, n1h[k], r1[k][:, 0:1])

    def nothing():
        pass

    swap_fetch.wait()
    lane_finish(0, own)
    for half in range(2):
        moved = nn(came[half].reshape(64, 1024), swap[...]).astype(BF)
        for lr in range(8 if half == 0 else 4):
            for g in range(4):
                at = (slice(128 * half + 16 * lr, 128 * half + 16 * lr + 16), slice(128 * g, 128 * g + 128))
                nat2[at] = moved[16 * g : 16 * g + 16, 128 * lr : 128 * lr + 128]
    first = forward(0, nn(ton_ref[...], nat2[...]))
    put(1, first.astype(BF))
    finish(exchange(1, True))
    second = forward(1, got(1))
    put(2, second.astype(BF))
    mixed_copies = exchange(2, False)
    finish(up_copies)

    def amid_one():
        ring_mid(1, 2, 0)

    backward(1, got(0), nothing, nothing, amid_one)
    ring_mid(1, 1, 0)
    d_second = backward_end(1)
    put(3, d_second.astype(BF))
    mid_copies = exchange(3, False)
    ring_end(1, 2, 0)
    grads_a(1)
    ring_end(1, 1, 0)
    ring_mid(1, 2, 1)
    finish(mid_copies)

    def up_zero():
        ring_mid(1, 0, 0)
        ring_mid(1, 1, 1)
        ring_end(1, 2, 1)

    def proj_zero():
        ring_end(1, 0, 0)
        ring_end(1, 1, 1)
        ring_last(1, 2)

    def amid_zero():
        ring_mid(1, 0, 1)
        ring_mid(0, 2, 0)
        ring_mid(0, 1, 0)
        ring_last(1, 1)

    backward(0, got(3), up_zero, proj_zero, amid_zero)
    grads_a(0)
    ring_end(1, 0, 1)
    ring_end(0, 2, 0)
    ring_end(0, 1, 0)
    d_first = backward_end(0)
    nat2[...] = tn(ton_ref[...], d_first.astype(BF)).astype(BF)
    for half in range(2):
        for lr in range(8):
            for g in range(4):
                at = (slice(16 * g, 16 * g + 16), slice(128 * lr, 128 * lr + 128))
                if half == 1 and lr >= 4:
                    turned[half, at[0], at[1]] = jnp.zeros((16, 128), BF)
                else:
                    row = 128 * half + 16 * lr
                    turned[half, at[0], at[1]] = nat2[row : row + 16, 128 * g : 128 * g + 128]
        moved = nn(turned[half], swap[...]).astype(BF)
        for g in range(4):
            for lane_block in range(8):
                leave2[8 * g + lane_block, half] = moved[
                    16 * g : 16 * g + 16, 128 * lane_block : 128 * lane_block + 128
                ]
    own = lane_start(1)
    ring_mid(0, 0, 0)
    ring_mid(0, 2, 1)
    ring_mid(0, 1, 1)
    ring_last(1, 0)
    finish(mixed_copies)
    natural = tn(son_ref[...], recv[2].reshape(4 * SLOT, C)).astype(BF)
    mixed_ref[...] = natural.reshape(12, 16, C)[:, 0:WLON, :]
    ring_end(0, 0, 0)
    ring_end(0, 2, 1)
    ring_end(0, 1, 1)
    ring_mid(0, 0, 1)
    ring_last(0, 2)
    ring_last(0, 1)
    lane_finish(1, own)
    for half in range(2):
        rows = tn(came2[:, half].reshape(512, 128), spread_ref[...]).astype(BF)
        n = 8 if half == 0 else 4
        denc_ref[8 * half : 8 * half + n] = rows[0 : 16 * n].reshape(n, 16, 32 * WLON)
    ring_end(0, 0, 1)
    ring_last(0, 0)
    for copy in sent:
        copy.wait_send()


def layers(encoded, upstream, w_qkv, w_proj, w_up, w_down):
    vmem = pl.BlockSpec(memory_space=pltpu.VMEM)
    hbm = pl.BlockSpec(memory_space=pl.ANY)
    dma = pltpu.SemaphoreType.DMA
    V = pltpu.VMEM
    return pl.pallas_call(
        layers_kernel,
        out_shape=(
            jax.ShapeDtypeStruct((12, WLON, C), BF),
            jax.ShapeDtypeStruct((12, 16, 32 * WLON), BF),
            jax.ShapeDtypeStruct((12, 2, C), F32),
            jax.ShapeDtypeStruct((2, 4, C), F32),
            jax.ShapeDtypeStruct((2, 16, C), F32),
            jax.ShapeDtypeStruct((2, 4, FF), F32),
        ),
        in_specs=[vmem] * 6 + [hbm] * 5,
        out_specs=(vmem,) * 6,
        scratch_shapes=[
            V((2, C, 3 * C), BF), V((2, C, C), BF), V((2, C, FF), BF), V((2, FF, C), BF),
            dma((2, 4)),
            V((1024, 1024), BF), dma, V((32, 2, 16, 128), BF), V((2, 4, 16, 1024), BF),
            V((32, 2, 16, 128), BF), V((32, 2, 16, 128), BF), dma((2, 32)), dma((2, 32)), dma((2,)),
            V((12 * 16, C), BF), V((2, 64, 1024), BF),
            V((12, 16, C), BF), V((4, 4, SLOT, C), BF), V((4, 4, SLOT, C), BF),
            dma((4, 4)), dma((4, 4)),
            V((2, T, C), F32), V((2, T, C), F32), V((2, T, C), BF), V((2, T, 128), F32),
            V((2, T, 3 * C), BF), V((2, HEADS, T, T), BF), V((2, T, C), BF),
            V((2, T, C), F32), V((2, T, C), BF), V((2, T, 128), F32),
            V((2, T, FF), F32), V((2, T, FF), BF), V((T, C), F32),
            V((2, T, 3 * C), BF), V((2, T, C), BF), V((2, T, FF), BF), V((2, T, C), BF), V((T, C), BF),
            V((2, T, C), BF), V((2, T, C), BF), V((2, T, C), BF), V((2, T, FF), BF),
            V((2, 2, T, 384), BF), V((2, 2, T, 128), BF), V((2, 2, T, 512), BF), V((2, 2, T, 128), BF),
            dma((2, 12)), dma((2, 12)),
            V((2, 3, 4, 4, 64, C), BF), V((2, 3, 2, 2, 64, C), BF), V((2, 3, 2, 2, 64, C), BF),
            V((2, 3, 2, 4, 64, C), BF),
            V((2, 3, 4, 64, C), BF), V((2, 3, 2, 32, C), BF), V((2, 3, 2, 32, C), BF),
            V((2, 3, 2, 64, C), BF),
            V((2, 3, 4, 16, C), F32), V((2, 3, 3, 16, C), F32),
            dma((2, 3, 15)), dma((2, 3, 15)),
        ],
        compiler_params=pltpu.CompilerParams(
            collective_id=0, has_side_effects=True, vmem_limit_bytes=60 * 2**20
        ),
    )(encoded, upstream, *permutations(), w_qkv, w_proj, w_up, w_down)


def on_device(encoded, upstream, w_qkv, w_proj, w_up, w_down):
    mixed, dencoded, qkv, proj, up, down = layers(
        encoded.reshape(12, 16, 32 * WLON), upstream.reshape(12, WLON, C), w_qkv, w_proj, w_up, w_down
    )
    return (
        mixed.reshape(upstream.shape),
        dencoded.reshape(encoded.shape),
        qkv.transpose(1, 2, 0),
        proj.swapaxes(1, 2),
        up.swapaxes(1, 2),
        down.swapaxes(1, 2),
    )


def solution(mesh):
    return jax.shard_map(
        on_device,
        mesh=mesh,
        in_specs=(P(None, "lat", "lon", None), P(None, "lat", "lon", None), P(), P(), P(), P()),
        out_specs=(
            P(None, "lat", "lon", None),
            P(None, "lat", "lon", None),
            P(None, None, ("lat", "lon")),
            P(None, None, ("lat", "lon")),
            P(None, None, ("lat", "lon")),
            P(None, None, ("lat", "lon")),
        ),
        check_vma=False,
    )
```

```python
import functools

import jax
import jax.numpy as jnp
import numpy as np
from jax import lax
from jax.experimental import pallas as pl
from jax.experimental.pallas import tpu as pltpu
from jax.sharding import PartitionSpec as P

HEADS = 16
WLAT = 6
WLON = 12
LEV = 2
C = 512
FF = 2048
T = LEV * WLAT * WLON
QUAD = T // 4
SLOT = 48
NORM_EPS = 1e-05
MESH = pl.DeviceIdType.MESH
BF = jnp.bfloat16
F32 = jnp.float32


def quadrant_order():
    return [
        (l, 3 * a + r, 6 * b + c)
        for a in range(2)
        for b in range(2)
        for l in range(LEV)
        for r in range(3)
        for c in range(6)
    ]


def permutations():
    slots_of_natural = np.zeros((4 * SLOT, T), np.float32)
    tokens_of_slots = np.zeros((T, 4 * SLOT), np.float32)
    tokens_of_padded = np.zeros((T, 12 * 16), np.float32)
    for t, (l, r, c) in enumerate(quadrant_order()):
        slot = t // QUAD * SLOT + t % QUAD
        slots_of_natural[slot, (r * WLON + c) * LEV + l] = 1
        tokens_of_slots[t, slot] = 1
        tokens_of_padded[t, (l * WLAT + r) * 16 + c] = 1
    spread = np.zeros((32 * 16, 32 * WLON), np.float32)
    for col in range(32 * WLON):
        spread[col // WLON * 16 + col % WLON, col] = 1
    swap = np.eye(1024, dtype=np.float32).reshape(8, 8, 16, 1024).swapaxes(0, 1).reshape(1024, 1024)
    matrices = (slots_of_natural, tokens_of_slots, tokens_of_padded, spread, swap)
    return [jnp.asarray(m, BF) for m in matrices]


def nn(a, b):
    return lax.dot_general(a, b, (((1,), (0,)), ((), ())), preferred_element_type=F32)


def nt(a, b):
    return lax.dot_general(a, b, (((1,), (1,)), ((), ())), preferred_element_type=F32)


def tn(a, b):
    return lax.dot_general(a, b, (((0,), (0,)), ((), ())), preferred_element_type=F32)


def norm(x):
    centred = x - jnp.mean(x, -1, keepdims=True)
    rstd = lax.rsqrt(jnp.mean(centred * centred, -1, keepdims=True) + NORM_EPS)
    return centred * rstd, rstd


def norm_back(dn, nhat, rstd):
    return rstd * (
        dn - jnp.mean(dn, -1, keepdims=True) - nhat * jnp.mean(dn * nhat, -1, keepdims=True)
    )


def layers_kernel(
    enc_hbm, up_hbm, son_hbm, tos_hbm, ton_hbm, spread_hbm, swap_hbm,
    wqkv_hbm, wproj_hbm, wup_hbm, wdown_hbm,
    mixed_hbm, denc_hbm, oqkv_hbm, oproj_hbm, oup_hbm, odown_hbm,
    enc_ref, up_ref, son_ref, tos_ref, ton_ref, spread_ref, in_sem,
    mixed_ref, denc_ref, oqkv_ref, oproj_ref, oup_ref, odown_ref, out_sem,
    wqkv, wproj, wup, wdown, wsem,
    swap, leave, came, leave2, came2, lane_send, lane_recv, own_sem, nat2, turned, send, recv, send_sem, recv_sem,
    xs, n1h, n1, r1, us, ps, att, n2h, n2, r2, gp, hs, acc, eq, ep, eu, ed, dab,
    pn1, patt, pn2, phs, peq, pep, peu, ped, pair_send, pair_recv,
    part, fwd, fsum, side, plane_out, plane_in, ring_send, ring_recv, plane_send, plane_recv,
):
    i, j = lax.axis_index("lat"), lax.axis_index("lon")
    nlat, nlon = lax.axis_size("lat"), lax.axis_size("lon")

    def device(di, dj):
        return (lax.rem(i + di + nlat, nlat), lax.rem(j + dj + nlon, nlon))

    core, z, y = lax.rem(i, 2), lax.rem(j, 4), j // 8
    x = i // 2 * 2 + lax.rem(j // 4, 2)

    def along(axis, steps):
        at = {"x": x, "y": y, "z": z}
        at[axis] = lax.rem(at[axis] + steps + 4, 4)
        return (at["x"] // 2 * 2 + core, at["y"] * 8 + lax.rem(at["x"], 2) * 4 + at["z"])

    def beside(axis, steps, other, others):
        at = {"x": x, "y": y, "z": z}
        at[axis] = lax.rem(at[axis] + steps + 4, 4)
        at[other] = lax.rem(at[other] + others + 4, 4)
        return (at["x"] // 2 * 2 + core, at["y"] * 8 + lax.rem(at["x"], 2) * 4 + at["z"])

    partner = (i + 1 - 2 * core, j)

    weights = ((wqkv_hbm, wqkv), (wproj_hbm, wproj), (wup_hbm, wup), (wdown_hbm, wdown))
    inputs = {}
    for at, (name, src, dst) in enumerate(
        (
            ("enc", enc_hbm, enc_ref), ("spread", spread_hbm, spread_ref), ("up", up_hbm, up_ref),
            ("son", son_hbm, son_ref), ("tos", tos_hbm, tos_ref), ("ton", ton_hbm, ton_ref),
            ("swap", swap_hbm, swap),
        )
    ):
        inputs[name] = pltpu.make_async_copy(src, dst, in_sem.at[at])
        inputs[name].start()
    fetches = []
    for k in range(2):
        for w, (src, dst) in enumerate(weights):
            fetch = pltpu.make_async_copy(src.at[k], dst.at[k], wsem.at[k, w])
            fetch.start()
            fetches.append(fetch)

    barrier = pltpu.get_barrier_semaphore()
    offsets = ((0, 1), (1, 0), (1, 1), (0, -1), (-1, 0), (-1, -1))
    greeted = [device(di, dj) for di, dj in offsets]
    greeted += [along(axis, steps) for axis in "xyz" for steps in (1, 2, 3)] + [partner]
    greeted += [beside("x", dx, other, d) for other in "yz" for dx in (1, 2, 3) for d in (1, 2, 3)]
    for other in greeted:
        pl.semaphore_signal(barrier, inc=1, device_id=other, device_id_type=MESH)

    @pl.loop(1, nlon)
    def _(step):
        pl.semaphore_signal(barrier, inc=1, device_id=device(0, step), device_id_type=MESH)

    inputs["enc"].wait()
    inputs["spread"].wait()
    columns_first = nt(spread_ref[...], enc_ref[...].reshape(12 * 16, 32 * WLON)).astype(BF)
    leave[:, 0] = columns_first[:, 0:128].reshape(32, 16, 128)
    leave[:, 1, :, 0:64] = columns_first[:, 128:192].reshape(32, 16, 64)
    leave[:, 1, :, 64:128] = jnp.zeros((32, 16, 64), BF)
    pl.semaphore_wait(barrier, len(greeted) + nlon - 1)
    mine = pl.ds(pl.multiple_of(lax.rem(j, 8) * 128, 128), 128)

    def lane_copy(step, event):
        to = lax.rem(j + step, nlon)
        if event == 0:
            src, dst = leave.at[to], came.at[:, j // 8, :, mine]
        else:
            src, dst = leave2.at[to], came2.at[j]
        return pltpu.make_async_remote_copy(
            src_ref=src, dst_ref=dst, send_sem=lane_send.at[event, step], recv_sem=lane_recv.at[event, step],
            device_id=(i, to), device_id_type=MESH,
        )

    def lane_start(event):
        @pl.loop(1, nlon)
        def _(step):
            lane_copy(step, event).start()

        if event == 0:
            src, dst = leave.at[j], came.at[:, j // 8, :, mine]
        else:
            src, dst = leave2.at[j], came2.at[j]
        own = pltpu.make_async_copy(src, dst, own_sem.at[event])
        own.start()
        return own

    def lane_finish(event, own):
        own.wait()

        @pl.loop(1, nlon)
        def _(step):
            lane_copy(step, event).wait()

    own = lane_start(0)

    def remote(src, dst, sems, index, to):
        copy = pltpu.make_async_remote_copy(
            src_ref=src, dst_ref=dst, send_sem=sems[0].at[index], recv_sem=sems[1].at[index],
            device_id=to, device_id_type=MESH,
        )
        copy.start()
        sent.append(copy)
        return copy

    sent = []
    pairs = {}
    wide = {"eq": 384, "ep": 128, "eu": 512, "ed": 128}
    whole = {"n1": (n1, pn1), "att": (att, patt), "n2": (n2, pn2), "hs": (hs, phs)}
    cut = {"eq": (eq, peq), "ep": (ep, pep), "eu": (eu, peu), "ed": (ed, ped)}

    def columns(name, hi, owner):
        width = wide[name]
        return pl.ds(pl.multiple_of((2 * hi + owner) * width, width), width)

    def give(k, name):
        sems = (pair_send, pair_recv)
        if name in whole:
            src, dst = whole[name]
            index = list(whole).index(name)
            pairs[k, name] = [remote(src.at[k], dst.at[k], sems, (k, index), partner)]
        else:
            src, dst = cut[name]
            index = 4 + 2 * list(cut).index(name)
            pairs[k, name] = [
                remote(src.at[k, :, columns(name, hi, 1 - core)], dst.at[k, hi], sems, (k, index + hi), partner)
                for hi in range(2)
            ]

    def take(k, name):
        for copy in pairs[k, name]:
            copy.wait_recv()

    orders = ("xyz", "yxz", "zyx", "zyx", "xyz", "yxz")
    where = {"x": x, "y": y, "z": z}
    rings = {}

    def chunk(k, p, t, half):
        return part.at[k, p, lax.rem(t + 4, 4), pl.ds(2 * half, 2)]

    def f32(ref):
        return ref[...].astype(F32)

    def ring_start(k, p):
        axis = orders[p][0]
        t = where[axis]
        after, before = along(axis, 1), along(axis, -1)
        sems = (ring_send, ring_recv)
        rings[k, p] = [
            remote(chunk(k, p, t + 2, 0), fwd.at[k, p, 0], sems, (k, p, 0), after),
            remote(chunk(k, p, t + 2, 1), fwd.at[k, p, 1], sems, (k, p, 1), before),
            remote(chunk(k, p, t + 1, 1), side.at[k, p, 0, pl.ds(2, 2)], sems, (k, p, 2), after),
            remote(chunk(k, p, t - 1, 0), side.at[k, p, 1, pl.ds(0, 2)], sems, (k, p, 3), before),
        ]

    def ring_mid(k, p):
        axis = orders[p][0]
        t = where[axis]
        after, before = along(axis, 1), along(axis, -1)
        copies = rings[k, p]
        sems = (ring_send, ring_recv)
        copies[0].wait_recv()
        fsum[k, p, 0] = (f32(fwd.at[k, p, 0]) + f32(chunk(k, p, t + 1, 0))).astype(BF)
        copies.append(remote(fsum.at[k, p, 0], side.at[k, p, 0, pl.ds(0, 2)], sems, (k, p, 4), after))
        copies[1].wait_recv()
        fsum[k, p, 1] = (f32(fwd.at[k, p, 1]) + f32(chunk(k, p, t - 1, 1))).astype(BF)
        copies.append(remote(fsum.at[k, p, 1], side.at[k, p, 1, pl.ds(2, 2)], sems, (k, p, 5), before))

    def plane_copy(k, p, step):
        _, second, third = orders[p]
        d2, d3 = step // 4, lax.rem(step, 4)
        src = plane_out.at[k, p, lax.rem(where[second] + d2, 4), lax.rem(where[third] + d3, 4)]
        return pltpu.make_async_remote_copy(
            src_ref=src, dst_ref=plane_in.at[k, p, step], send_sem=plane_send.at[k, p, step],
            recv_sem=plane_recv.at[k, p, step], device_id=beside(second, d2, third, d3), device_id_type=MESH,
        )

    def ring_end(k, p):
        for copy in rings[k, p][2:]:
            copy.wait_recv()
        t = where[orders[p][0]]
        total = f32(part.at[k, p, t]) + f32(side.at[k, p, 0]) + f32(side.at[k, p, 1])
        for s2 in range(4):
            for s3 in range(4):
                if p // 2 == 0:
                    rows = (total[s2, 12 * s3 : 12 * s3 + 12], total[s2, 48 + 4 * s3 : 52 + 4 * s3])
                    rows = jnp.concatenate(rows, 0)
                elif p // 2 == 1:
                    rows = total[s2, 16 * s3 : 16 * s3 + 16]
                else:
                    rows = [total[s2, 16 * hb + 4 * s3 : 16 * hb + 4 * s3 + 4] for hb in range(4)]
                    rows = jnp.concatenate(rows, 0)
                plane_out[k, p, s2, s3] = rows.astype(BF)

        @pl.loop(1, 16)
        def _(step):
            plane_copy(k, p, step).start()

    def ring_last(k, p):
        @pl.loop(1, 16)
        def _(step):
            plane_copy(k, p, step).wait()

        _, second, third = orders[p]
        total = f32(plane_out.at[k, p, where[second], where[third]])
        for step in range(1, 16):
            total += f32(plane_in.at[k, p, step])
        lanes = slice(256 * (p % 2), 256 * (p % 2) + 256)
        if p // 2 == 0:
            oqkv_ref[:, k, lanes] = total[0:12]
            oproj_ref[k, :, lanes] = total[12:16]
        elif p // 2 == 1:
            oup_ref[k, :, lanes] = total
        else:
            for hb in range(4):
                at = slice(hb * C + lanes.start, hb * C + lanes.stop)
                odown_ref[k, :, at] = total[4 * hb : 4 * hb + 4]

    def both(k, name, hi, own, theirs):
        src, dst = cut[name]
        return tn(src[k, :, columns(name, hi, core)], own) + tn(dst[k, hi], theirs)

    def keep(k, p, first, second, rows, g):
        for s in range(2):
            at = (first, second) if orders[p + s][0] == orders[p][0] else (second, first)
            part[k, p + s, at[0], at[1], rows, :] = g[:, 256 * s : 256 * s + 256]

    def grads_a(k):
        for name in ("n1", "att", "ep", "eq"):
            take(k, name)
        for hi in range(2):
            g = both(k, "eq", hi, n1[k], pn1[k]).astype(BF)
            for at in range(8):
                keep(k, 0, 2 * hi + at % 2, at // 2, slice(0, 48), g[48 * at : 48 * at + 48])
            g = both(k, "ep", hi, att[k], patt[k]).astype(BF)
            for at in range(8):
                keep(k, 0, 2 * hi + at % 2, at // 2, slice(48, 64), g[16 * at : 16 * at + 16])
        ring_start(k, 0)
        ring_start(k, 1)

    def grads_b(k):
        for name in ("n2", "eu"):
            take(k, name)
        for hi in range(2):
            g = both(k, "eu", hi, n2[k], pn2[k]).astype(BF)
            for at in range(32):
                row = (2 * hi + at // 4 % 2) * 16
                keep(k, 2, at % 4, at // 8, slice(row, row + 16), g[16 * at : 16 * at + 16])
        ring_start(k, 2)
        ring_start(k, 3)

    def grads_c(k):
        for name in ("hs", "ed"):
            take(k, name)
        for hi in range(2):
            for hb in range(4):
                cols = slice(hb * C, hb * C + C)
                g = both(k, "ed", hi, hs[k, :, cols], phs[k, :, cols]).astype(BF)
                for at in range(8):
                    row = 16 * hb
                    keep(k, 4, 2 * hi + at % 2, at // 2, slice(row, row + 16), g[16 * at : 16 * at + 16])
        ring_start(k, 4)
        ring_start(k, 5)

    def exchange(event, forward):
        copies = []
        for q in range(4):
            a, b = q // 2, q % 2
            di, dj = (a - 1, b - 1) if forward else (a, b)
            if (di, dj) == (0, 0):
                recv[event, 3 - q] = send[event, q]
            else:
                copy = pltpu.make_async_remote_copy(
                    src_ref=send.at[event, q], dst_ref=recv.at[event, 3 - q],
                    send_sem=send_sem.at[event, q], recv_sem=recv_sem.at[event, 3 - q],
                    device_id=device(di, dj), device_id_type=MESH,
                )
                copy.start()
                copies.append(copy)
        return copies

    def finish(copies):
        for copy in copies:
            copy.wait()

    def put(event, tokens):
        send[event] = tn(tos_ref[...], tokens).astype(BF).reshape(4, SLOT, C)

    def got(event):
        return nn(tos_ref[...], recv[event].reshape(4 * SLOT, C))

    for name in ("up", "son", "tos", "ton"):
        inputs[name].wait()
    send[0] = nn(son_ref[...], up_ref[...].reshape(T, C)).astype(BF).reshape(4, SLOT, C)
    up_copies = exchange(0, True)

    lane = lax.broadcasted_iota(jnp.int32, (1, 128), 1)
    head_mask = [((lane >= 32 * s) & (lane < 32 * s + 32)).astype(BF) for s in range(4)]
    half_t = lax.broadcasted_iota(jnp.int32, (T, T), 0) < T // 2
    half_s = lax.broadcasted_iota(jnp.int32, (T, T), 1) < T // 2
    apart = jnp.where(half_t == half_s, 0.0, 1.0).astype(F32)
    last = jnp.where(i == nlat - 1, 1.0, 0.0).astype(F32)

    def forward(k, x):
        xs[k] = x
        nhat, rstd = norm(x)
        n1h[k] = nhat
        r1[k] = jnp.broadcast_to(rstd, (T, 128))
        n1[k] = nhat.astype(BF)
        give(k, "n1")
        fetches[4 * k].wait()

        @pl.loop(0, 3)
        def _(s):
            cols = pl.ds(pl.multiple_of(s * C, C), C)
            us[k, :, cols] = nn(n1[k], wqkv[k, :, cols]).astype(BF)

        @pl.loop(0, 4)
        def _(g):
            def part(w):
                return us[k, :, pl.ds(pl.multiple_of(w * C + g * 128, 128), 128)]

            q, key, v = part(0), part(1), part(2)
            total = jnp.zeros((T, 128), F32)
            for s in range(4):
                e = jnp.exp(nt(q * head_mask[s], key) * (32**-0.5))
                if k == 1:
                    e = e * (1.0 - last * apart)
                p = (e / jnp.sum(e, -1, keepdims=True)).astype(BF)
                ps[k, g * 4 + s] = p
                total += nn(p, v * head_mask[s])
            att[k, :, pl.ds(pl.multiple_of(g * 128, 128), 128)] = total.astype(BF)

        give(k, "att")
        fetches[4 * k + 1].wait()
        m = xs[k] + nn(att[k], wproj[k])
        acc[...] = m
        nhat, rstd = norm(m)
        n2h[k] = nhat
        r2[k] = jnp.broadcast_to(rstd, (T, 128))
        n2[k] = nhat.astype(BF)
        give(k, "n2")
        fetches[4 * k + 2].wait()
        fetches[4 * k + 3].wait()

        @pl.loop(0, 4)
        def _(s):
            cols = pl.ds(pl.multiple_of(s * C, C), C)
            z = nn(n2[k], wup[k, :, cols])
            cdf = 0.5 * (1.0 + lax.erf(z * (2.0**-0.5)))
            gp[k, :, cols] = cdf + z * (jnp.exp(-0.5 * z * z) * ((2.0 * np.pi) ** -0.5))
            h = (z * cdf).astype(BF)
            hs[k, :, cols] = h
            acc[...] += nn(h, wdown[k, cols, :])

        give(k, "hs")
        return acc[...]

    def backward(k, ct, after_up, after_proj, amid):
        acc[...] = ct
        ed[k] = ct.astype(BF)
        give(k, "ed")

        @pl.loop(0, 4)
        def _(s):
            cols = pl.ds(pl.multiple_of(s * C, C), C)
            dh = nt(ed[k], wdown[k, cols, :]).astype(BF).astype(F32)
            eu[k, :, cols] = (dh * gp[k, :, cols]).astype(BF)

        give(k, "eu")
        after_up()
        dn2 = nt(eu[k], wup[k]).astype(BF).astype(F32)
        dm = acc[...] + norm_back(dn2, n2h[k], r2[k][:, 0:1])
        acc[...] = dm
        ep[k] = dm.astype(BF)
        give(k, "ep")
        grads_c(k)
        dab[...] = nt(ep[k], wproj[k]).astype(BF)
        grads_b(k)
        after_proj()

        def heads(g):
            def at(w):
                return pl.ds(pl.multiple_of(w * C + g * 128, 128), 128)

            q, key, v = us[k, :, at(0)], us[k, :, at(1)], us[k, :, at(2)]
            da = dab[:, at(0)]
            dq = jnp.zeros((T, 128), F32)
            dk = jnp.zeros((T, 128), F32)
            dv = jnp.zeros((T, 128), F32)
            for s in range(4):
                p = ps[k, g * 4 + s]
                dah = da * head_mask[s]
                dp = nt(dah, v).astype(BF).astype(F32)
                dv += tn(p, dah)
                pf = p.astype(F32)
                ds = pf * (dp - jnp.sum(dp * pf, -1, keepdims=True))
                ds = (ds * (32**-0.5)).astype(BF)
                dq += nn(ds, key * head_mask[s])
                dk += tn(ds, q * head_mask[s])
            eq[k, :, at(0)] = dq.astype(BF)
            eq[k, :, at(1)] = dk.astype(BF)
            eq[k, :, at(2)] = dv.astype(BF)

        for half in range(2):
            pl.loop(2 * half, 2 * half + 2)(heads)
            amid(half)
        give(k, "eq")

    def backward_end(k):
        dn1 = nt(eq[k], wqkv[k]).astype(BF).astype(F32)
        return acc[...] + norm_back(dn1, n1h[k], r1[k][:, 0:1])

    def nothing():
        pass

    inputs["swap"].wait()
    lane_finish(0, own)
    for half in range(2):
        moved = nn(came[half].reshape(64, 1024), swap[...]).astype(BF)
        for lr in range(8 if half == 0 else 4):
            for g in range(4):
                at = (slice(128 * half + 16 * lr, 128 * half + 16 * lr + 16), slice(128 * g, 128 * g + 128))
                nat2[at] = moved[16 * g : 16 * g + 16, 128 * lr : 128 * lr + 128]
    first = forward(0, nn(ton_ref[...], nat2[...]))
    put(1, first.astype(BF))
    finish(exchange(1, True))
    second = forward(1, got(1))
    put(2, second.astype(BF))
    mixed_copies = exchange(2, False)
    finish(up_copies)

    def mids(k, parts):
        for p in parts:
            ring_mid(k, p)

    def ends(k, parts):
        for p in parts:
            ring_end(k, p)

    def lasts(k, parts):
        for p in parts:
            ring_last(k, p)

    def amid_one(half):
        if half == 1:
            mids(1, (4, 5))

    backward(1, got(0), nothing, nothing, amid_one)
    d_second = backward_end(1)
    put(3, d_second.astype(BF))
    mid_copies = exchange(3, False)
    grads_a(1)
    mids(1, (2, 3))
    finish(mid_copies)

    def up_zero():
        ends(1, (4, 5))
        mids(1, (0, 1))

    def proj_zero():
        ends(1, (2, 3))

    def amid_zero(half):
        if half == 0:
            ends(1, (0, 1))
        else:
            mids(0, (4, 5, 2, 3))

    backward(0, got(3), up_zero, proj_zero, amid_zero)
    grads_a(0)
    ends(0, (4, 5))
    d_first = backward_end(0)
    nat2[...] = tn(ton_ref[...], d_first.astype(BF)).astype(BF)
    for half in range(2):
        for lr in range(8):
            for g in range(4):
                at = (slice(16 * g, 16 * g + 16), slice(128 * lr, 128 * lr + 128))
                if half == 1 and lr >= 4:
                    turned[half, at[0], at[1]] = jnp.zeros((16, 128), BF)
                else:
                    row = 128 * half + 16 * lr
                    turned[half, at[0], at[1]] = nat2[row : row + 16, 128 * g : 128 * g + 128]
        moved = nn(turned[half], swap[...]).astype(BF)
        for g in range(4):
            for lane_block in range(8):
                leave2[8 * g + lane_block, half] = moved[
                    16 * g : 16 * g + 16, 128 * lane_block : 128 * lane_block + 128
                ]
    own = lane_start(1)
    mids(0, (0, 1))
    ends(0, (2, 3))
    finish(mixed_copies)
    natural = tn(son_ref[...], recv[2].reshape(4 * SLOT, C)).astype(BF)
    mixed_ref[...] = natural.reshape(T // LEV, LEV, C)
    stores = []

    def store(src, dst):
        stores.append(pltpu.make_async_copy(src, dst, out_sem.at[len(stores)]))
        stores[-1].start()

    store(mixed_ref, mixed_hbm)
    lasts(1, range(6))
    ends(0, (0, 1))
    lasts(0, (4, 5, 2, 3))
    store(oup_ref, oup_hbm)
    store(odown_ref, odown_hbm)
    lane_finish(1, own)
    for half in range(2):
        rows = tn(came2[:, half].reshape(512, 128), spread_ref[...]).astype(BF)
        n = 8 if half == 0 else 4
        denc_ref[8 * half : 8 * half + n] = rows[0 : 16 * n].reshape(n, 16, 32 * WLON)
    store(denc_ref, denc_hbm)
    lasts(0, (0, 1))
    store(oqkv_ref, oqkv_hbm)
    store(oproj_ref, oproj_hbm)
    for copy in sent:
        copy.wait_send()
    finish(stores)


def copies_kernel(*refs):
    copies = [pltpu.make_async_copy(refs[n], refs[6 + n], refs[12].at[n]) for n in range(6)]
    for copy in copies:
        copy.start()
    for copy in copies:
        copy.wait()


def layers(encoded, upstream, w_qkv, w_proj, w_up, w_down):
    hbm = pl.BlockSpec(memory_space=pl.ANY)
    dma = pltpu.SemaphoreType.DMA
    V = pltpu.VMEM
    shapes = (
        jax.ShapeDtypeStruct((T // LEV, LEV, C), BF),
        jax.ShapeDtypeStruct((12, 16, 32 * WLON), BF),
        jax.ShapeDtypeStruct((12, 2, C), F32),
        jax.ShapeDtypeStruct((2, 4, C), F32),
        jax.ShapeDtypeStruct((2, 16, C), F32),
        jax.ShapeDtypeStruct((2, 4, FF), F32),
    )
    results = pl.pallas_call(
        layers_kernel,
        out_shape=shapes,
        in_specs=[hbm] * 11,
        out_specs=(hbm,) * 6,
        scratch_shapes=[
            V((12, 16, 32 * WLON), BF), V((T // LEV, LEV, C), BF), V((4 * SLOT, T), BF), V((T, 4 * SLOT), BF),
            V((T, 12 * 16), BF), V((512, 32 * WLON), BF), dma((7,)),
            *[V(shape.shape, shape.dtype) for shape in shapes], dma((6,)),
            V((2, C, 3 * C), BF), V((2, C, C), BF), V((2, C, FF), BF), V((2, FF, C), BF),
            dma((2, 4)),
            V((1024, 1024), BF), V((32, 2, 16, 128), BF), V((2, 4, 16, 1024), BF),
            V((32, 2, 16, 128), BF), V((32, 2, 16, 128), BF), dma((2, 32)), dma((2, 32)), dma((2,)),
            V((12 * 16, C), BF), V((2, 64, 1024), BF),
            V((4, 4, SLOT, C), BF), V((4, 4, SLOT, C), BF),
            dma((4, 4)), dma((4, 4)),
            V((2, T, C), F32), V((2, T, C), F32), V((2, T, C), BF), V((2, T, 128), F32),
            V((2, T, 3 * C), BF), V((2, HEADS, T, T), BF), V((2, T, C), BF),
            V((2, T, C), F32), V((2, T, C), BF), V((2, T, 128), F32),
            V((2, T, FF), F32), V((2, T, FF), BF), V((T, C), F32),
            V((2, T, 3 * C), BF), V((2, T, C), BF), V((2, T, FF), BF), V((2, T, C), BF), V((T, C), BF),
            V((2, T, C), BF), V((2, T, C), BF), V((2, T, C), BF), V((2, T, FF), BF),
            V((2, 2, T, 384), BF), V((2, 2, T, 128), BF), V((2, 2, T, 512), BF), V((2, 2, T, 128), BF),
            dma((2, 12)), dma((2, 12)),
            V((2, 6, 4, 4, 64, 256), BF), V((2, 6, 2, 2, 64, 256), BF), V((2, 6, 2, 2, 64, 256), BF),
            V((2, 6, 2, 4, 64, 256), BF), V((2, 6, 4, 4, 16, 256), BF), V((2, 6, 16, 16, 256), BF),
            dma((2, 6, 6)), dma((2, 6, 6)), dma((2, 6, 16)), dma((2, 6, 16)),
        ],
        compiler_params=pltpu.CompilerParams(
            collective_id=0, has_side_effects=True, vmem_limit_bytes=60 * 2**20
        ),
    )(encoded, upstream, *permutations(), w_qkv, w_proj, w_up, w_down)
    return pl.pallas_call(
        copies_kernel,
        out_shape=shapes,
        in_specs=[hbm] * 6,
        out_specs=(hbm,) * 6,
        scratch_shapes=[dma((6,))],
    )(*results)


def on_device(encoded, upstream, w_qkv, w_proj, w_up, w_down):
    mixed, dencoded, qkv, proj, up, down = layers(
        encoded.reshape(12, 16, 32 * WLON),
        upstream.transpose(1, 2, 0, 3).reshape(T // LEV, LEV, C),
        w_qkv, w_proj, w_up, w_down,
    )
    return (
        mixed.reshape(WLAT, WLON, LEV, C).transpose(2, 0, 1, 3),
        dencoded.reshape(encoded.shape),
        qkv.transpose(1, 2, 0),
        proj.swapaxes(1, 2),
        up.swapaxes(1, 2),
        down.swapaxes(1, 2),
    )


def solution(mesh):
    return jax.shard_map(
        on_device,
        mesh=mesh,
        in_specs=(P(None, "lat", "lon", None), P(None, "lat", "lon", None), P(), P(), P(), P()),
        out_specs=(
            P(None, "lat", "lon", None),
            P(None, "lat", "lon", None),
            P(None, None, ("lat", "lon")),
            P(None, None, ("lat", "lon")),
            P(None, None, ("lat", "lon")),
            P(None, None, ("lat", "lon")),
        ),
        check_vma=False,
    )
```

```python
import functools

import jax
import jax.numpy as jnp
import numpy as np
from jax import lax
from jax.experimental import pallas as pl
from jax.experimental.pallas import tpu as pltpu
from jax.sharding import PartitionSpec as P

HEADS = 16
WLAT = 6
WLON = 12
LEV = 2
C = 512
FF = 2048
T = LEV * WLAT * WLON
QUAD = T // 4
SLOT = 48
NORM_EPS = 1e-05
MESH = pl.DeviceIdType.MESH
BF = jnp.bfloat16
F32 = jnp.float32


def quadrant_order():
    return [
        (l, 3 * a + r, 6 * b + c)
        for a in range(2)
        for b in range(2)
        for l in range(LEV)
        for r in range(3)
        for c in range(6)
    ]


def permutations():
    slots_of_natural = np.zeros((4 * SLOT, T), np.float32)
    tokens_of_slots = np.zeros((T, 4 * SLOT), np.float32)
    tokens_of_padded = np.zeros((T, 12 * 16), np.float32)
    for t, (l, r, c) in enumerate(quadrant_order()):
        slot = t // QUAD * SLOT + t % QUAD
        slots_of_natural[slot, (r * WLON + c) * LEV + l] = 1
        tokens_of_slots[t, slot] = 1
        tokens_of_padded[t, (l * WLAT + r) * 16 + c] = 1
    spread = np.zeros((32 * 16, 32 * WLON), np.float32)
    for col in range(32 * WLON):
        spread[col // WLON * 16 + col % WLON, col] = 1
    swap = np.eye(1024, dtype=np.float32).reshape(8, 8, 16, 1024).swapaxes(0, 1).reshape(1024, 1024)
    matrices = (slots_of_natural, tokens_of_slots, tokens_of_padded, spread, swap)
    return [jnp.asarray(m, BF) for m in matrices]


def nn(a, b):
    return lax.dot_general(a, b, (((1,), (0,)), ((), ())), preferred_element_type=F32)


def nt(a, b):
    return lax.dot_general(a, b, (((1,), (1,)), ((), ())), preferred_element_type=F32)


def tn(a, b):
    return lax.dot_general(a, b, (((0,), (0,)), ((), ())), preferred_element_type=F32)


def norm(x):
    centred = x - jnp.mean(x, -1, keepdims=True)
    rstd = lax.rsqrt(jnp.mean(centred * centred, -1, keepdims=True) + NORM_EPS)
    return centred * rstd, rstd


def norm_back(dn, nhat, rstd):
    return rstd * (
        dn - jnp.mean(dn, -1, keepdims=True) - nhat * jnp.mean(dn * nhat, -1, keepdims=True)
    )


def layers_kernel(
    enc_hbm, up_hbm, son_hbm, tos_hbm, ton_hbm, spread_hbm, swap_hbm,
    wqkv_hbm, wproj_hbm, wup_hbm, wdown_hbm,
    mixed_hbm, denc_hbm, oqkv_hbm, oproj_hbm, oup_hbm, odown_hbm,
    enc_ref, up_ref, son_ref, tos_ref, ton_ref, spread_ref, in_sem,
    mixed_ref, denc_ref, oqkv_ref, oproj_ref, oup_ref, odown_ref, out_sem,
    wqkv, wproj, wup, wdown, wsem,
    swap, leave, came, leave2, came2, lane_send, lane_recv, nat2, turned, send, recv, send_sem, recv_sem,
    xs, n1h, n1, r1, us, ps, att, n2h, n2, r2, gp, hs, acc, eq, ep, eu, ed, dab,
    pn1, patt, pn2, phs, peq, pep, peu, ped, pair_send, pair_recv,
    part, fwd, fsum, side, plane_out, plane_in, ring_send, ring_recv, plane_send, plane_recv,
):
    i, j = lax.axis_index("lat"), lax.axis_index("lon")
    nlat, nlon = lax.axis_size("lat"), lax.axis_size("lon")

    def device(di, dj):
        return (lax.rem(i + di + nlat, nlat), lax.rem(j + dj + nlon, nlon))

    core, z, y = lax.rem(i, 2), lax.rem(j, 4), j // 8
    x = i // 2 * 2 + lax.rem(j // 4, 2)

    def along(axis, steps):
        at = {"x": x, "y": y, "z": z}
        at[axis] = lax.rem(at[axis] + steps + 4, 4)
        return (at["x"] // 2 * 2 + core, at["y"] * 8 + lax.rem(at["x"], 2) * 4 + at["z"])

    def beside(axis, steps, other, others):
        at = {"x": x, "y": y, "z": z}
        at[axis] = lax.rem(at[axis] + steps + 4, 4)
        at[other] = lax.rem(at[other] + others + 4, 4)
        return (at["x"] // 2 * 2 + core, at["y"] * 8 + lax.rem(at["x"], 2) * 4 + at["z"])

    partner = (i + 1 - 2 * core, j)

    weights = ((wqkv_hbm, wqkv), (wproj_hbm, wproj), (wup_hbm, wup), (wdown_hbm, wdown))
    inputs = {}
    for at, (name, src, dst) in enumerate(
        (
            ("enc", enc_hbm, enc_ref), ("spread", spread_hbm, spread_ref), ("up", up_hbm, up_ref),
            ("son", son_hbm, son_ref), ("tos", tos_hbm, tos_ref), ("ton", ton_hbm, ton_ref),
            ("swap", swap_hbm, swap),
        )
    ):
        inputs[name] = pltpu.make_async_copy(src, dst, in_sem.at[at])
        inputs[name].start()
    fetches = []
    for k in range(2):
        for w, (src, dst) in enumerate(weights):
            fetch = pltpu.make_async_copy(src.at[k], dst.at[k], wsem.at[k, w])
            fetch.start()
            fetches.append(fetch)

    barrier = pltpu.get_barrier_semaphore()
    far = lambda xl, dy, dz: (lax.rem(i + 2, 4), lax.rem(y + dy, 4) * 8 + xl * 4 + lax.rem(z + dz, 4))
    greeted = [device(1, 0), device(-1, 0), device(1, 1), device(-1, -1)]
    greeted += [far(xl, 0, dz) for xl in range(2) for dz in range(4)]
    greeted += [far(xl, dy, 0) for xl in range(2) for dy in (1, 2, 3)]
    for other in greeted:
        pl.semaphore_signal(barrier, inc=1, device_id=other, device_id_type=MESH)

    @pl.loop(1, nlon)
    def _(step):
        pl.semaphore_signal(barrier, inc=1, device_id=device(0, step), device_id_type=MESH)

    inputs["enc"].wait()
    inputs["spread"].wait()
    columns_first = nt(spread_ref[...], enc_ref[...].reshape(12 * 16, 32 * WLON)).astype(BF)
    leave[:, 0] = columns_first[:, 0:128].reshape(32, 16, 128)
    leave[:, 1, :, 0:64] = columns_first[:, 128:192].reshape(32, 16, 64)
    leave[:, 1, :, 64:128] = jnp.zeros((32, 16, 64), BF)
    pl.semaphore_wait(barrier, len(greeted) + nlon - 1)
    mine = pl.ds(pl.multiple_of(lax.rem(j, 8) * 128, 128), 128)

    def lane_copy(step, event):
        to = lax.rem(j + step, nlon)
        if event == 0:
            src, dst = leave.at[to], came.at[:, j // 8, :, mine]
        else:
            src, dst = leave2.at[to], came2.at[j]
        return pltpu.make_async_remote_copy(
            src_ref=src, dst_ref=dst, send_sem=lane_send.at[event], recv_sem=lane_recv.at[event],
            device_id=(i, to), device_id_type=MESH,
        )

    def lane_start(event):
        @pl.loop(1, nlon)
        def _(step):
            lane_copy(step, event).start()

        if event == 0:
            src, dst = leave.at[j], came.at[:, j // 8, :, mine]
        else:
            src, dst = leave2.at[j], came2.at[j]
        pltpu.make_async_copy(src, dst, lane_recv.at[event]).start()

    def lane_finish(event):
        await_bytes((came, came2)[event], lane_recv.at[event])
        await_bytes((leave, leave2)[event].at[pl.ds(0, 31)], lane_send.at[event])

    lane_start(0)

    def remote(src, dst, sems, to):
        pltpu.make_async_remote_copy(
            src_ref=src, dst_ref=dst, send_sem=sems[0], recv_sem=sems[1], device_id=to, device_id_type=MESH
        ).start()

    def await_bytes(like, sem):
        pltpu.make_async_copy(like, like, sem).wait()

    wide = {"eq": 384, "ep": 128, "eu": 512, "ed": 128}
    whole = {"n1": (n1, pn1), "att": (att, patt), "n2": (n2, pn2), "hs": (hs, phs)}
    cut = {"eq": (eq, peq), "ep": (ep, pep), "eu": (eu, peu), "ed": (ed, ped)}

    def columns(name, hi, owner):
        width = wide[name]
        return pl.ds(pl.multiple_of((2 * hi + owner) * width, width), width)

    names = ("n1", "att", "n2", "hs", "eq", "ep", "eu", "ed")

    def give(k, name):
        sems = (pair_send.at[k, names.index(name)], pair_recv.at[k, names.index(name)])
        if name in whole:
            src, dst = whole[name]
            remote(src.at[k], dst.at[k], sems, partner)
        else:
            src, dst = cut[name]
            for hi in range(2):
                remote(src.at[k, :, columns(name, hi, 1 - core)], dst.at[k, hi], sems, partner)

    def taken(k, name, sems):
        dst = (whole[name] if name in whole else cut[name])[1]
        await_bytes(dst.at[k], sems.at[k, names.index(name)])

    def take(k, name):
        taken(k, name, pair_recv)

    orders = ("xyz", "yxz", "zyx", "zyx", "xyz", "yxz")
    where = {"x": x, "y": y, "z": z}

    def chunk(k, p, t, half):
        return part.at[k, p, lax.rem(t + 4, 4), pl.ds(2 * half, 2)]

    def f32(ref):
        return ref[...].astype(F32)

    def ring_start(k, p):
        axis = orders[p][0]
        t = where[axis]
        after, before = along(axis, 1), along(axis, -1)
        out = ring_send.at[k, p]
        remote(chunk(k, p, t + 2, 0), fwd.at[k, p, 0], (out, ring_recv.at[k, p, 0]), after)
        remote(chunk(k, p, t + 2, 1), fwd.at[k, p, 1], (out, ring_recv.at[k, p, 1]), before)
        remote(chunk(k, p, t + 1, 1), side.at[k, p, 0, pl.ds(2, 2)], (out, ring_recv.at[k, p, 2]), after)
        remote(chunk(k, p, t - 1, 0), side.at[k, p, 1, pl.ds(0, 2)], (out, ring_recv.at[k, p, 2]), before)

    def ring_mid(k, p):
        axis = orders[p][0]
        t = where[axis]
        after, before = along(axis, 1), along(axis, -1)
        sems = (ring_send.at[k, p], ring_recv.at[k, p, 2])
        await_bytes(fwd.at[k, p, 0], ring_recv.at[k, p, 0])
        fsum[k, p, 0] = (f32(fwd.at[k, p, 0]) + f32(chunk(k, p, t + 1, 0))).astype(BF)
        remote(fsum.at[k, p, 0], side.at[k, p, 0, pl.ds(0, 2)], sems, after)
        await_bytes(fwd.at[k, p, 1], ring_recv.at[k, p, 1])
        fsum[k, p, 1] = (f32(fwd.at[k, p, 1]) + f32(chunk(k, p, t - 1, 1))).astype(BF)
        remote(fsum.at[k, p, 1], side.at[k, p, 1, pl.ds(2, 2)], sems, before)

    def plane_copy(k, p, step):
        _, second, third = orders[p]
        d2, d3 = step // 4, lax.rem(step, 4)
        src = plane_out.at[k, p, lax.rem(where[second] + d2, 4), lax.rem(where[third] + d3, 4)]
        return pltpu.make_async_remote_copy(
            src_ref=src, dst_ref=plane_in.at[k, p, step], send_sem=plane_send.at[k, p],
            recv_sem=plane_recv.at[k, p], device_id=beside(second, d2, third, d3), device_id_type=MESH,
        )

    def ring_end(k, p):
        await_bytes(side.at[k, p], ring_recv.at[k, p, 2])
        t = where[orders[p][0]]
        total = f32(part.at[k, p, t]) + f32(side.at[k, p, 0]) + f32(side.at[k, p, 1])
        for s2 in range(4):
            for s3 in range(4):
                if p // 2 == 0:
                    rows = (total[s2, 12 * s3 : 12 * s3 + 12], total[s2, 48 + 4 * s3 : 52 + 4 * s3])
                    rows = jnp.concatenate(rows, 0)
                elif p // 2 == 1:
                    rows = total[s2, 16 * s3 : 16 * s3 + 16]
                else:
                    rows = [total[s2, 16 * hb + 4 * s3 : 16 * hb + 4 * s3 + 4] for hb in range(4)]
                    rows = jnp.concatenate(rows, 0)
                plane_out[k, p, s2, s3] = rows.astype(BF)

        @pl.loop(1, 16)
        def _(step):
            plane_copy(k, p, step).start()

    def ring_last(k, p):
        await_bytes(plane_in.at[k, p, pl.ds(1, 15)], plane_recv.at[k, p])
        _, second, third = orders[p]
        total = f32(plane_out.at[k, p, where[second], where[third]])
        for step in range(1, 16):
            total += f32(plane_in.at[k, p, step])
        lanes = slice(256 * (p % 2), 256 * (p % 2) + 256)
        if p // 2 == 0:
            oqkv_ref[:, k, lanes] = total[0:12]
            oproj_ref[k, :, lanes] = total[12:16]
        elif p // 2 == 1:
            oup_ref[k, :, lanes] = total
        else:
            for hb in range(4):
                at = slice(hb * C + lanes.start, hb * C + lanes.stop)
                odown_ref[k, :, at] = total[4 * hb : 4 * hb + 4]

    def both(k, name, hi, own, theirs):
        src, dst = cut[name]
        return tn(src[k, :, columns(name, hi, core)], own) + tn(dst[k, hi], theirs)

    def keep(k, p, first, second, rows, g):
        for s in range(2):
            at = (first, second) if orders[p + s][0] == orders[p][0] else (second, first)
            part[k, p + s, at[0], at[1], rows, :] = g[:, 256 * s : 256 * s + 256]

    def grads_a(k):
        for name in ("n1", "att", "ep", "eq"):
            take(k, name)
        for hi in range(2):
            g = both(k, "eq", hi, n1[k], pn1[k]).astype(BF)
            for at in range(8):
                keep(k, 0, 2 * hi + at % 2, at // 2, slice(0, 48), g[48 * at : 48 * at + 48])
            g = both(k, "ep", hi, att[k], patt[k]).astype(BF)
            for at in range(8):
                keep(k, 0, 2 * hi + at % 2, at // 2, slice(48, 64), g[16 * at : 16 * at + 16])
        ring_start(k, 0)
        ring_start(k, 1)

    def grads_b(k):
        for name in ("n2", "eu"):
            take(k, name)
        for hi in range(2):
            g = both(k, "eu", hi, n2[k], pn2[k]).astype(BF)
            for at in range(32):
                row = (2 * hi + at // 4 % 2) * 16
                keep(k, 2, at % 4, at // 8, slice(row, row + 16), g[16 * at : 16 * at + 16])
        ring_start(k, 2)
        ring_start(k, 3)

    def grads_c(k):
        for name in ("hs", "ed"):
            take(k, name)
        for hi in range(2):
            for hb in range(4):
                cols = slice(hb * C, hb * C + C)
                g = both(k, "ed", hi, hs[k, :, cols], phs[k, :, cols]).astype(BF)
                for at in range(8):
                    row = 16 * hb
                    keep(k, 4, 2 * hi + at % 2, at // 2, slice(row, row + 16), g[16 * at : 16 * at + 16])
        ring_start(k, 4)
        ring_start(k, 5)

    def exchange(event, forward):
        for q in range(4):
            a, b = q // 2, q % 2
            di, dj = (a - 1, b - 1) if forward else (a, b)
            if (di, dj) == (0, 0):
                recv[event, 3 - q] = send[event, q]
            else:
                sems = (send_sem.at[event], recv_sem.at[event])
                remote(send.at[event, q], recv.at[event, 3 - q], sems, device(di, dj))

    def arrive(event):
        await_bytes(recv.at[event, pl.ds(0, 3)], recv_sem.at[event])

    def put(event, tokens):
        send[event] = tn(tos_ref[...], tokens).astype(BF).reshape(4, SLOT, C)

    def got(event):
        return nn(tos_ref[...], recv[event].reshape(4 * SLOT, C))

    for name in ("up", "son", "tos", "ton"):
        inputs[name].wait()
    send[0] = nn(son_ref[...], up_ref[...].reshape(T, C)).astype(BF).reshape(4, SLOT, C)
    exchange(0, True)

    lane = lax.broadcasted_iota(jnp.int32, (1, 128), 1)
    head_mask = [((lane >= 32 * s) & (lane < 32 * s + 32)).astype(BF) for s in range(4)]
    half_t = lax.broadcasted_iota(jnp.int32, (T, T), 0) < T // 2
    half_s = lax.broadcasted_iota(jnp.int32, (T, T), 1) < T // 2
    apart = jnp.where(half_t == half_s, 0.0, 1.0).astype(F32)
    last = jnp.where(i == nlat - 1, 1.0, 0.0).astype(F32)
    extra = [((lane == (32 * s + 64) % 128) | (lane == (32 * s + 64) % 128 + 1)) for s in range(4)]
    inside = [(lane >= 32 * s) & (lane < 32 * s + 32) for s in range(4)]
    first_extra = lax.rem(lane, 32) == 0
    gather_rows = lax.broadcasted_iota(jnp.int32, (128, 128), 0) // 32
    gather_cols = lax.broadcasted_iota(jnp.int32, (128, 128), 1)
    gather = jnp.where(
        (lax.rem(gather_cols, 32) < 2) & (lax.rem(gather_cols // 32 + 2, 4) == gather_rows), 1.0, 0.0
    ).astype(BF)

    def forward(k, x):
        xs[k] = x
        nhat, rstd = norm(x)
        n1h[k] = nhat
        r1[k] = jnp.broadcast_to(rstd, (T, 128))
        n1[k] = nhat.astype(BF)
        give(k, "n1")
        fetches[4 * k].wait()

        @pl.loop(0, 3)
        def _(s):
            cols = pl.ds(pl.multiple_of(s * C, C), C)
            us[k, :, cols] = nn(n1[k], wqkv[k, :, cols]).astype(BF)

        @pl.loop(0, 4)
        def _(g):
            def part(w):
                return us[k, :, pl.ds(pl.multiple_of(w * C + g * 128, 128), 128)]

            q, key, v = part(0), part(1), part(2)
            total = jnp.zeros((T, 128), F32)
            for s in range(4):
                e = jnp.exp(nt(q * head_mask[s], key) * (32**-0.5))
                if k == 1:
                    e = e * (1.0 - last * apart)
                p = ((e * (1.0 / (0.25 * jnp.sum(e, -1, keepdims=True)))) * 0.25).astype(BF)
                ps[k, g * 4 + s] = p
                total += nn(p, v * head_mask[s])
            att[k, :, pl.ds(pl.multiple_of(g * 128, 128), 128)] = total.astype(BF)

        give(k, "att")
        fetches[4 * k + 1].wait()
        m = xs[k] + nn(att[k], wproj[k])
        acc[...] = m
        nhat, rstd = norm(m)
        n2h[k] = nhat
        r2[k] = jnp.broadcast_to(rstd, (T, 128))
        n2[k] = nhat.astype(BF)
        give(k, "n2")
        fetches[4 * k + 2].wait()
        fetches[4 * k + 3].wait()

        @pl.loop(0, 4)
        def _(s):
            cols = pl.ds(pl.multiple_of(s * C, C), C)
            z = nn(n2[k], wup[k, :, cols])
            cdf = 0.5 * (1.0 + lax.erf(z * (2.0**-0.5)))
            gp[k, :, cols] = cdf + z * (jnp.exp(-0.5 * z * z) * ((2.0 * np.pi) ** -0.5))
            h = (z * cdf).astype(BF)
            hs[k, :, cols] = h
            acc[...] += nn(h, wdown[k, cols, :])

        give(k, "hs")
        return acc[...]

    def backward(k, ct, after_up, after_proj, amid):
        acc[...] = ct
        ed[k] = ct.astype(BF)
        give(k, "ed")

        @pl.loop(0, 4)
        def _(s):
            cols = pl.ds(pl.multiple_of(s * C, C), C)
            dh = nt(ed[k], wdown[k, cols, :]).astype(BF).astype(F32)
            eu[k, :, cols] = (dh * gp[k, :, cols]).astype(BF)

        give(k, "eu")
        after_up()
        dn2 = nt(eu[k], wup[k]).astype(BF).astype(F32)
        dm = acc[...] + norm_back(dn2, n2h[k], r2[k][:, 0:1])
        acc[...] = dm
        ep[k] = dm.astype(BF)
        give(k, "ep")
        grads_c(k)
        dab[...] = nt(ep[k], wproj[k]).astype(BF)
        grads_b(k)
        after_proj()

        def heads(g):
            def at(w):
                return pl.ds(pl.multiple_of(w * C + g * 128, 128), 128)

            q, key, v = us[k, :, at(0)], us[k, :, at(1)], us[k, :, at(2)]
            da = dab[:, at(0)]
            dq = jnp.zeros((T, 128), F32)
            dk = jnp.zeros((T, 128), F32)
            dv = jnp.zeros((T, 128), F32)
            prod = da.astype(F32) * att[k, :, at(0)].astype(F32)
            high = prod.astype(BF)
            low = (prod - high.astype(F32)).astype(BF)
            sums = nn(high, gather) + nn(low, gather)
            sums_high = sums.astype(BF).astype(F32)
            sums = jnp.where(first_extra, sums_high, sums - sums_high).astype(BF)
            for s in range(4):
                p = ps[k, g * 4 + s]
                dah = da * head_mask[s]
                with_sums = jnp.where(inside[s], da, jnp.where(extra[s], sums, jnp.zeros_like(sums)))
                dp = nt(with_sums, jnp.where(extra[s], -jnp.ones_like(v), v))
                dv += tn(p, dah)
                ds = (p.astype(F32) * dp).astype(BF)
                dq += nn(ds, key * head_mask[s])
                dk += tn(ds, q * head_mask[s])
            eq[k, :, at(0)] = (dq * (32**-0.5)).astype(BF)
            eq[k, :, at(1)] = (dk * (32**-0.5)).astype(BF)
            eq[k, :, at(2)] = dv.astype(BF)

        for half in range(2):
            pl.loop(2 * half, 2 * half + 2)(heads)
            amid(half)
        give(k, "eq")

    def backward_end(k):
        dn1 = nt(eq[k], wqkv[k]).astype(BF).astype(F32)
        return acc[...] + norm_back(dn1, n1h[k], r1[k][:, 0:1])

    def nothing():
        pass

    inputs["swap"].wait()
    lane_finish(0)
    for half in range(2):
        moved = nn(came[half].reshape(64, 1024), swap[...]).astype(BF)
        for lr in range(8 if half == 0 else 4):
            for g in range(4):
                at = (slice(128 * half + 16 * lr, 128 * half + 16 * lr + 16), slice(128 * g, 128 * g + 128))
                nat2[at] = moved[16 * g : 16 * g + 16, 128 * lr : 128 * lr + 128]
    first = forward(0, nn(ton_ref[...], nat2[...]))
    put(1, first.astype(BF))
    exchange(1, True)
    arrive(1)
    second = forward(1, got(1))
    put(2, second.astype(BF))
    exchange(2, False)
    arrive(0)

    def mids(k, parts):
        for p in parts:
            ring_mid(k, p)

    def ends(k, parts):
        for p in parts:
            ring_end(k, p)

    def lasts(k, parts):
        for p in parts:
            ring_last(k, p)

    def amid_one(half):
        if half == 1:
            mids(1, (4, 5))

    backward(1, got(0), nothing, nothing, amid_one)
    d_second = backward_end(1)
    put(3, d_second.astype(BF))
    exchange(3, False)
    grads_a(1)
    mids(1, (2, 3))
    arrive(3)

    def up_zero():
        ends(1, (4, 5))
        mids(1, (0, 1))

    def proj_zero():
        ends(1, (2, 3))

    def amid_zero(half):
        if half == 0:
            ends(1, (0, 1))
        else:
            mids(0, (4, 5, 2, 3))

    backward(0, got(3), up_zero, proj_zero, amid_zero)
    grads_a(0)
    ends(0, (4, 5))
    d_first = backward_end(0)
    nat2[...] = tn(ton_ref[...], d_first.astype(BF)).astype(BF)
    for half in range(2):
        for lr in range(8):
            for g in range(4):
                at = (slice(16 * g, 16 * g + 16), slice(128 * lr, 128 * lr + 128))
                if half == 1 and lr >= 4:
                    turned[half, at[0], at[1]] = jnp.zeros((16, 128), BF)
                else:
                    row = 128 * half + 16 * lr
                    turned[half, at[0], at[1]] = nat2[row : row + 16, 128 * g : 128 * g + 128]
        moved = nn(turned[half], swap[...]).astype(BF)
        for g in range(4):
            for lane_block in range(8):
                leave2[8 * g + lane_block, half] = moved[
                    16 * g : 16 * g + 16, 128 * lane_block : 128 * lane_block + 128
                ]
    lane_start(1)
    mids(0, (0, 1))
    ends(0, (2, 3))
    arrive(2)
    natural = tn(son_ref[...], recv[2].reshape(4 * SLOT, C)).astype(BF)
    mixed_ref[...] = natural.reshape(T // LEV, LEV, C)
    stores = []

    def store(src, dst):
        stores.append(pltpu.make_async_copy(src, dst, out_sem.at[len(stores)]))
        stores[-1].start()

    store(mixed_ref, mixed_hbm)
    lasts(1, range(6))
    ends(0, (0, 1))
    lasts(0, (4, 5, 2, 3))
    store(oup_ref, oup_hbm)
    store(odown_ref, odown_hbm)
    lane_finish(1)
    for half in range(2):
        rows = tn(came2[:, half].reshape(512, 128), spread_ref[...]).astype(BF)
        n = 8 if half == 0 else 4
        denc_ref[8 * half : 8 * half + n] = rows[0 : 16 * n].reshape(n, 16, 32 * WLON)
    store(denc_ref, denc_hbm)
    lasts(0, (0, 1))
    store(oqkv_ref, oqkv_hbm)
    store(oproj_ref, oproj_hbm)
    for event in range(4):
        await_bytes(send.at[event, pl.ds(0, 3)], send_sem.at[event])
    for k in range(2):
        for name in names:
            taken(k, name, pair_send)
        for p in range(6):
            await_bytes(part.at[k, p, pl.ds(0, 3)], ring_send.at[k, p])
            await_bytes(plane_in.at[k, p, pl.ds(1, 15)], plane_send.at[k, p])
    for copy in stores:
        copy.wait()


def copies_kernel(*refs):
    for n in range(6):
        refs[6 + n][...] = refs[n][...]


def layers(encoded, upstream, w_qkv, w_proj, w_up, w_down):
    hbm = pl.BlockSpec(memory_space=pl.ANY)
    vmem = pl.BlockSpec(memory_space=pltpu.VMEM)
    dma = pltpu.SemaphoreType.DMA
    V = pltpu.VMEM
    shapes = (
        jax.ShapeDtypeStruct((T // LEV, LEV, C), BF),
        jax.ShapeDtypeStruct((12, 16, 32 * WLON), BF),
        jax.ShapeDtypeStruct((12, 2, C), F32),
        jax.ShapeDtypeStruct((2, 4, C), F32),
        jax.ShapeDtypeStruct((2, 16, C), F32),
        jax.ShapeDtypeStruct((2, 4, FF), F32),
    )
    results = pl.pallas_call(
        layers_kernel,
        out_shape=shapes,
        in_specs=[hbm] * 11,
        out_specs=(hbm,) * 6,
        scratch_shapes=[
            V((12, 16, 32 * WLON), BF), V((T // LEV, LEV, C), BF), V((4 * SLOT, T), BF), V((T, 4 * SLOT), BF),
            V((T, 12 * 16), BF), V((512, 32 * WLON), BF), dma((7,)),
            *[V(shape.shape, shape.dtype) for shape in shapes], dma((6,)),
            V((2, C, 3 * C), BF), V((2, C, C), BF), V((2, C, FF), BF), V((2, FF, C), BF),
            dma((2, 4)),
            V((1024, 1024), BF), V((32, 2, 16, 128), BF), V((2, 4, 16, 1024), BF),
            V((32, 2, 16, 128), BF), V((32, 2, 16, 128), BF), dma((2,)), dma((2,)),
            V((12 * 16, C), BF), V((2, 64, 1024), BF),
            V((4, 4, SLOT, C), BF), V((4, 4, SLOT, C), BF),
            dma((4,)), dma((4,)),
            V((2, T, C), F32), V((2, T, C), F32), V((2, T, C), BF), V((2, T, 128), F32),
            V((2, T, 3 * C), BF), V((2, HEADS, T, T), BF), V((2, T, C), BF),
            V((2, T, C), F32), V((2, T, C), BF), V((2, T, 128), F32),
            V((2, T, FF), F32), V((2, T, FF), BF), V((T, C), F32),
            V((2, T, 3 * C), BF), V((2, T, C), BF), V((2, T, FF), BF), V((2, T, C), BF), V((T, C), BF),
            V((2, T, C), BF), V((2, T, C), BF), V((2, T, C), BF), V((2, T, FF), BF),
            V((2, 2, T, 384), BF), V((2, 2, T, 128), BF), V((2, 2, T, 512), BF), V((2, 2, T, 128), BF),
            dma((2, 8)), dma((2, 8)),
            V((2, 6, 4, 4, 64, 256), BF), V((2, 6, 2, 2, 64, 256), BF), V((2, 6, 2, 2, 64, 256), BF),
            V((2, 6, 2, 4, 64, 256), BF), V((2, 6, 4, 4, 16, 256), BF), V((2, 6, 16, 16, 256), BF),
            dma((2, 6)), dma((2, 6, 3)), dma((2, 6)), dma((2, 6)),
        ],
        compiler_params=pltpu.CompilerParams(
            collective_id=0, has_side_effects=True, vmem_limit_bytes=60 * 2**20
        ),
    )(encoded, upstream, *permutations(), w_qkv, w_proj, w_up, w_down)
    return pl.pallas_call(
        copies_kernel,
        out_shape=shapes,
        in_specs=[vmem] * 6,
        out_specs=(vmem,) * 6,
    )(*results)


def on_device(encoded, upstream, w_qkv, w_proj, w_up, w_down):
    mixed, dencoded, qkv, proj, up, down = layers(
        encoded.reshape(12, 16, 32 * WLON),
        upstream.transpose(1, 2, 0, 3).reshape(T // LEV, LEV, C),
        w_qkv, w_proj, w_up, w_down,
    )
    return (
        mixed.reshape(WLAT, WLON, LEV, C).transpose(2, 0, 1, 3),
        dencoded.reshape(encoded.shape),
        qkv.transpose(1, 2, 0),
        proj.swapaxes(1, 2),
        up.swapaxes(1, 2),
        down.swapaxes(1, 2),
    )


def solution(mesh):
    return jax.shard_map(
        on_device,
        mesh=mesh,
        in_specs=(P(None, "lat", "lon", None), P(None, "lat", "lon", None), P(), P(), P(), P()),
        out_specs=(
            P(None, "lat", "lon", None),
            P(None, "lat", "lon", None),
            P(None, None, ("lat", "lon")),
            P(None, None, ("lat", "lon")),
            P(None, None, ("lat", "lon")),
            P(None, None, ("lat", "lon")),
        ),
        check_vma=False,
    )
```

```python
import functools

import jax
import jax.numpy as jnp
import numpy as np
from jax import lax
from jax.experimental import pallas as pl
from jax.experimental.pallas import tpu as pltpu
from jax.sharding import PartitionSpec as P

HEADS = 16
WLAT = 6
WLON = 12
LEV = 2
C = 512
FF = 2048
T = LEV * WLAT * WLON
QUAD = T // 4
SLOT = 48
NORM_EPS = 1e-05
MESH = pl.DeviceIdType.MESH
BF = jnp.bfloat16
F32 = jnp.float32


def quadrant_order():
    return [
        (l, 3 * a + r, 6 * b + c)
        for a in range(2)
        for b in range(2)
        for l in range(LEV)
        for r in range(3)
        for c in range(6)
    ]


def permutations():
    slots_of_natural = np.zeros((4 * SLOT, T), np.float32)
    tokens_of_slots = np.zeros((T, 4 * SLOT), np.float32)
    tokens_of_padded = np.zeros((T, 12 * 16), np.float32)
    for t, (l, r, c) in enumerate(quadrant_order()):
        slot = t // QUAD * SLOT + t % QUAD
        slots_of_natural[slot, (r * WLON + c) * LEV + l] = 1
        tokens_of_slots[t, slot] = 1
        tokens_of_padded[t, (l * WLAT + r) * 16 + c] = 1
    spread = np.zeros((32 * 16, 32 * WLON), np.float32)
    for col in range(32 * WLON):
        spread[col // WLON * 16 + col % WLON, col] = 1
    swap = np.eye(1024, dtype=np.float32).reshape(8, 8, 16, 1024).swapaxes(0, 1).reshape(1024, 1024)
    matrices = (slots_of_natural, tokens_of_slots, tokens_of_padded, spread, swap)
    return [jnp.asarray(m, BF) for m in matrices]


def nn(a, b):
    return lax.dot_general(a, b, (((1,), (0,)), ((), ())), preferred_element_type=F32)


def nt(a, b):
    return lax.dot_general(a, b, (((1,), (1,)), ((), ())), preferred_element_type=F32)


def tn(a, b):
    return lax.dot_general(a, b, (((0,), (0,)), ((), ())), preferred_element_type=F32)


def norm(x):
    centred = x - jnp.mean(x, -1, keepdims=True)
    rstd = lax.rsqrt(jnp.mean(centred * centred, -1, keepdims=True) + NORM_EPS)
    return centred * rstd, rstd


def norm_back(dn, nhat, rstd):
    return rstd * (
        dn - jnp.mean(dn, -1, keepdims=True) - nhat * jnp.mean(dn * nhat, -1, keepdims=True)
    )


def layers_kernel(
    enc_hbm, up_hbm, son_hbm, tos_hbm, ton_hbm, spread_hbm, swap_hbm,
    wqkv_hbm, wproj_hbm, wup_hbm, wdown_hbm,
    mixed_hbm, denc_hbm, oqkv_hbm, oproj_hbm, oup_hbm, odown_hbm,
    enc_ref, up_ref, son_ref, tos_ref, ton_ref, spread_ref, in_sem,
    mixed_ref, denc_ref, oqkv_ref, oproj_ref, oup_ref, odown_ref, out_sem,
    wqkv, wproj, wup, wdown, wsem,
    swap, leave, came, leave2, came2, lane_send, lane_recv, nat2, turned, send, recv, send_sem, recv_sem,
    xs, n1h, n1, r1, us, ps, att, seen, n2h, n2, r2, gp, hs, acc, eq, ep, eu, ed, dab,
    pn1, patt, pn2, phs, peq, pep, peu, ped, pair_send, pair_recv,
    part, fwd, fsum, side, plane_out, plane_in, ring_send, ring_recv, plane_send, plane_recv,
):
    i, j = lax.axis_index("lat"), lax.axis_index("lon")
    nlat, nlon = lax.axis_size("lat"), lax.axis_size("lon")

    def device(di, dj):
        return (lax.rem(i + di + nlat, nlat), lax.rem(j + dj + nlon, nlon))

    core, z, y = lax.rem(i, 2), lax.rem(j, 4), j // 8
    x = i // 2 * 2 + lax.rem(j // 4, 2)

    def along(axis, steps):
        at = {"x": x, "y": y, "z": z}
        at[axis] = lax.rem(at[axis] + steps + 4, 4)
        return (at["x"] // 2 * 2 + core, at["y"] * 8 + lax.rem(at["x"], 2) * 4 + at["z"])

    def beside(axis, steps, other, others):
        at = {"x": x, "y": y, "z": z}
        at[axis] = lax.rem(at[axis] + steps + 4, 4)
        at[other] = lax.rem(at[other] + others + 4, 4)
        return (at["x"] // 2 * 2 + core, at["y"] * 8 + lax.rem(at["x"], 2) * 4 + at["z"])

    partner = (i + 1 - 2 * core, j)

    weights = ((wqkv_hbm, wqkv), (wproj_hbm, wproj), (wup_hbm, wup), (wdown_hbm, wdown))
    inputs = {}
    for at, (name, src, dst) in enumerate(
        (
            ("enc", enc_hbm, enc_ref), ("spread", spread_hbm, spread_ref), ("up", up_hbm, up_ref),
            ("son", son_hbm, son_ref), ("tos", tos_hbm, tos_ref), ("ton", ton_hbm, ton_ref),
            ("swap", swap_hbm, swap),
        )
    ):
        inputs[name] = pltpu.make_async_copy(src, dst, in_sem.at[at])
        inputs[name].start()
    fetches = []
    for k in range(2):
        for w, (src, dst) in enumerate(weights):
            fetch = pltpu.make_async_copy(src.at[k], dst.at[k], wsem.at[k, w])
            fetch.start()
            fetches.append(fetch)

    barrier = pltpu.get_barrier_semaphore()
    far = lambda xl, dy, dz: (lax.rem(i + 2, 4), lax.rem(y + dy, 4) * 8 + xl * 4 + lax.rem(z + dz, 4))
    greeted = [device(1, 0), device(-1, 0), device(1, 1), device(-1, -1)]
    greeted += [far(xl, 0, dz) for xl in range(2) for dz in range(4)]
    greeted += [far(xl, dy, 0) for xl in range(2) for dy in (1, 2, 3)]
    for other in greeted:
        pl.semaphore_signal(barrier, inc=1, device_id=other, device_id_type=MESH)

    @pl.loop(1, nlon)
    def _(step):
        pl.semaphore_signal(barrier, inc=1, device_id=device(0, step), device_id_type=MESH)

    inputs["enc"].wait()
    inputs["spread"].wait()
    columns_first = nt(spread_ref[...], enc_ref[...].reshape(12 * 16, 32 * WLON)).astype(BF)
    leave[:, 0] = columns_first[:, 0:128].reshape(32, 16, 128)
    leave[:, 1, :, 0:64] = columns_first[:, 128:192].reshape(32, 16, 64)
    leave[:, 1, :, 64:128] = jnp.zeros((32, 16, 64), BF)
    pl.semaphore_wait(barrier, len(greeted) + nlon - 1)
    mine = pl.ds(pl.multiple_of(lax.rem(j, 8) * 128, 128), 128)

    def lane_copy(step, event):
        to = lax.rem(j + step, nlon)
        if event == 0:
            src, dst = leave.at[to], came.at[:, j // 8, :, mine]
        else:
            src, dst = leave2.at[to], came2.at[j]
        return pltpu.make_async_remote_copy(
            src_ref=src, dst_ref=dst, send_sem=lane_send.at[event], recv_sem=lane_recv.at[event],
            device_id=(i, to), device_id_type=MESH,
        )

    def lane_start(event):
        @pl.loop(1, nlon)
        def _(step):
            lane_copy(step, event).start()

        if event == 0:
            src, dst = leave.at[j], came.at[:, j // 8, :, mine]
        else:
            src, dst = leave2.at[j], came2.at[j]
        pltpu.make_async_copy(src, dst, lane_recv.at[event]).start()

    def lane_finish(event):
        await_bytes((came, came2)[event], lane_recv.at[event])
        await_bytes((leave, leave2)[event].at[pl.ds(0, 31)], lane_send.at[event])

    lane_start(0)

    def remote(src, dst, sems, to):
        pltpu.make_async_remote_copy(
            src_ref=src, dst_ref=dst, send_sem=sems[0], recv_sem=sems[1], device_id=to, device_id_type=MESH
        ).start()

    def await_bytes(like, sem):
        pltpu.make_async_copy(like, like, sem).wait()

    wide = {"eq": 384, "ep": 128, "eu": 512, "ed": 128}
    whole = {"n1": (n1, pn1), "att": (att, patt), "n2": (n2, pn2), "hs": (hs, phs)}
    cut = {"eq": (eq, peq), "ep": (ep, pep), "eu": (eu, peu), "ed": (ed, ped)}

    def columns(name, hi, owner):
        width = wide[name]
        return pl.ds(pl.multiple_of((2 * hi + owner) * width, width), width)

    names = ("n1", "att", "n2", "hs", "eq", "ep", "eu", "ed")

    def give(k, name):
        sems = (pair_send.at[k, names.index(name)], pair_recv.at[k, names.index(name)])
        if name in whole:
            src, dst = whole[name]
            remote(src.at[k], dst.at[k], sems, partner)
        else:
            src, dst = cut[name]
            for hi in range(2):
                remote(src.at[k, :, columns(name, hi, 1 - core)], dst.at[k, hi], sems, partner)

    def taken(k, name, sems):
        dst = (whole[name] if name in whole else cut[name])[1]
        await_bytes(dst.at[k], sems.at[k, names.index(name)])

    def take(k, name):
        taken(k, name, pair_recv)

    orders = ("xyz", "yxz", "zyx", "zyx", "xyz", "yxz")
    where = {"x": x, "y": y, "z": z}

    def chunk(k, p, t, half):
        return part.at[k, p, lax.rem(t + 4, 4), pl.ds(2 * half, 2)]

    def f32(ref):
        return ref[...].astype(F32)

    def ring_start(k, p):
        axis = orders[p][0]
        t = where[axis]
        after, before = along(axis, 1), along(axis, -1)
        out = ring_send.at[k, p]
        remote(chunk(k, p, t + 2, 0), fwd.at[k, p, 0], (out, ring_recv.at[k, p, 0]), after)
        remote(chunk(k, p, t + 2, 1), fwd.at[k, p, 1], (out, ring_recv.at[k, p, 1]), before)
        remote(chunk(k, p, t + 1, 1), side.at[k, p, 0, pl.ds(2, 2)], (out, ring_recv.at[k, p, 2]), after)
        remote(chunk(k, p, t - 1, 0), side.at[k, p, 1, pl.ds(0, 2)], (out, ring_recv.at[k, p, 2]), before)

    def ring_mid(k, p):
        axis = orders[p][0]
        t = where[axis]
        after, before = along(axis, 1), along(axis, -1)
        sems = (ring_send.at[k, p], ring_recv.at[k, p, 2])
        await_bytes(fwd.at[k, p, 0], ring_recv.at[k, p, 0])
        fsum[k, p, 0] = (f32(fwd.at[k, p, 0]) + f32(chunk(k, p, t + 1, 0))).astype(BF)
        remote(fsum.at[k, p, 0], side.at[k, p, 0, pl.ds(0, 2)], sems, after)
        await_bytes(fwd.at[k, p, 1], ring_recv.at[k, p, 1])
        fsum[k, p, 1] = (f32(fwd.at[k, p, 1]) + f32(chunk(k, p, t - 1, 1))).astype(BF)
        remote(fsum.at[k, p, 1], side.at[k, p, 1, pl.ds(2, 2)], sems, before)

    def plane_copy(k, p, step):
        _, second, third = orders[p]
        d2, d3 = step // 4, lax.rem(step, 4)
        src = plane_out.at[k, p, lax.rem(where[second] + d2, 4), lax.rem(where[third] + d3, 4)]
        return pltpu.make_async_remote_copy(
            src_ref=src, dst_ref=plane_in.at[k, p, step], send_sem=plane_send.at[k, p],
            recv_sem=plane_recv.at[k, p], device_id=beside(second, d2, third, d3), device_id_type=MESH,
        )

    def ring_end(k, p):
        await_bytes(side.at[k, p], ring_recv.at[k, p, 2])
        t = where[orders[p][0]]
        total = f32(part.at[k, p, t]) + f32(side.at[k, p, 0]) + f32(side.at[k, p, 1])
        for s2 in range(4):
            for s3 in range(4):
                if p // 2 == 0:
                    rows = (total[s2, 12 * s3 : 12 * s3 + 12], total[s2, 48 + 4 * s3 : 52 + 4 * s3])
                    rows = jnp.concatenate(rows, 0)
                elif p // 2 == 1:
                    rows = total[s2, 16 * s3 : 16 * s3 + 16]
                else:
                    rows = [total[s2, 16 * hb + 4 * s3 : 16 * hb + 4 * s3 + 4] for hb in range(4)]
                    rows = jnp.concatenate(rows, 0)
                plane_out[k, p, s2, s3] = rows.astype(BF)

        @pl.loop(1, 16)
        def _(step):
            plane_copy(k, p, step).start()

    def ring_last(k, p):
        await_bytes(plane_in.at[k, p, pl.ds(1, 15)], plane_recv.at[k, p])
        _, second, third = orders[p]
        total = f32(plane_out.at[k, p, where[second], where[third]])
        for step in range(1, 16):
            total += f32(plane_in.at[k, p, step])
        lanes = slice(256 * (p % 2), 256 * (p % 2) + 256)
        if p // 2 == 0:
            oqkv_ref[:, k, lanes] = total[0:12]
            oproj_ref[k, :, lanes] = total[12:16]
        elif p // 2 == 1:
            oup_ref[k, :, lanes] = total
        else:
            for hb in range(4):
                at = slice(hb * C + lanes.start, hb * C + lanes.stop)
                odown_ref[k, :, at] = total[4 * hb : 4 * hb + 4]

    def both(k, name, hi, own, theirs):
        src, dst = cut[name]
        return tn(src[k, :, columns(name, hi, core)], own) + tn(dst[k, hi], theirs)

    def keep(k, p, first, second, rows, g):
        for s in range(2):
            at = (first, second) if orders[p + s][0] == orders[p][0] else (second, first)
            part[k, p + s, at[0], at[1], rows, :] = g[:, 256 * s : 256 * s + 256]

    def grads_a(k):
        for name in ("n1", "att", "ep", "eq"):
            take(k, name)
        for hi in range(2):
            g = both(k, "eq", hi, n1[k], pn1[k]).astype(BF)
            for at in range(8):
                keep(k, 0, 2 * hi + at % 2, at // 2, slice(0, 48), g[48 * at : 48 * at + 48])
            g = both(k, "ep", hi, att[k], patt[k]).astype(BF)
            for at in range(8):
                keep(k, 0, 2 * hi + at % 2, at // 2, slice(48, 64), g[16 * at : 16 * at + 16])
        ring_start(k, 0)
        ring_start(k, 1)

    def grads_b(k):
        for name in ("n2", "eu"):
            take(k, name)
        for hi in range(2):
            g = both(k, "eu", hi, n2[k], pn2[k]).astype(BF)
            for at in range(32):
                row = (2 * hi + at // 4 % 2) * 16
                keep(k, 2, at % 4, at // 8, slice(row, row + 16), g[16 * at : 16 * at + 16])
        ring_start(k, 2)
        ring_start(k, 3)

    def grads_c(k):
        for name in ("hs", "ed"):
            take(k, name)
        for hi in range(2):
            for hb in range(4):
                cols = slice(hb * C, hb * C + C)
                g = both(k, "ed", hi, hs[k, :, cols], phs[k, :, cols]).astype(BF)
                for at in range(8):
                    row = 16 * hb
                    keep(k, 4, 2 * hi + at % 2, at // 2, slice(row, row + 16), g[16 * at : 16 * at + 16])
        ring_start(k, 4)
        ring_start(k, 5)

    def exchange(event, forward):
        for q in range(4):
            a, b = q // 2, q % 2
            di, dj = (a - 1, b - 1) if forward else (a, b)
            if (di, dj) == (0, 0):
                recv[event, 3 - q] = send[event, q]
            else:
                sems = (send_sem.at[event], recv_sem.at[event])
                remote(send.at[event, q], recv.at[event, 3 - q], sems, device(di, dj))

    def arrive(event):
        await_bytes(recv.at[event, pl.ds(0, 3)], recv_sem.at[event])

    def put(event, tokens):
        send[event] = tn(tos_ref[...], tokens).astype(BF).reshape(4, SLOT, C)

    def got(event):
        return nn(tos_ref[...], recv[event].reshape(4 * SLOT, C))

    for name in ("up", "son", "tos", "ton"):
        inputs[name].wait()
    send[0] = nn(son_ref[...], up_ref[...].reshape(T, C)).astype(BF).reshape(4, SLOT, C)
    exchange(0, True)

    lane = lax.broadcasted_iota(jnp.int32, (1, 128), 1)
    head_mask = [((lane >= 32 * s) & (lane < 32 * s + 32)).astype(BF) for s in range(4)]
    half_t = lax.broadcasted_iota(jnp.int32, (T, T), 0) < T // 2
    half_s = lax.broadcasted_iota(jnp.int32, (T, T), 1) < T // 2
    one = jnp.where((i == nlat - 1) & (half_t != half_s), 0.0, 1.0).astype(F32)
    for s in range(4):
        seen[T * s : T * s + T] = one
    inside = [(lane >= 32 * s) & (lane < 32 * s + 32) for s in range(4)]
    two = lax.broadcasted_iota(jnp.int32, (128, 128), 1) < 2
    ones_two = jnp.where(two, 1.0, 0.0).astype(BF)
    minus_two = jnp.where(lax.broadcasted_iota(jnp.int32, (T, 128), 1) < 2, -1.0, 0.0).astype(BF)

    def forward(k, x):
        xs[k] = x
        nhat, rstd = norm(x)
        n1h[k] = nhat
        r1[k] = jnp.broadcast_to(rstd, (T, 128))
        n1[k] = nhat.astype(BF)
        give(k, "n1")
        fetches[4 * k].wait()

        for s in range(3):
            cols = slice(s * C, s * C + C)
            us[k, :, cols] = nn(n1[k], wqkv[k, :, cols]).astype(BF)

        @pl.loop(0, 4)
        def _(g):
            def part(w):
                return us[k, :, pl.ds(pl.multiple_of(w * C + g * 128, 128), 128)]

            q, key, v = part(0), part(1), part(2)
            stacked = jnp.concatenate([q * m for m in head_mask], 0)
            e = jnp.exp2(nt(stacked, key) * (32**-0.5 / np.log(2.0)))
            if k == 1:
                e = e * seen[...]
            p = ((e * (1.0 / (0.25 * jnp.sum(e, -1, keepdims=True)))) * 0.25).astype(BF)
            ps[k, g] = p
            out = nn(p, v)
            total = jnp.zeros((T, 128), F32)
            for s in range(4):
                total += jnp.where(inside[s], out[T * s : T * s + T], 0.0)
            att[k, :, pl.ds(pl.multiple_of(g * 128, 128), 128)] = total.astype(BF)

        give(k, "att")
        fetches[4 * k + 1].wait()
        m = xs[k] + nn(att[k], wproj[k])
        acc[...] = m
        nhat, rstd = norm(m)
        n2h[k] = nhat
        r2[k] = jnp.broadcast_to(rstd, (T, 128))
        n2[k] = nhat.astype(BF)
        give(k, "n2")
        fetches[4 * k + 2].wait()
        fetches[4 * k + 3].wait()

        for s in range(4):
            cols = slice(s * C, s * C + C)
            z = nn(n2[k], wup[k, :, cols])
            cdf = 0.5 * (1.0 + lax.erf(z * (2.0**-0.5)))
            gp[k, :, cols] = cdf + z * (jnp.exp(-0.5 * z * z) * ((2.0 * np.pi) ** -0.5))
            h = (z * cdf).astype(BF)
            hs[k, :, cols] = h
            acc[...] += nn(h, wdown[k, cols, :])

        give(k, "hs")
        return acc[...]

    def backward(k, ct, after_up, after_proj, amid):
        acc[...] = ct
        ed[k] = ct.astype(BF)
        give(k, "ed")

        for s in range(4):
            cols = slice(s * C, s * C + C)
            dh = nt(ed[k], wdown[k, cols, :]).astype(BF).astype(F32)
            eu[k, :, cols] = (dh * gp[k, :, cols]).astype(BF)

        give(k, "eu")
        after_up()
        dn2 = nt(eu[k], wup[k]).astype(BF).astype(F32)
        dm = acc[...] + norm_back(dn2, n2h[k], r2[k][:, 0:1])
        acc[...] = dm
        ep[k] = dm.astype(BF)
        give(k, "ep")
        grads_c(k)
        dab[...] = nt(ep[k], wproj[k]).astype(BF)
        grads_b(k)
        after_proj()

        def heads(g):
            def at(w):
                return pl.ds(pl.multiple_of(w * C + g * 128, 128), 128)

            q, key, v = us[k, :, at(0)], us[k, :, at(1)], us[k, :, at(2)]
            da = dab[:, at(0)]
            prod = da.astype(F32) * att[k, :, at(0)].astype(F32)
            high = prod.astype(BF)
            low = (prod - high.astype(F32)).astype(BF)
            stacked_da = jnp.concatenate([da * m for m in head_mask], 0)
            sums = nn(jnp.concatenate([high * m for m in head_mask], 0), ones_two)
            sums += nn(jnp.concatenate([low * m for m in head_mask], 0), ones_two)
            sums_high = sums.astype(BF).astype(F32)
            sums = jnp.where(lane == 0, sums_high, sums - sums_high).astype(BF)
            p = ps[k, g]
            dp = nt(jnp.concatenate([stacked_da, sums], 1), jnp.concatenate([v, minus_two], 1))
            ds = (p.astype(F32) * dp).astype(BF)
            dv = tn(p, stacked_da)
            dk = tn(ds, jnp.concatenate([q * m for m in head_mask], 0))
            out = nn(ds, key)
            dq = jnp.zeros((T, 128), F32)
            for s in range(4):
                dq += jnp.where(inside[s], out[T * s : T * s + T], 0.0)
            eq[k, :, at(0)] = (dq * (32**-0.5)).astype(BF)
            eq[k, :, at(1)] = (dk * (32**-0.5)).astype(BF)
            eq[k, :, at(2)] = dv.astype(BF)

        for half in range(2):
            pl.loop(2 * half, 2 * half + 2)(heads)
            amid(half)
        give(k, "eq")

    def backward_end(k):
        dn1 = nt(eq[k], wqkv[k]).astype(BF).astype(F32)
        return acc[...] + norm_back(dn1, n1h[k], r1[k][:, 0:1])

    def nothing():
        pass

    inputs["swap"].wait()
    lane_finish(0)
    for half in range(2):
        moved = nn(came[half].reshape(64, 1024), swap[...]).astype(BF)
        for lr in range(8 if half == 0 else 4):
            for g in range(4):
                at = (slice(128 * half + 16 * lr, 128 * half + 16 * lr + 16), slice(128 * g, 128 * g + 128))
                nat2[at] = moved[16 * g : 16 * g + 16, 128 * lr : 128 * lr + 128]
    first = forward(0, nn(ton_ref[...], nat2[...]))
    put(1, first.astype(BF))
    exchange(1, True)
    arrive(1)
    second = forward(1, got(1))
    put(2, second.astype(BF))
    exchange(2, False)
    arrive(0)

    def mids(k, parts):
        for p in parts:
            ring_mid(k, p)

    def ends(k, parts):
        for p in parts:
            ring_end(k, p)

    def lasts(k, parts):
        for p in parts:
            ring_last(k, p)

    def amid_one(half):
        if half == 1:
            mids(1, (4, 5))

    backward(1, got(0), nothing, nothing, amid_one)
    d_second = backward_end(1)
    put(3, d_second.astype(BF))
    exchange(3, False)
    grads_a(1)
    mids(1, (2, 3))
    arrive(3)

    def up_zero():
        ends(1, (4, 5))
        mids(1, (0, 1))

    def proj_zero():
        ends(1, (2, 3))

    def amid_zero(half):
        if half == 0:
            ends(1, (0, 1))
        else:
            mids(0, (4, 5, 2, 3))

    backward(0, got(3), up_zero, proj_zero, amid_zero)
    grads_a(0)
    ends(0, (4, 5))
    d_first = backward_end(0)
    nat2[...] = tn(ton_ref[...], d_first.astype(BF)).astype(BF)
    for half in range(2):
        for lr in range(8):
            for g in range(4):
                at = (slice(16 * g, 16 * g + 16), slice(128 * lr, 128 * lr + 128))
                if half == 1 and lr >= 4:
                    turned[half, at[0], at[1]] = jnp.zeros((16, 128), BF)
                else:
                    row = 128 * half + 16 * lr
                    turned[half, at[0], at[1]] = nat2[row : row + 16, 128 * g : 128 * g + 128]
        moved = nn(turned[half], swap[...]).astype(BF)
        for g in range(4):
            for lane_block in range(8):
                leave2[8 * g + lane_block, half] = moved[
                    16 * g : 16 * g + 16, 128 * lane_block : 128 * lane_block + 128
                ]
    lane_start(1)
    mids(0, (0, 1))
    ends(0, (2, 3))
    arrive(2)
    natural = tn(son_ref[...], recv[2].reshape(4 * SLOT, C)).astype(BF)
    mixed_ref[...] = natural.reshape(T // LEV, LEV, C)
    stores = []

    def store(src, dst):
        stores.append(pltpu.make_async_copy(src, dst, out_sem.at[len(stores)]))
        stores[-1].start()

    store(mixed_ref, mixed_hbm)
    lasts(1, range(6))
    ends(0, (0, 1))
    lasts(0, (4, 5, 2, 3))
    store(oup_ref, oup_hbm)
    store(odown_ref, odown_hbm)
    lane_finish(1)
    for half in range(2):
        rows = tn(came2[:, half].reshape(512, 128), spread_ref[...]).astype(BF)
        n = 8 if half == 0 else 4
        denc_ref[8 * half : 8 * half + n] = rows[0 : 16 * n].reshape(n, 16, 32 * WLON)
    store(denc_ref, denc_hbm)
    lasts(0, (0, 1))
    store(oqkv_ref, oqkv_hbm)
    store(oproj_ref, oproj_hbm)
    for event in range(4):
        await_bytes(send.at[event, pl.ds(0, 3)], send_sem.at[event])
    for k in range(2):
        for name in names:
            taken(k, name, pair_send)
        for p in range(6):
            await_bytes(part.at[k, p, pl.ds(0, 3)], ring_send.at[k, p])
            await_bytes(plane_in.at[k, p, pl.ds(1, 15)], plane_send.at[k, p])
    for copy in stores:
        copy.wait()


def copies_kernel(*refs):
    for n in range(6):
        refs[6 + n][...] = refs[n][...]


def layers(encoded, upstream, w_qkv, w_proj, w_up, w_down):
    hbm = pl.BlockSpec(memory_space=pl.ANY)
    vmem = pl.BlockSpec(memory_space=pltpu.VMEM)
    dma = pltpu.SemaphoreType.DMA
    V = pltpu.VMEM
    shapes = (
        jax.ShapeDtypeStruct((T // LEV, LEV, C), BF),
        jax.ShapeDtypeStruct((12, 16, 32 * WLON), BF),
        jax.ShapeDtypeStruct((12, 2, C), F32),
        jax.ShapeDtypeStruct((2, 4, C), F32),
        jax.ShapeDtypeStruct((2, 16, C), F32),
        jax.ShapeDtypeStruct((2, 4, FF), F32),
    )
    results = pl.pallas_call(
        layers_kernel,
        out_shape=shapes,
        in_specs=[hbm] * 11,
        out_specs=(hbm,) * 6,
        scratch_shapes=[
            V((12, 16, 32 * WLON), BF), V((T // LEV, LEV, C), BF), V((4 * SLOT, T), BF), V((T, 4 * SLOT), BF),
            V((T, 12 * 16), BF), V((512, 32 * WLON), BF), dma((7,)),
            *[V(shape.shape, shape.dtype) for shape in shapes], dma((6,)),
            V((2, C, 3 * C), BF), V((2, C, C), BF), V((2, C, FF), BF), V((2, FF, C), BF),
            dma((2, 4)),
            V((1024, 1024), BF), V((32, 2, 16, 128), BF), V((2, 4, 16, 1024), BF),
            V((32, 2, 16, 128), BF), V((32, 2, 16, 128), BF), dma((2,)), dma((2,)),
            V((12 * 16, C), BF), V((2, 64, 1024), BF),
            V((4, 4, SLOT, C), BF), V((4, 4, SLOT, C), BF),
            dma((4,)), dma((4,)),
            V((2, T, C), F32), V((2, T, C), F32), V((2, T, C), BF), V((2, T, 128), F32),
            V((2, T, 3 * C), BF), V((2, 4, 4 * T, T), BF), V((2, T, C), BF),
            V((4 * T, T), F32),
            V((2, T, C), F32), V((2, T, C), BF), V((2, T, 128), F32),
            V((2, T, FF), F32), V((2, T, FF), BF), V((T, C), F32),
            V((2, T, 3 * C), BF), V((2, T, C), BF), V((2, T, FF), BF), V((2, T, C), BF), V((T, C), BF),
            V((2, T, C), BF), V((2, T, C), BF), V((2, T, C), BF), V((2, T, FF), BF),
            V((2, 2, T, 384), BF), V((2, 2, T, 128), BF), V((2, 2, T, 512), BF), V((2, 2, T, 128), BF),
            dma((2, 8)), dma((2, 8)),
            V((2, 6, 4, 4, 64, 256), BF), V((2, 6, 2, 2, 64, 256), BF), V((2, 6, 2, 2, 64, 256), BF),
            V((2, 6, 2, 4, 64, 256), BF), V((2, 6, 4, 4, 16, 256), BF), V((2, 6, 16, 16, 256), BF),
            dma((2, 6)), dma((2, 6, 3)), dma((2, 6)), dma((2, 6)),
        ],
        compiler_params=pltpu.CompilerParams(
            collective_id=0, has_side_effects=True, vmem_limit_bytes=60 * 2**20
        ),
    )(encoded, upstream, *permutations(), w_qkv, w_proj, w_up, w_down)
    return pl.pallas_call(
        copies_kernel,
        out_shape=shapes,
        in_specs=[vmem] * 6,
        out_specs=(vmem,) * 6,
    )(*results)


def on_device(encoded, upstream, w_qkv, w_proj, w_up, w_down):
    mixed, dencoded, qkv, proj, up, down = layers(
        encoded.reshape(12, 16, 32 * WLON),
        upstream.transpose(1, 2, 0, 3).reshape(T // LEV, LEV, C),
        w_qkv, w_proj, w_up, w_down,
    )
    return (
        mixed.reshape(WLAT, WLON, LEV, C).transpose(2, 0, 1, 3),
        dencoded.reshape(encoded.shape),
        qkv.transpose(1, 2, 0),
        proj.swapaxes(1, 2),
        up.swapaxes(1, 2),
        down.swapaxes(1, 2),
    )


def solution(mesh):
    return jax.shard_map(
        on_device,
        mesh=mesh,
        in_specs=(P(None, "lat", "lon", None), P(None, "lat", "lon", None), P(), P(), P(), P()),
        out_specs=(
            P(None, "lat", "lon", None),
            P(None, "lat", "lon", None),
            P(None, None, ("lat", "lon")),
            P(None, None, ("lat", "lon")),
            P(None, None, ("lat", "lon")),
            P(None, None, ("lat", "lon")),
        ),
        check_vma=False,
    )
```

```python
import functools

import jax
import jax.numpy as jnp
import numpy as np
from jax import lax
from jax.experimental import pallas as pl
from jax.experimental.pallas import tpu as pltpu
from jax.sharding import PartitionSpec as P

HEADS = 16
WLAT = 6
WLON = 12
LEV = 2
C = 512
FF = 2048
T = LEV * WLAT * WLON
QUAD = T // 4
SLOT = 48
NORM_EPS = 1e-05
MESH = pl.DeviceIdType.MESH
BF = jnp.bfloat16
F32 = jnp.float32


def quadrant_order():
    return [
        (l, 3 * a + r, 6 * b + c)
        for a in range(2)
        for b in range(2)
        for l in range(LEV)
        for r in range(3)
        for c in range(6)
    ]


def permutations():
    slots_of_natural = np.zeros((4 * SLOT, T), np.float32)
    tokens_of_slots = np.zeros((T, 4 * SLOT), np.float32)
    tokens_of_padded = np.zeros((T, 12 * 16), np.float32)
    for t, (l, r, c) in enumerate(quadrant_order()):
        slot = t // QUAD * SLOT + t % QUAD
        slots_of_natural[slot, (r * WLON + c) * LEV + l] = 1
        tokens_of_slots[t, slot] = 1
        tokens_of_padded[t, (l * WLAT + r) * 16 + c] = 1
    spread = np.zeros((32 * 16, 32 * WLON), np.float32)
    for col in range(32 * WLON):
        spread[col // WLON * 16 + col % WLON, col] = 1
    swap = np.eye(1024, dtype=np.float32).reshape(8, 8, 16, 1024).swapaxes(0, 1).reshape(1024, 1024)
    matrices = (slots_of_natural, tokens_of_slots, tokens_of_padded, spread, swap)
    return [jnp.asarray(m, BF) for m in matrices]


def nn(a, b):
    return lax.dot_general(a, b, (((1,), (0,)), ((), ())), preferred_element_type=F32)


def nt(a, b):
    return lax.dot_general(a, b, (((1,), (1,)), ((), ())), preferred_element_type=F32)


def tn(a, b):
    return lax.dot_general(a, b, (((0,), (0,)), ((), ())), preferred_element_type=F32)


def norm(x):
    centred = x - jnp.mean(x, -1, keepdims=True)
    rstd = lax.rsqrt(jnp.mean(centred * centred, -1, keepdims=True) + NORM_EPS)
    return centred * rstd, rstd


def norm_back(dn, nhat, rstd):
    return rstd * (
        dn - jnp.mean(dn, -1, keepdims=True) - nhat * jnp.mean(dn * nhat, -1, keepdims=True)
    )


def layers_kernel(
    enc_hbm, up_hbm, son_hbm, tos_hbm, ton_hbm, spread_hbm, swap_hbm,
    wqkv_hbm, wproj_hbm, wup_hbm, wdown_hbm,
    mixed_hbm, denc_hbm, oqkv_hbm, oproj_hbm, oup_hbm, odown_hbm,
    enc_ref, up_ref, son_ref, tos_ref, ton_ref, spread_ref, in_sem,
    mixed_ref, denc_ref, oqkv_ref, oproj_ref, oup_ref, odown_ref, out_sem,
    wqkv, wproj, wup, wdown, wsem,
    swap, leave, came, leave2, came2, lane_send, lane_recv, nat2, turned, send, recv, send_sem, recv_sem,
    xs, n1h, n1, r1, us, ps, att, seen, n2h, n2, r2, gp, hs, acc, eq, ep, eu, ed, dab,
    pn1, patt, pn2, phs, peq, pep, peu, ped, pair_send, pair_recv,
    part, fwd, fsum, side, plane_out, plane_in, ring_send, ring_recv, plane_send, plane_recv,
):
    i, j = lax.axis_index("lat"), lax.axis_index("lon")
    nlat, nlon = lax.axis_size("lat"), lax.axis_size("lon")

    def device(di, dj):
        return (lax.rem(i + di + nlat, nlat), lax.rem(j + dj + nlon, nlon))

    core, z, y = lax.rem(i, 2), lax.rem(j, 4), j // 8
    x = i // 2 * 2 + lax.rem(j // 4, 2)

    def along(axis, steps):
        at = {"x": x, "y": y, "z": z}
        at[axis] = lax.rem(at[axis] + steps + 4, 4)
        return (at["x"] // 2 * 2 + core, at["y"] * 8 + lax.rem(at["x"], 2) * 4 + at["z"])

    def beside(axis, steps, other, others):
        at = {"x": x, "y": y, "z": z}
        at[axis] = lax.rem(at[axis] + steps + 4, 4)
        at[other] = lax.rem(at[other] + others + 4, 4)
        return (at["x"] // 2 * 2 + core, at["y"] * 8 + lax.rem(at["x"], 2) * 4 + at["z"])

    partner = (i + 1 - 2 * core, j)

    weights = ((wqkv_hbm, wqkv), (wproj_hbm, wproj), (wup_hbm, wup), (wdown_hbm, wdown))
    inputs = {}
    for at, (name, src, dst) in enumerate(
        (
            ("enc", enc_hbm, enc_ref), ("spread", spread_hbm, spread_ref), ("up", up_hbm, up_ref),
            ("son", son_hbm, son_ref), ("tos", tos_hbm, tos_ref), ("ton", ton_hbm, ton_ref),
            ("swap", swap_hbm, swap),
        )
    ):
        inputs[name] = pltpu.make_async_copy(src, dst, in_sem.at[at])
    inputs["enc"].start()
    inputs["spread"].start()
    fetches = [
        pltpu.make_async_copy(src.at[k], dst.at[k], wsem.at[k, w]) for k in range(2) for w, (src, dst) in enumerate(weights)
    ]

    barrier = pltpu.get_barrier_semaphore()
    far = lambda xl, dy, dz: (lax.rem(i + 2, 4), lax.rem(y + dy, 4) * 8 + xl * 4 + lax.rem(z + dz, 4))
    greeted = [device(1, 0), device(-1, 0), device(1, 1), device(-1, -1)]
    greeted += [far(xl, 0, dz) for xl in range(2) for dz in range(4)]
    greeted += [far(xl, dy, 0) for xl in range(2) for dy in (1, 2, 3)]
    for other in greeted:
        pl.semaphore_signal(barrier, inc=1, device_id=other, device_id_type=MESH)

    @pl.loop(1, nlon)
    def _(step):
        pl.semaphore_signal(barrier, inc=1, device_id=device(0, step), device_id_type=MESH)

    for name in ("up", "son", "tos", "ton", "swap"):
        inputs[name].start()
    for fetch in fetches:
        fetch.start()

    inputs["enc"].wait()
    inputs["spread"].wait()
    columns_first = nt(spread_ref[...], enc_ref[...].reshape(12 * 16, 32 * WLON)).astype(BF)
    leave[:, 0] = columns_first[:, 0:128].reshape(32, 16, 128)
    leave[:, 1, :, 0:64] = columns_first[:, 128:192].reshape(32, 16, 64)
    leave[:, 1, :, 64:128] = jnp.zeros((32, 16, 64), BF)
    pl.semaphore_wait(barrier, len(greeted) + nlon - 1)
    mine = pl.ds(pl.multiple_of(lax.rem(j, 8) * 128, 128), 128)

    def lane_copy(step, event):
        to = lax.rem(j + step, nlon)
        if event == 0:
            src, dst = leave.at[to], came.at[:, j // 8, :, mine]
        else:
            src, dst = leave2.at[to], came2.at[j]
        return pltpu.make_async_remote_copy(
            src_ref=src, dst_ref=dst, send_sem=lane_send.at[event], recv_sem=lane_recv.at[event],
            device_id=(i, to), device_id_type=MESH,
        )

    def lane_start(event):
        @pl.loop(1, nlon)
        def _(step):
            lane_copy(step, event).start()

        if event == 0:
            src, dst = leave.at[j], came.at[:, j // 8, :, mine]
        else:
            src, dst = leave2.at[j], came2.at[j]
        pltpu.make_async_copy(src, dst, lane_recv.at[event]).start()

    def lane_finish(event):
        await_bytes((came, came2)[event], lane_recv.at[event])
        await_bytes((leave, leave2)[event].at[pl.ds(0, 31)], lane_send.at[event])

    lane_start(0)

    def remote(src, dst, sems, to):
        pltpu.make_async_remote_copy(
            src_ref=src, dst_ref=dst, send_sem=sems[0], recv_sem=sems[1], device_id=to, device_id_type=MESH
        ).start()

    def await_bytes(like, sem):
        pltpu.make_async_copy(like, like, sem).wait()

    wide = {"eq": 384, "ep": 128, "eu": 512, "ed": 128}
    whole = {"n1": (n1, pn1), "att": (att, patt), "n2": (n2, pn2), "hs": (hs, phs)}
    cut = {"eq": (eq, peq), "ep": (ep, pep), "eu": (eu, peu), "ed": (ed, ped)}

    def columns(name, hi, owner):
        width = wide[name]
        return pl.ds(pl.multiple_of((2 * hi + owner) * width, width), width)

    names = ("n1", "att", "n2", "hs", "eq", "ep", "eu", "ed")

    def give(k, name):
        sems = (pair_send.at[k, names.index(name)], pair_recv.at[k, names.index(name)])
        if name in whole:
            src, dst = whole[name]
            remote(src.at[k], dst.at[k], sems, partner)
        else:
            src, dst = cut[name]
            for hi in range(2):
                remote(src.at[k, :, columns(name, hi, 1 - core)], dst.at[k, hi], sems, partner)

    def taken(k, name, sems):
        dst = (whole[name] if name in whole else cut[name])[1]
        await_bytes(dst.at[k], sems.at[k, names.index(name)])

    def take(k, name):
        taken(k, name, pair_recv)

    orders = ("xyz", "xyz", "yxz", "yxz", "zyx", "zyx")
    where = {"x": x, "y": y, "z": z}

    def chunk(k, p, t, half):
        return part.at[k, p, lax.rem(t + 4, 4), pl.ds(2 * half, 2)]

    def f32(ref):
        return ref[...].astype(F32)

    def ring_start(k, p):
        axis = orders[p][0]
        t = where[axis]
        after, before = along(axis, 1), along(axis, -1)
        out = ring_send.at[k, p]
        remote(chunk(k, p, t + 2, 0), fwd.at[k, p, 0], (out, ring_recv.at[k, p, 0]), after)
        remote(chunk(k, p, t + 2, 1), fwd.at[k, p, 1], (out, ring_recv.at[k, p, 1]), before)
        remote(chunk(k, p, t + 1, 1), side.at[k, p, 0, pl.ds(2, 2)], (out, ring_recv.at[k, p, 2]), after)
        remote(chunk(k, p, t - 1, 0), side.at[k, p, 1, pl.ds(0, 2)], (out, ring_recv.at[k, p, 2]), before)

    def ring_mid(k, p):
        axis = orders[p][0]
        t = where[axis]
        after, before = along(axis, 1), along(axis, -1)
        sems = (ring_send.at[k, p], ring_recv.at[k, p, 2])
        await_bytes(fwd.at[k, p, 0], ring_recv.at[k, p, 0])
        fsum[k, p, 0] = (f32(fwd.at[k, p, 0]) + f32(chunk(k, p, t + 1, 0))).astype(BF)
        remote(fsum.at[k, p, 0], side.at[k, p, 0, pl.ds(0, 2)], sems, after)
        await_bytes(fwd.at[k, p, 1], ring_recv.at[k, p, 1])
        fsum[k, p, 1] = (f32(fwd.at[k, p, 1]) + f32(chunk(k, p, t - 1, 1))).astype(BF)
        remote(fsum.at[k, p, 1], side.at[k, p, 1, pl.ds(2, 2)], sems, before)

    def plane_copy(k, p, count, step):
        _, second, third = orders[p]
        d2, d3 = step // 4, lax.rem(step, 4)
        held = pl.ds(p % 2, count)
        src = plane_out.at[k, p // 2, lax.rem(where[second] + d2, 4), lax.rem(where[third] + d3, 4), held]
        return pltpu.make_async_remote_copy(
            src_ref=src, dst_ref=plane_in.at[k, p // 2, step, held], send_sem=plane_send.at[k, p],
            recv_sem=plane_recv.at[k, p], device_id=beside(second, d2, third, d3), device_id_type=MESH,
        )

    def plane_start(k, p, count):
        planes.append((k, p, count))

        @pl.loop(1, 16)
        def _(step):
            plane_copy(k, p, count, step).start()

    planes = []

    def plane_bytes(k, p, count):
        return plane_in.at[k, p // 2, pl.ds(1, 15), pl.ds(p % 2, count)]

    def plane_arrive(k, p, count):
        await_bytes(plane_bytes(k, p, count), plane_recv.at[k, p])

    def ring_end(k, p):
        await_bytes(side.at[k, p], ring_recv.at[k, p, 2])
        t = where[orders[p][0]]
        total = f32(part.at[k, p, t]) + f32(side.at[k, p, 0]) + f32(side.at[k, p, 1])
        for s2 in range(4):
            for s3 in range(4):
                if p in (0, 2):
                    rows = (total[s2, 12 * s3 : 12 * s3 + 12], total[s2, 48 + 4 * s3 : 52 + 4 * s3])
                    rows = jnp.concatenate(rows, 0)
                elif p in (4, 5):
                    rows = total[s2, 16 * s3 : 16 * s3 + 16]
                else:
                    rows = [total[s2, 16 * hb + 4 * s3 : 16 * hb + 4 * s3 + 4] for hb in range(4)]
                    rows = jnp.concatenate(rows, 0)
                plane_out[k, p // 2, s2, s3, p % 2] = rows.astype(BF)

    def ring_last(k, p):
        _, second, third = orders[p]
        total = f32(plane_out.at[k, p // 2, where[second], where[third], p % 2])
        for step in range(1, 16):
            total += f32(plane_in.at[k, p // 2, step, p % 2])
        half = p % 2 if p in (4, 5) else p // 2
        lanes = slice(256 * half, 256 * half + 256)
        if p in (0, 2):
            oqkv_ref[:, k, lanes] = total[0:12]
            oproj_ref[k, :, lanes] = total[12:16]
        elif p in (4, 5):
            oup_ref[k, :, lanes] = total
        else:
            for hb in range(4):
                at = slice(hb * C + lanes.start, hb * C + lanes.stop)
                odown_ref[k, :, at] = total[4 * hb : 4 * hb + 4]

    def both(k, name, hi, own, theirs):
        src, dst = cut[name]
        return tn(src[k, :, columns(name, hi, core)], own) + tn(dst[k, hi], theirs)

    def keep(k, p, first, second, rows, g):
        for s in range(2):
            q = p + s if p == 4 else p + 2 * s
            at = (first, second) if orders[q][0] == orders[p][0] else (second, first)
            part[k, q, at[0], at[1], rows, :] = g[:, 256 * s : 256 * s + 256]

    def grads_a(k):
        for name in ("n1", "att", "ep", "eq"):
            take(k, name)
        for hi in range(2):
            g = both(k, "eq", hi, n1[k], pn1[k]).astype(BF)
            for at in range(8):
                keep(k, 0, 2 * hi + at % 2, at // 2, slice(0, 48), g[48 * at : 48 * at + 48])
            g = both(k, "ep", hi, att[k], patt[k]).astype(BF)
            for at in range(8):
                keep(k, 0, 2 * hi + at % 2, at // 2, slice(48, 64), g[16 * at : 16 * at + 16])
        ring_start(k, 0)
        ring_start(k, 2)

    def grads_b(k):
        for name in ("n2", "eu"):
            take(k, name)
        for hi in range(2):
            g = both(k, "eu", hi, n2[k], pn2[k]).astype(BF)
            for at in range(32):
                row = (2 * hi + at // 4 % 2) * 16
                keep(k, 4, at % 4, at // 8, slice(row, row + 16), g[16 * at : 16 * at + 16])
        ring_start(k, 4)
        ring_start(k, 5)

    def grads_c(k):
        for name in ("hs", "ed"):
            take(k, name)
        for hi in range(2):
            for hb in range(4):
                cols = slice(hb * C, hb * C + C)
                g = both(k, "ed", hi, hs[k, :, cols], phs[k, :, cols]).astype(BF)
                for at in range(8):
                    row = 16 * hb
                    keep(k, 1, 2 * hi + at % 2, at // 2, slice(row, row + 16), g[16 * at : 16 * at + 16])
        ring_start(k, 1)
        ring_start(k, 3)

    def exchange(event, forward):
        for q in range(4):
            a, b = q // 2, q % 2
            di, dj = (a - 1, b - 1) if forward else (a, b)
            if (di, dj) == (0, 0):
                recv[event, 3 - q] = send[event, q]
            else:
                sems = (send_sem.at[event], recv_sem.at[event])
                remote(send.at[event, q], recv.at[event, 3 - q], sems, device(di, dj))

    def arrive(event):
        await_bytes(recv.at[event, pl.ds(0, 3)], recv_sem.at[event])

    def put(event, tokens):
        send[event] = tn(tos_ref[...], tokens).astype(BF).reshape(4, SLOT, C)

    def got(event):
        return nn(tos_ref[...], recv[event].reshape(4 * SLOT, C))

    for name in ("up", "son", "tos", "ton"):
        inputs[name].wait()
    send[0] = nn(son_ref[...], up_ref[...].reshape(T, C)).astype(BF).reshape(4, SLOT, C)
    exchange(0, True)

    lane = lax.broadcasted_iota(jnp.int32, (1, 128), 1)
    head_mask = [((lane >= 32 * s) & (lane < 32 * s + 32)).astype(BF) for s in range(4)]
    half_t = lax.broadcasted_iota(jnp.int32, (T, T), 0) < T // 2
    half_s = lax.broadcasted_iota(jnp.int32, (T, T), 1) < T // 2
    one = jnp.where((i == nlat - 1) & (half_t != half_s), 0.0, 1.0).astype(F32)
    for s in range(4):
        seen[T * s : T * s + T] = one
    inside = [(lane >= 32 * s) & (lane < 32 * s + 32) for s in range(4)]
    two = lax.broadcasted_iota(jnp.int32, (128, 128), 1) < 2
    ones_two = jnp.where(two, 1.0, 0.0).astype(BF)
    minus_two = jnp.where(lax.broadcasted_iota(jnp.int32, (T, 128), 1) < 2, -1.0, 0.0).astype(BF)

    def forward(k, x):
        xs[k] = x
        nhat, rstd = norm(x)
        n1h[k] = nhat
        r1[k] = jnp.broadcast_to(rstd, (T, 128))
        n1[k] = nhat.astype(BF)
        give(k, "n1")
        fetches[4 * k].wait()

        for s in range(3):
            cols = slice(s * C, s * C + C)
            us[k, :, cols] = nn(n1[k], wqkv[k, :, cols]).astype(BF)

        @pl.loop(0, 4)
        def _(g):
            def part(w):
                return us[k, :, pl.ds(pl.multiple_of(w * C + g * 128, 128), 128)]

            q, key, v = part(0), part(1), part(2)
            stacked = jnp.concatenate([q * m for m in head_mask], 0)
            e = jnp.exp2(nt(stacked, key) * (32**-0.5 / np.log(2.0)))
            if k == 1:
                e = e * seen[...]
            p = ((e * (1.0 / (0.25 * jnp.sum(e, -1, keepdims=True)))) * 0.25).astype(BF)
            ps[k, g] = p
            out = nn(p, v)
            total = jnp.zeros((T, 128), F32)
            for s in range(4):
                total += jnp.where(inside[s], out[T * s : T * s + T], 0.0)
            att[k, :, pl.ds(pl.multiple_of(g * 128, 128), 128)] = total.astype(BF)

        give(k, "att")
        fetches[4 * k + 1].wait()
        m = xs[k] + nn(att[k], wproj[k])
        acc[...] = m
        nhat, rstd = norm(m)
        n2h[k] = nhat
        r2[k] = jnp.broadcast_to(rstd, (T, 128))
        n2[k] = nhat.astype(BF)
        give(k, "n2")
        fetches[4 * k + 2].wait()
        fetches[4 * k + 3].wait()

        for s in range(4):
            cols = slice(s * C, s * C + C)
            z = nn(n2[k], wup[k, :, cols])
            cdf = 0.5 * (1.0 + lax.erf(z * (2.0**-0.5)))
            gp[k, :, cols] = cdf + z * (jnp.exp(-0.5 * z * z) * ((2.0 * np.pi) ** -0.5))
            h = (z * cdf).astype(BF)
            hs[k, :, cols] = h
            acc[...] += nn(h, wdown[k, cols, :])

        give(k, "hs")
        return acc[...]

    def backward(k, ct, after_up, after_proj, amid):
        acc[...] = ct
        ed[k] = ct.astype(BF)
        give(k, "ed")

        for s in range(4):
            cols = slice(s * C, s * C + C)
            dh = nt(ed[k], wdown[k, cols, :]).astype(BF).astype(F32)
            eu[k, :, cols] = (dh * gp[k, :, cols]).astype(BF)

        give(k, "eu")
        after_up()
        dn2 = nt(eu[k], wup[k]).astype(BF).astype(F32)
        dm = acc[...] + norm_back(dn2, n2h[k], r2[k][:, 0:1])
        acc[...] = dm
        ep[k] = dm.astype(BF)
        give(k, "ep")
        grads_c(k)
        dab[...] = nt(ep[k], wproj[k]).astype(BF)
        grads_b(k)
        after_proj()

        def heads(g):
            def at(w):
                return pl.ds(pl.multiple_of(w * C + g * 128, 128), 128)

            q, key, v = us[k, :, at(0)], us[k, :, at(1)], us[k, :, at(2)]
            da = dab[:, at(0)]
            prod = da.astype(F32) * att[k, :, at(0)].astype(F32)
            high = prod.astype(BF)
            low = (prod - high.astype(F32)).astype(BF)
            stacked_da = jnp.concatenate([da * m for m in head_mask], 0)
            sums = nn(jnp.concatenate([high * m for m in head_mask], 0), ones_two)
            sums += nn(jnp.concatenate([low * m for m in head_mask], 0), ones_two)
            sums_high = sums.astype(BF).astype(F32)
            sums = jnp.where(lane == 0, sums_high, sums - sums_high).astype(BF)
            p = ps[k, g]
            dp = nt(jnp.concatenate([stacked_da, sums], 1), jnp.concatenate([v, minus_two], 1))
            ds = (p.astype(F32) * dp).astype(BF)
            dv = tn(p, stacked_da)
            dk = tn(ds, jnp.concatenate([q * m for m in head_mask], 0))
            out = nn(ds, key)
            dq = jnp.zeros((T, 128), F32)
            for s in range(4):
                dq += jnp.where(inside[s], out[T * s : T * s + T], 0.0)
            eq[k, :, at(0)] = (dq * (32**-0.5)).astype(BF)
            eq[k, :, at(1)] = (dk * (32**-0.5)).astype(BF)
            eq[k, :, at(2)] = dv.astype(BF)

        for half in range(2):
            pl.loop(2 * half, 2 * half + 2)(heads)
            amid(half)
        give(k, "eq")

    def backward_end(k):
        dn1 = nt(eq[k], wqkv[k]).astype(BF).astype(F32)
        return acc[...] + norm_back(dn1, n1h[k], r1[k][:, 0:1])

    def nothing():
        pass

    inputs["swap"].wait()
    lane_finish(0)
    for half in range(2):
        moved = nn(came[half].reshape(64, 1024), swap[...]).astype(BF)
        for lr in range(8 if half == 0 else 4):
            for g in range(4):
                at = (slice(128 * half + 16 * lr, 128 * half + 16 * lr + 16), slice(128 * g, 128 * g + 128))
                nat2[at] = moved[16 * g : 16 * g + 16, 128 * lr : 128 * lr + 128]
    first = forward(0, nn(ton_ref[...], nat2[...]))
    put(1, first.astype(BF))
    exchange(1, True)
    arrive(1)
    second = forward(1, got(1))
    put(2, second.astype(BF))
    exchange(2, False)
    arrive(0)

    def mids(k, parts):
        for p in parts:
            ring_mid(k, p)

    def ends(k, parts):
        for p in parts:
            ring_end(k, p)

    def lasts(k, parts):
        for p in parts:
            ring_last(k, p)

    def amid_one(half):
        if half == 1:
            mids(1, (1, 3))

    backward(1, got(0), nothing, nothing, amid_one)
    d_second = backward_end(1)
    put(3, d_second.astype(BF))
    exchange(3, False)
    grads_a(1)
    mids(1, (4, 5))
    arrive(3)

    def up_zero():
        mids(1, (0, 2))

    def proj_zero():
        ends(1, (1, 3, 4, 5))
        plane_start(1, 4, 2)

    def amid_zero(half):
        if half == 0:
            ends(1, (0, 2))
            plane_start(1, 0, 2)
            plane_start(1, 2, 2)
        else:
            mids(0, (1, 3, 4, 5))

    backward(0, got(3), up_zero, proj_zero, amid_zero)
    grads_a(0)
    d_first = backward_end(0)
    nat2[...] = tn(ton_ref[...], d_first.astype(BF)).astype(BF)
    for half in range(2):
        for lr in range(8):
            for g in range(4):
                at = (slice(16 * g, 16 * g + 16), slice(128 * lr, 128 * lr + 128))
                if half == 1 and lr >= 4:
                    turned[half, at[0], at[1]] = jnp.zeros((16, 128), BF)
                else:
                    row = 128 * half + 16 * lr
                    turned[half, at[0], at[1]] = nat2[row : row + 16, 128 * g : 128 * g + 128]
        moved = nn(turned[half], swap[...]).astype(BF)
        for g in range(4):
            for lane_block in range(8):
                leave2[8 * g + lane_block, half] = moved[
                    16 * g : 16 * g + 16, 128 * lane_block : 128 * lane_block + 128
                ]
    lane_start(1)
    mids(0, (0, 2))
    ends(0, (1, 3))
    plane_start(0, 1, 1)
    plane_start(0, 3, 1)
    ends(0, (4, 5))
    plane_start(0, 4, 2)
    arrive(2)
    natural = tn(son_ref[...], recv[2].reshape(4 * SLOT, C)).astype(BF)
    mixed_ref[...] = natural.reshape(T // LEV, LEV, C)
    stores = []

    def store(src, dst):
        stores.append(pltpu.make_async_copy(src, dst, out_sem.at[len(stores)]))
        stores[-1].start()

    store(mixed_ref, mixed_hbm)
    ends(0, (0, 2))
    plane_start(0, 0, 1)
    plane_start(0, 2, 1)
    for group in (0, 2, 4):
        plane_arrive(1, group, 2)
    lasts(1, range(6))
    plane_arrive(0, 1, 1)
    plane_arrive(0, 3, 1)
    plane_arrive(0, 4, 2)
    lasts(0, (1, 3, 4, 5))
    store(oup_ref, oup_hbm)
    store(odown_ref, odown_hbm)
    lane_finish(1)
    for half in range(2):
        rows = tn(came2[:, half].reshape(512, 128), spread_ref[...]).astype(BF)
        n = 8 if half == 0 else 4
        denc_ref[8 * half : 8 * half + n] = rows[0 : 16 * n].reshape(n, 16, 32 * WLON)
    store(denc_ref, denc_hbm)
    plane_arrive(0, 0, 1)
    plane_arrive(0, 2, 1)
    lasts(0, (0, 2))
    store(oqkv_ref, oqkv_hbm)
    store(oproj_ref, oproj_hbm)
    for event in range(4):
        await_bytes(send.at[event, pl.ds(0, 3)], send_sem.at[event])
    for k in range(2):
        for name in names:
            taken(k, name, pair_send)
        for p in range(6):
            await_bytes(part.at[k, p, pl.ds(0, 3)], ring_send.at[k, p])
    for k, p, count in planes:
        await_bytes(plane_bytes(k, p, count), plane_send.at[k, p])
    for copy in stores:
        copy.wait()


def copies_kernel(*refs):
    for n in range(6):
        refs[6 + n][...] = refs[n][...]


def layers(encoded, upstream, w_qkv, w_proj, w_up, w_down):
    hbm = pl.BlockSpec(memory_space=pl.ANY)
    vmem = pl.BlockSpec(memory_space=pltpu.VMEM)
    dma = pltpu.SemaphoreType.DMA
    V = pltpu.VMEM
    shapes = (
        jax.ShapeDtypeStruct((T // LEV, LEV, C), BF),
        jax.ShapeDtypeStruct((12, 16, 32 * WLON), BF),
        jax.ShapeDtypeStruct((12, 2, C), F32),
        jax.ShapeDtypeStruct((2, 4, C), F32),
        jax.ShapeDtypeStruct((2, 16, C), F32),
        jax.ShapeDtypeStruct((2, 4, FF), F32),
    )
    results = pl.pallas_call(
        layers_kernel,
        out_shape=shapes,
        in_specs=[hbm] * 11,
        out_specs=(hbm,) * 6,
        scratch_shapes=[
            V((12, 16, 32 * WLON), BF), V((T // LEV, LEV, C), BF), V((4 * SLOT, T), BF), V((T, 4 * SLOT), BF),
            V((T, 12 * 16), BF), V((512, 32 * WLON), BF), dma((7,)),
            *[V(shape.shape, shape.dtype) for shape in shapes], dma((6,)),
            V((2, C, 3 * C), BF), V((2, C, C), BF), V((2, C, FF), BF), V((2, FF, C), BF),
            dma((2, 4)),
            V((1024, 1024), BF), V((32, 2, 16, 128), BF), V((2, 4, 16, 1024), BF),
            V((32, 2, 16, 128), BF), V((32, 2, 16, 128), BF), dma((2,)), dma((2,)),
            V((12 * 16, C), BF), V((2, 64, 1024), BF),
            V((4, 4, SLOT, C), BF), V((4, 4, SLOT, C), BF),
            dma((4,)), dma((4,)),
            V((2, T, C), F32), V((2, T, C), F32), V((2, T, C), BF), V((2, T, 128), F32),
            V((2, T, 3 * C), BF), V((2, 4, 4 * T, T), BF), V((2, T, C), BF),
            V((4 * T, T), F32),
            V((2, T, C), F32), V((2, T, C), BF), V((2, T, 128), F32),
            V((2, T, FF), F32), V((2, T, FF), BF), V((T, C), F32),
            V((2, T, 3 * C), BF), V((2, T, C), BF), V((2, T, FF), BF), V((2, T, C), BF), V((T, C), BF),
            V((2, T, C), BF), V((2, T, C), BF), V((2, T, C), BF), V((2, T, FF), BF),
            V((2, 2, T, 384), BF), V((2, 2, T, 128), BF), V((2, 2, T, 512), BF), V((2, 2, T, 128), BF),
            dma((2, 8)), dma((2, 8)),
            V((2, 6, 4, 4, 64, 256), BF), V((2, 6, 2, 2, 64, 256), BF), V((2, 6, 2, 2, 64, 256), BF),
            V((2, 6, 2, 4, 64, 256), BF), V((2, 3, 4, 4, 2, 16, 256), BF), V((2, 3, 16, 2, 16, 256), BF),
            dma((2, 6)), dma((2, 6, 3)), dma((2, 6)), dma((2, 6)),
        ],
        compiler_params=pltpu.CompilerParams(
            collective_id=0, has_side_effects=True, vmem_limit_bytes=60 * 2**20
        ),
    )(encoded, upstream, *permutations(), w_qkv, w_proj, w_up, w_down)
    return pl.pallas_call(
        copies_kernel,
        out_shape=shapes,
        in_specs=[vmem] * 6,
        out_specs=(vmem,) * 6,
    )(*results)


def on_device(encoded, upstream, w_qkv, w_proj, w_up, w_down):
    mixed, dencoded, qkv, proj, up, down = layers(
        encoded.reshape(12, 16, 32 * WLON),
        upstream.transpose(1, 2, 0, 3).reshape(T // LEV, LEV, C),
        w_qkv, w_proj, w_up, w_down,
    )
    return (
        mixed.reshape(WLAT, WLON, LEV, C).transpose(2, 0, 1, 3),
        dencoded.reshape(encoded.shape),
        qkv.transpose(1, 2, 0),
        proj.swapaxes(1, 2),
        up.swapaxes(1, 2),
        down.swapaxes(1, 2),
    )


def solution(mesh):
    return jax.shard_map(
        on_device,
        mesh=mesh,
        in_specs=(P(None, "lat", "lon", None), P(None, "lat", "lon", None), P(), P(), P(), P()),
        out_specs=(
            P(None, "lat", "lon", None),
            P(None, "lat", "lon", None),
            P(None, None, ("lat", "lon")),
            P(None, None, ("lat", "lon")),
            P(None, None, ("lat", "lon")),
            P(None, None, ("lat", "lon")),
        ),
        check_vma=False,
    )
```

```python
import functools

import jax
import jax.numpy as jnp
import numpy as np
from jax import lax
from jax.experimental import pallas as pl
from jax.experimental.pallas import tpu as pltpu
from jax.sharding import PartitionSpec as P

HEADS = 16
WLAT = 6
WLON = 12
LEV = 2
C = 512
FF = 2048
T = LEV * WLAT * WLON
QUAD = T // 4
SLOT = 48
NORM_EPS = 1e-05
MESH = pl.DeviceIdType.MESH
BF = jnp.bfloat16
F32 = jnp.float32


def quadrant_order():
    return [
        (l, 3 * a + r, 6 * b + c)
        for a in range(2)
        for b in range(2)
        for l in range(LEV)
        for r in range(3)
        for c in range(6)
    ]


def permutations():
    slots_of_natural = np.zeros((4 * SLOT, T), np.float32)
    tokens_of_slots = np.zeros((T, 4 * SLOT), np.float32)
    tokens_of_padded = np.zeros((T, 12 * 16), np.float32)
    for t, (l, r, c) in enumerate(quadrant_order()):
        slot = t // QUAD * SLOT + t % QUAD
        slots_of_natural[slot, (r * WLON + c) * LEV + l] = 1
        tokens_of_slots[t, slot] = 1
        tokens_of_padded[t, (l * WLAT + r) * 16 + c] = 1
    spread = np.zeros((32 * 16, 32 * WLON), np.float32)
    for col in range(32 * WLON):
        spread[col // WLON * 16 + col % WLON, col] = 1
    swap = np.eye(1024, dtype=np.float32).reshape(8, 8, 16, 1024).swapaxes(0, 1).reshape(1024, 1024)
    matrices = (slots_of_natural, tokens_of_slots, tokens_of_padded, spread, swap)
    return [jnp.asarray(m, BF) for m in matrices]


def nn(a, b):
    return lax.dot_general(a, b, (((1,), (0,)), ((), ())), preferred_element_type=F32)


def nt(a, b):
    return lax.dot_general(a, b, (((1,), (1,)), ((), ())), preferred_element_type=F32)


def tn(a, b):
    return lax.dot_general(a, b, (((0,), (0,)), ((), ())), preferred_element_type=F32)


def norm(x):
    centred = x - jnp.mean(x, -1, keepdims=True)
    rstd = lax.rsqrt(jnp.mean(centred * centred, -1, keepdims=True) + NORM_EPS)
    return centred * rstd, rstd


def norm_back(dn, nhat, rstd):
    return rstd * (
        dn - jnp.mean(dn, -1, keepdims=True) - nhat * jnp.mean(dn * nhat, -1, keepdims=True)
    )


def layers_kernel(
    enc_hbm, up_hbm, son_hbm, tos_hbm, ton_hbm, spread_hbm, swap_hbm,
    wqkv_hbm, wproj_hbm, wup_hbm, wdown_hbm,
    mixed_hbm, denc_hbm, oqkv_hbm, oproj_hbm, oup_hbm, odown_hbm,
    enc_ref, up_ref, son_ref, tos_ref, ton_ref, spread_ref, in_sem,
    mixed_ref, denc_ref, oqkv_ref, oproj_ref, oup_ref, odown_ref, out_sem,
    wqkv, wproj, wup, wdown, wsem,
    swap, leave, came, leave2, came2, lane_send, lane_recv, nat2, turned, send, recv, send_sem, recv_sem,
    xs, n1h, n1, r1, us, ps, att, seen, n2h, n2, r2, gp, hs, acc, eq, ep, eu, ed, dab,
    pn1, patt, pn2, phs, peq, pep, peu, ped, pair_send, pair_recv,
    part, fwd, fsum, side, plane_out, plane_in, ring_send, ring_recv, plane_send, plane_recv,
):
    i, j = lax.axis_index("lat"), lax.axis_index("lon")
    nlat, nlon = lax.axis_size("lat"), lax.axis_size("lon")

    def device(di, dj):
        return (lax.rem(i + di + nlat, nlat), lax.rem(j + dj + nlon, nlon))

    core, z, y = lax.rem(i, 2), lax.rem(j, 4), j // 8
    x = i // 2 * 2 + lax.rem(j // 4, 2)

    def along(axis, steps):
        at = {"x": x, "y": y, "z": z}
        at[axis] = lax.rem(at[axis] + steps + 4, 4)
        return (at["x"] // 2 * 2 + core, at["y"] * 8 + lax.rem(at["x"], 2) * 4 + at["z"])

    def beside(axis, steps, other, others):
        at = {"x": x, "y": y, "z": z}
        at[axis] = lax.rem(at[axis] + steps + 4, 4)
        at[other] = lax.rem(at[other] + others + 4, 4)
        return (at["x"] // 2 * 2 + core, at["y"] * 8 + lax.rem(at["x"], 2) * 4 + at["z"])

    partner = (i + 1 - 2 * core, j)

    weights = ((wqkv_hbm, wqkv), (wproj_hbm, wproj), (wup_hbm, wup), (wdown_hbm, wdown))
    inputs = {}
    for at, (name, src, dst) in enumerate(
        (
            ("enc", enc_hbm, enc_ref), ("spread", spread_hbm, spread_ref), ("up", up_hbm, up_ref),
            ("son", son_hbm, son_ref), ("tos", tos_hbm, tos_ref), ("ton", ton_hbm, ton_ref),
            ("swap", swap_hbm, swap),
        )
    ):
        inputs[name] = pltpu.make_async_copy(src, dst, in_sem.at[at])
    inputs["enc"].start()
    inputs["spread"].start()
    fetches = [
        pltpu.make_async_copy(src.at[k], dst.at[k], wsem.at[k, w]) for k in range(2) for w, (src, dst) in enumerate(weights)
    ]

    barrier = pltpu.get_barrier_semaphore()
    far = lambda xl, dy, dz: (lax.rem(i + 2, 4), lax.rem(y + dy, 4) * 8 + xl * 4 + lax.rem(z + dz, 4))
    greeted = [device(1, 0), device(-1, 0), device(1, 1), device(-1, -1)]
    greeted += [far(xl, 0, dz) for xl in range(2) for dz in range(4)]
    greeted += [far(xl, dy, 0) for xl in range(2) for dy in (1, 2, 3)]
    for other in greeted:
        pl.semaphore_signal(barrier, inc=1, device_id=other, device_id_type=MESH)

    @pl.loop(1, nlon)
    def _(step):
        pl.semaphore_signal(barrier, inc=1, device_id=device(0, step), device_id_type=MESH)

    for name in ("up", "son", "tos", "ton", "swap"):
        inputs[name].start()
    for fetch in fetches:
        fetch.start()

    inputs["enc"].wait()
    inputs["spread"].wait()
    columns_first = nt(spread_ref[...], enc_ref[...].reshape(12 * 16, 32 * WLON)).astype(BF)
    leave[:, 0] = columns_first[:, 0:128].reshape(32, 16, 128)
    leave[:, 1, :, 0:64] = columns_first[:, 128:192].reshape(32, 16, 64)
    leave[:, 1, :, 64:128] = jnp.zeros((32, 16, 64), BF)
    pl.semaphore_wait(barrier, len(greeted) + nlon - 1)
    mine = pl.ds(pl.multiple_of(lax.rem(j, 8) * 128, 128), 128)

    def lane_copy(step, event):
        to = lax.rem(j + step, nlon)
        if event == 0:
            src, dst = leave.at[to], came.at[:, j // 8, :, mine]
        else:
            src, dst = leave2.at[to], came2.at[j]
        return pltpu.make_async_remote_copy(
            src_ref=src, dst_ref=dst, send_sem=lane_send.at[event], recv_sem=lane_recv.at[event],
            device_id=(i, to), device_id_type=MESH,
        )

    def lane_start(event):
        @pl.loop(1, nlon)
        def _(step):
            lane_copy(step, event).start()

        if event == 0:
            src, dst = leave.at[j], came.at[:, j // 8, :, mine]
        else:
            src, dst = leave2.at[j], came2.at[j]
        pltpu.make_async_copy(src, dst, lane_recv.at[event]).start()

    def lane_finish(event):
        await_bytes((came, came2)[event], lane_recv.at[event])
        await_bytes((leave, leave2)[event].at[pl.ds(0, 31)], lane_send.at[event])

    lane_start(0)

    def remote(src, dst, sems, to):
        pltpu.make_async_remote_copy(
            src_ref=src, dst_ref=dst, send_sem=sems[0], recv_sem=sems[1], device_id=to, device_id_type=MESH
        ).start()

    def await_bytes(like, sem):
        pltpu.make_async_copy(like, like, sem).wait()

    wide = {"eq": 384, "ep": 128, "eu": 512, "ed": 128}
    whole = {"n1": (n1, pn1), "att": (att, patt), "n2": (n2, pn2), "hs": (hs, phs)}
    cut = {"eq": (eq, peq), "ep": (ep, pep), "eu": (eu, peu), "ed": (ed, ped)}

    def columns(name, hi, owner):
        width = wide[name]
        return pl.ds(pl.multiple_of((2 * hi + owner) * width, width), width)

    names = ("n1", "att", "n2", "hs", "eq", "ep", "eu", "ed")

    def give(k, name):
        sems = (pair_send.at[k, names.index(name)], pair_recv.at[k, names.index(name)])
        if name in whole:
            src, dst = whole[name]
            remote(src.at[k], dst.at[k], sems, partner)
        else:
            src, dst = cut[name]
            for hi in range(2):
                remote(src.at[k, :, columns(name, hi, 1 - core)], dst.at[k, hi], sems, partner)

    def taken(k, name, sems):
        dst = (whole[name] if name in whole else cut[name])[1]
        await_bytes(dst.at[k], sems.at[k, names.index(name)])

    def take(k, name):
        taken(k, name, pair_recv)

    orders = ("xyz", "xyz", "yxz", "yxz", "zyx", "zyx")
    where = {"x": x, "y": y, "z": z}

    def chunk(k, p, t, half):
        return part.at[k, p, lax.rem(t + 4, 4), pl.ds(2 * half, 2)]

    def f32(ref):
        return ref[...].astype(F32)

    def ring_start(k, p):
        axis = orders[p][0]
        t = where[axis]
        after, before = along(axis, 1), along(axis, -1)
        out = ring_send.at[k, p]
        remote(chunk(k, p, t + 2, 0), fwd.at[k, p, 0], (out, ring_recv.at[k, p, 0]), after)
        remote(chunk(k, p, t + 2, 1), fwd.at[k, p, 1], (out, ring_recv.at[k, p, 1]), before)
        remote(chunk(k, p, t + 1, 1), side.at[k, p, 0, pl.ds(2, 2)], (out, ring_recv.at[k, p, 2]), after)
        remote(chunk(k, p, t - 1, 0), side.at[k, p, 1, pl.ds(0, 2)], (out, ring_recv.at[k, p, 2]), before)

    def ring_mid(k, p):
        axis = orders[p][0]
        t = where[axis]
        after, before = along(axis, 1), along(axis, -1)
        sems = (ring_send.at[k, p], ring_recv.at[k, p, 2])
        await_bytes(fwd.at[k, p, 0], ring_recv.at[k, p, 0])
        fsum[k, p, 0] = (f32(fwd.at[k, p, 0]) + f32(chunk(k, p, t + 1, 0))).astype(BF)
        remote(fsum.at[k, p, 0], side.at[k, p, 0, pl.ds(0, 2)], sems, after)
        await_bytes(fwd.at[k, p, 1], ring_recv.at[k, p, 1])
        fsum[k, p, 1] = (f32(fwd.at[k, p, 1]) + f32(chunk(k, p, t - 1, 1))).astype(BF)
        remote(fsum.at[k, p, 1], side.at[k, p, 1, pl.ds(2, 2)], sems, before)

    def plane_copy(k, p, count, step):
        _, second, third = orders[p]
        d2, d3 = step // 4, lax.rem(step, 4)
        held = pl.ds(p % 2, count)
        src = plane_out.at[k, p // 2, lax.rem(where[second] + d2, 4), lax.rem(where[third] + d3, 4), held]
        return pltpu.make_async_remote_copy(
            src_ref=src, dst_ref=plane_in.at[k, p // 2, step, held], send_sem=plane_send.at[k, p],
            recv_sem=plane_recv.at[k, p], device_id=beside(second, d2, third, d3), device_id_type=MESH,
        )

    def plane_start(k, p, count):
        planes.append((k, p, count))

        @pl.loop(1, 16)
        def _(step):
            plane_copy(k, p, count, step).start()

    planes = []

    def plane_bytes(k, p, count):
        return plane_in.at[k, p // 2, pl.ds(1, 15), pl.ds(p % 2, count)]

    def plane_arrive(k, p, count):
        await_bytes(plane_bytes(k, p, count), plane_recv.at[k, p])

    def ring_end(k, p):
        await_bytes(side.at[k, p], ring_recv.at[k, p, 2])
        t = where[orders[p][0]]
        total = f32(part.at[k, p, t]) + f32(side.at[k, p, 0]) + f32(side.at[k, p, 1])
        for s2 in range(4):
            for s3 in range(4):
                if p in (0, 2):
                    rows = (total[s2, 12 * s3 : 12 * s3 + 12], total[s2, 48 + 4 * s3 : 52 + 4 * s3])
                    rows = jnp.concatenate(rows, 0)
                elif p in (4, 5):
                    rows = total[s2, 16 * s3 : 16 * s3 + 16]
                else:
                    rows = [total[s2, 16 * hb + 4 * s3 : 16 * hb + 4 * s3 + 4] for hb in range(4)]
                    rows = jnp.concatenate(rows, 0)
                plane_out[k, p // 2, s2, s3, p % 2] = rows.astype(BF)

    def ring_last(k, p):
        _, second, third = orders[p]
        total = f32(plane_out.at[k, p // 2, where[second], where[third], p % 2])
        for step in range(1, 16):
            total += f32(plane_in.at[k, p // 2, step, p % 2])
        half = p % 2 if p in (4, 5) else p // 2
        lanes = slice(256 * half, 256 * half + 256)
        if p in (0, 2):
            oqkv_ref[:, k, lanes] = total[0:12]
            oproj_ref[k, :, lanes] = total[12:16]
        elif p in (4, 5):
            oup_ref[k, :, lanes] = total
        else:
            for hb in range(4):
                at = slice(hb * C + lanes.start, hb * C + lanes.stop)
                odown_ref[k, :, at] = total[4 * hb : 4 * hb + 4]

    def both(k, name, hi, own, theirs):
        src, dst = cut[name]
        return tn(src[k, :, columns(name, hi, core)], own) + tn(dst[k, hi], theirs)

    def keep(k, p, first, second, rows, g):
        for s in range(2):
            q = p + s if p == 4 else p + 2 * s
            at = (first, second) if orders[q][0] == orders[p][0] else (second, first)
            part[k, q, at[0], at[1], rows, :] = g[:, 256 * s : 256 * s + 256]

    def grads_a(k):
        for name in ("n1", "att", "ep", "eq"):
            take(k, name)
        for hi in range(2):
            g = both(k, "eq", hi, n1[k], pn1[k]).astype(BF)
            for at in range(8):
                keep(k, 0, 2 * hi + at % 2, at // 2, slice(0, 48), g[48 * at : 48 * at + 48])
            g = both(k, "ep", hi, att[k], patt[k]).astype(BF)
            for at in range(8):
                keep(k, 0, 2 * hi + at % 2, at // 2, slice(48, 64), g[16 * at : 16 * at + 16])
        ring_start(k, 0)
        ring_start(k, 2)

    def grads_b(k):
        for name in ("n2", "eu"):
            take(k, name)
        for hi in range(2):
            g = both(k, "eu", hi, n2[k], pn2[k]).astype(BF)
            for at in range(32):
                row = (2 * hi + at // 4 % 2) * 16
                keep(k, 4, at % 4, at // 8, slice(row, row + 16), g[16 * at : 16 * at + 16])
        ring_start(k, 4)
        ring_start(k, 5)

    def grads_c(k):
        for name in ("hs", "ed"):
            take(k, name)
        for hi in range(2):
            for hb in range(4):
                cols = slice(hb * C, hb * C + C)
                g = both(k, "ed", hi, hs[k, :, cols], phs[k, :, cols]).astype(BF)
                for at in range(8):
                    row = 16 * hb
                    keep(k, 1, 2 * hi + at % 2, at // 2, slice(row, row + 16), g[16 * at : 16 * at + 16])
        ring_start(k, 1)
        ring_start(k, 3)

    def exchange(event, forward):
        for q in range(4):
            a, b = q // 2, q % 2
            di, dj = (a - 1, b - 1) if forward else (a, b)
            if (di, dj) == (0, 0):
                recv[event, 3 - q] = send[event, q]
            else:
                sems = (send_sem.at[event], recv_sem.at[event])
                remote(send.at[event, q], recv.at[event, 3 - q], sems, device(di, dj))

    def arrive(event):
        await_bytes(recv.at[event, pl.ds(0, 3)], recv_sem.at[event])

    def put(event, tokens):
        send[event] = tn(tos_ref[...], tokens).astype(BF).reshape(4, SLOT, C)

    def got(event):
        return nn(tos_ref[...], recv[event].reshape(4 * SLOT, C))

    for name in ("up", "son", "tos", "ton"):
        inputs[name].wait()
    send[0] = nn(son_ref[...], up_ref[...].reshape(T, C)).astype(BF).reshape(4, SLOT, C)
    exchange(0, True)

    lane = lax.broadcasted_iota(jnp.int32, (1, 128), 1)
    head_mask = [((lane >= 32 * s) & (lane < 32 * s + 32)).astype(BF) for s in range(4)]
    half_t = lax.broadcasted_iota(jnp.int32, (T, T), 0) < T // 2
    half_s = lax.broadcasted_iota(jnp.int32, (T, T), 1) < T // 2
    one = jnp.where((i == nlat - 1) & (half_t != half_s), 0.0, 1.0).astype(F32)
    for s in range(4):
        seen[T * s : T * s + T] = one
    inside = [(lane >= 32 * s) & (lane < 32 * s + 32) for s in range(4)]
    two = lax.broadcasted_iota(jnp.int32, (128, 128), 1) < 2
    ones_two = jnp.where(two, 1.0, 0.0).astype(BF)
    minus_two = jnp.where(lax.broadcasted_iota(jnp.int32, (T, 128), 1) < 2, -1.0, 0.0).astype(BF)

    def forward(k, x):
        xs[k] = x
        nhat, rstd = norm(x)
        n1h[k] = nhat
        r1[k] = jnp.broadcast_to(rstd, (T, 128))
        n1[k] = nhat.astype(BF)
        give(k, "n1")
        fetches[4 * k].wait()

        for s in range(3):
            cols = slice(s * C, s * C + C)
            us[k, :, cols] = nn(n1[k], wqkv[k, :, cols]).astype(BF)

        for g in range(4):
            def part(w):
                return us[k, :, pl.ds(w * C + g * 128, 128)]

            q, key, v = part(0), part(1), part(2)
            stacked = jnp.concatenate([q * m for m in head_mask], 0)
            e = jnp.exp2(nt(stacked, key) * (32**-0.5 / np.log(2.0)))
            if k == 1:
                e = e * seen[...]
            p = ((e * (1.0 / (0.25 * jnp.sum(e, -1, keepdims=True)))) * 0.25).astype(BF)
            ps[k, g] = p
            out = nn(p, v)
            total = jnp.zeros((T, 128), F32)
            for s in range(4):
                total += jnp.where(inside[s], out[T * s : T * s + T], 0.0)
            att[k, :, pl.ds(g * 128, 128)] = total.astype(BF)

        give(k, "att")
        fetches[4 * k + 1].wait()
        m = xs[k] + nn(att[k], wproj[k])
        acc[...] = m
        nhat, rstd = norm(m)
        n2h[k] = nhat
        r2[k] = jnp.broadcast_to(rstd, (T, 128))
        n2[k] = nhat.astype(BF)
        give(k, "n2")
        fetches[4 * k + 2].wait()
        fetches[4 * k + 3].wait()

        for s in range(4):
            cols = slice(s * C, s * C + C)
            z = nn(n2[k], wup[k, :, cols])
            cdf = 0.5 * (1.0 + lax.erf(z * (2.0**-0.5)))
            gp[k, :, cols] = cdf + z * (jnp.exp(-0.5 * z * z) * ((2.0 * np.pi) ** -0.5))
            h = (z * cdf).astype(BF)
            hs[k, :, cols] = h
            acc[...] += nn(h, wdown[k, cols, :])

        give(k, "hs")
        return acc[...]

    def backward(k, ct, after_up, after_proj, amid):
        acc[...] = ct
        ed[k] = ct.astype(BF)
        give(k, "ed")

        for s in range(4):
            cols = slice(s * C, s * C + C)
            dh = nt(ed[k], wdown[k, cols, :]).astype(BF).astype(F32)
            eu[k, :, cols] = (dh * gp[k, :, cols]).astype(BF)

        give(k, "eu")
        grads_c(k)
        after_up()
        dn2 = nt(eu[k], wup[k]).astype(BF).astype(F32)
        dm = acc[...] + norm_back(dn2, n2h[k], r2[k][:, 0:1])
        acc[...] = dm
        ep[k] = dm.astype(BF)
        give(k, "ep")
        grads_b(k)
        dab[...] = nt(ep[k], wproj[k]).astype(BF)
        after_proj()

        def heads(g):
            def at(w):
                return slice(w * C + g * 128, w * C + g * 128 + 128)

            q, key, v = us[k, :, at(0)], us[k, :, at(1)], us[k, :, at(2)]
            da = dab[:, at(0)]
            prod = da.astype(F32) * att[k, :, at(0)].astype(F32)
            high = prod.astype(BF)
            low = (prod - high.astype(F32)).astype(BF)
            stacked_da = jnp.concatenate([da * m for m in head_mask], 0)
            sums = nn(jnp.concatenate([high * m for m in head_mask], 0), ones_two)
            sums += nn(jnp.concatenate([low * m for m in head_mask], 0), ones_two)
            sums_high = sums.astype(BF).astype(F32)
            sums = jnp.where(lane == 0, sums_high, sums - sums_high).astype(BF)
            p = ps[k, g]
            dp = nt(jnp.concatenate([stacked_da, sums], 1), jnp.concatenate([v, minus_two], 1))
            ds = (p.astype(F32) * dp).astype(BF)
            dv = tn(p, stacked_da)
            dk = tn(ds, jnp.concatenate([q * m for m in head_mask], 0))
            out = nn(ds, key)
            dq = jnp.zeros((T, 128), F32)
            for s in range(4):
                dq += jnp.where(inside[s], out[T * s : T * s + T], 0.0)
            eq[k, :, at(0)] = (dq * (32**-0.5)).astype(BF)
            eq[k, :, at(1)] = (dk * (32**-0.5)).astype(BF)
            eq[k, :, at(2)] = dv.astype(BF)

        for half in range(2):
            for g in range(2 * half, 2 * half + 2):
                heads(g)
            amid(half)
        give(k, "eq")

    def backward_end(k):
        dn1 = nt(eq[k], wqkv[k]).astype(BF).astype(F32)
        return acc[...] + norm_back(dn1, n1h[k], r1[k][:, 0:1])

    def nothing():
        pass

    inputs["swap"].wait()
    lane_finish(0)
    for half in range(2):
        moved = nn(came[half].reshape(64, 1024), swap[...]).astype(BF)
        for lr in range(8 if half == 0 else 4):
            for g in range(4):
                at = (slice(128 * half + 16 * lr, 128 * half + 16 * lr + 16), slice(128 * g, 128 * g + 128))
                nat2[at] = moved[16 * g : 16 * g + 16, 128 * lr : 128 * lr + 128]
    first = forward(0, nn(ton_ref[...], nat2[...]))
    put(1, first.astype(BF))
    exchange(1, True)
    arrive(1)
    second = forward(1, got(1))
    put(2, second.astype(BF))
    exchange(2, False)
    arrive(0)

    def mids(k, parts):
        for p in parts:
            ring_mid(k, p)

    def ends(k, parts):
        for p in parts:
            ring_end(k, p)

    def lasts(k, parts):
        for p in parts:
            ring_last(k, p)

    def amid_one(half):
        if half == 1:
            mids(1, (1, 3))

    backward(1, got(0), nothing, nothing, amid_one)
    d_second = backward_end(1)
    put(3, d_second.astype(BF))
    exchange(3, False)
    grads_a(1)
    mids(1, (4, 5))
    arrive(3)

    def up_zero():
        mids(1, (0, 2))

    def proj_zero():
        ends(1, (1, 3, 4, 5))
        plane_start(1, 4, 2)

    def amid_zero(half):
        if half == 0:
            ends(1, (0, 2))
            plane_start(1, 0, 2)
            plane_start(1, 2, 2)
        else:
            mids(0, (1, 3, 4, 5))

    backward(0, got(3), up_zero, proj_zero, amid_zero)
    grads_a(0)
    d_first = backward_end(0)
    nat2[...] = tn(ton_ref[...], d_first.astype(BF)).astype(BF)
    for half in range(2):
        for lr in range(8):
            for g in range(4):
                at = (slice(16 * g, 16 * g + 16), slice(128 * lr, 128 * lr + 128))
                if half == 1 and lr >= 4:
                    turned[half, at[0], at[1]] = jnp.zeros((16, 128), BF)
                else:
                    row = 128 * half + 16 * lr
                    turned[half, at[0], at[1]] = nat2[row : row + 16, 128 * g : 128 * g + 128]
        moved = nn(turned[half], swap[...]).astype(BF)
        for g in range(4):
            for lane_block in range(8):
                leave2[8 * g + lane_block, half] = moved[
                    16 * g : 16 * g + 16, 128 * lane_block : 128 * lane_block + 128
                ]
    mids(0, (0, 2))
    lane_start(1)
    ends(0, (1, 3))
    plane_start(0, 1, 1)
    plane_start(0, 3, 1)
    ends(0, (4, 5))
    plane_start(0, 4, 2)
    arrive(2)
    natural = tn(son_ref[...], recv[2].reshape(4 * SLOT, C)).astype(BF)
    mixed_ref[...] = natural.reshape(T // LEV, LEV, C)
    stores = []

    def store(src, dst):
        stores.append(pltpu.make_async_copy(src, dst, out_sem.at[len(stores)]))
        stores[-1].start()

    store(mixed_ref, mixed_hbm)
    ends(0, (0, 2))
    plane_start(0, 0, 1)
    plane_start(0, 2, 1)
    for group in (0, 2, 4):
        plane_arrive(1, group, 2)
    lasts(1, range(6))
    plane_arrive(0, 1, 1)
    plane_arrive(0, 3, 1)
    plane_arrive(0, 4, 2)
    lasts(0, (1, 3, 4, 5))
    store(oup_ref, oup_hbm)
    store(odown_ref, odown_hbm)
    lane_finish(1)
    for half in range(2):
        rows = tn(came2[:, half].reshape(512, 128), spread_ref[...]).astype(BF)
        n = 8 if half == 0 else 4
        denc_ref[8 * half : 8 * half + n] = rows[0 : 16 * n].reshape(n, 16, 32 * WLON)
    store(denc_ref, denc_hbm)
    plane_arrive(0, 0, 1)
    plane_arrive(0, 2, 1)
    lasts(0, (0, 2))
    store(oqkv_ref, oqkv_hbm)
    store(oproj_ref, oproj_hbm)
    for event in range(4):
        await_bytes(send.at[event, pl.ds(0, 3)], send_sem.at[event])
    for k in range(2):
        for name in names:
            taken(k, name, pair_send)
        for p in range(6):
            await_bytes(part.at[k, p, pl.ds(0, 3)], ring_send.at[k, p])
    for k, p, count in planes:
        await_bytes(plane_bytes(k, p, count), plane_send.at[k, p])
    for copy in stores:
        copy.wait()


def copies_kernel(*refs):
    for n in range(6):
        refs[6 + n][...] = refs[n][...]


def layers(encoded, upstream, w_qkv, w_proj, w_up, w_down):
    hbm = pl.BlockSpec(memory_space=pl.ANY)
    vmem = pl.BlockSpec(memory_space=pltpu.VMEM)
    dma = pltpu.SemaphoreType.DMA
    V = pltpu.VMEM
    shapes = (
        jax.ShapeDtypeStruct((T // LEV, LEV, C), BF),
        jax.ShapeDtypeStruct((12, 16, 32 * WLON), BF),
        jax.ShapeDtypeStruct((12, 2, C), F32),
        jax.ShapeDtypeStruct((2, 4, C), F32),
        jax.ShapeDtypeStruct((2, 16, C), F32),
        jax.ShapeDtypeStruct((2, 4, FF), F32),
    )
    results = pl.pallas_call(
        layers_kernel,
        out_shape=shapes,
        in_specs=[hbm] * 11,
        out_specs=(hbm,) * 6,
        scratch_shapes=[
            V((12, 16, 32 * WLON), BF), V((T // LEV, LEV, C), BF), V((4 * SLOT, T), BF), V((T, 4 * SLOT), BF),
            V((T, 12 * 16), BF), V((512, 32 * WLON), BF), dma((7,)),
            *[V(shape.shape, shape.dtype) for shape in shapes], dma((6,)),
            V((2, C, 3 * C), BF), V((2, C, C), BF), V((2, C, FF), BF), V((2, FF, C), BF),
            dma((2, 4)),
            V((1024, 1024), BF), V((32, 2, 16, 128), BF), V((2, 4, 16, 1024), BF),
            V((32, 2, 16, 128), BF), V((32, 2, 16, 128), BF), dma((2,)), dma((2,)),
            V((12 * 16, C), BF), V((2, 64, 1024), BF),
            V((4, 4, SLOT, C), BF), V((4, 4, SLOT, C), BF),
            dma((4,)), dma((4,)),
            V((2, T, C), F32), V((2, T, C), F32), V((2, T, C), BF), V((2, T, 128), F32),
            V((2, T, 3 * C), BF), V((2, 4, 4 * T, T), BF), V((2, T, C), BF),
            V((4 * T, T), F32),
            V((2, T, C), F32), V((2, T, C), BF), V((2, T, 128), F32),
            V((2, T, FF), F32), V((2, T, FF), BF), V((T, C), F32),
            V((2, T, 3 * C), BF), V((2, T, C), BF), V((2, T, FF), BF), V((2, T, C), BF), V((T, C), BF),
            V((2, T, C), BF), V((2, T, C), BF), V((2, T, C), BF), V((2, T, FF), BF),
            V((2, 2, T, 384), BF), V((2, 2, T, 128), BF), V((2, 2, T, 512), BF), V((2, 2, T, 128), BF),
            dma((2, 8)), dma((2, 8)),
            V((2, 6, 4, 4, 64, 256), BF), V((2, 6, 2, 2, 64, 256), BF), V((2, 6, 2, 2, 64, 256), BF),
            V((2, 6, 2, 4, 64, 256), BF), V((2, 3, 4, 4, 2, 16, 256), BF), V((2, 3, 16, 2, 16, 256), BF),
            dma((2, 6)), dma((2, 6, 3)), dma((2, 6)), dma((2, 6)),
        ],
        compiler_params=pltpu.CompilerParams(
            collective_id=0, has_side_effects=True, vmem_limit_bytes=60 * 2**20
        ),
    )(encoded, upstream, *permutations(), w_qkv, w_proj, w_up, w_down)
    return pl.pallas_call(
        copies_kernel,
        out_shape=shapes,
        in_specs=[vmem] * 6,
        out_specs=(vmem,) * 6,
    )(*results)


def on_device(encoded, upstream, w_qkv, w_proj, w_up, w_down):
    mixed, dencoded, qkv, proj, up, down = layers(
        encoded.reshape(12, 16, 32 * WLON),
        upstream.transpose(1, 2, 0, 3).reshape(T // LEV, LEV, C),
        w_qkv, w_proj, w_up, w_down,
    )
    return (
        mixed.reshape(WLAT, WLON, LEV, C).transpose(2, 0, 1, 3),
        dencoded.reshape(encoded.shape),
        qkv.transpose(1, 2, 0),
        proj.swapaxes(1, 2),
        up.swapaxes(1, 2),
        down.swapaxes(1, 2),
    )


def solution(mesh):
    return jax.shard_map(
        on_device,
        mesh=mesh,
        in_specs=(P(None, "lat", "lon", None), P(None, "lat", "lon", None), P(), P(), P(), P()),
        out_specs=(
            P(None, "lat", "lon", None),
            P(None, "lat", "lon", None),
            P(None, None, ("lat", "lon")),
            P(None, None, ("lat", "lon")),
            P(None, None, ("lat", "lon")),
            P(None, None, ("lat", "lon")),
        ),
        check_vma=False,
    )
```

```python
import functools

import jax
import jax.numpy as jnp
import numpy as np
from jax import lax
from jax.experimental import pallas as pl
from jax.experimental.pallas import tpu as pltpu
from jax.sharding import PartitionSpec as P

HEADS = 16
WLAT = 6
WLON = 12
LEV = 2
C = 512
FF = 2048
T = LEV * WLAT * WLON
QUAD = T // 4
SLOT = 48
NORM_EPS = 1e-05
MESH = pl.DeviceIdType.MESH
BF = jnp.bfloat16
F32 = jnp.float32


def quadrant_order():
    return [
        (l, 3 * a + r, 6 * b + c)
        for a in range(2)
        for b in range(2)
        for l in range(LEV)
        for r in range(3)
        for c in range(6)
    ]


def permutations():
    slots_of_natural = np.zeros((4 * SLOT, T), np.float32)
    tokens_of_slots = np.zeros((T, 4 * SLOT), np.float32)
    tokens_of_padded = np.zeros((T, 12 * 16), np.float32)
    for t, (l, r, c) in enumerate(quadrant_order()):
        slot = t // QUAD * SLOT + t % QUAD
        slots_of_natural[slot, (r * WLON + c) * LEV + l] = 1
        tokens_of_slots[t, slot] = 1
        tokens_of_padded[t, (l * WLAT + r) * 16 + c] = 1
    spread = np.zeros((32 * 16, 32 * WLON), np.float32)
    for col in range(32 * WLON):
        spread[col // WLON * 16 + col % WLON, col] = 1
    swap = np.eye(1024, dtype=np.float32).reshape(8, 8, 16, 1024).swapaxes(0, 1).reshape(1024, 1024)
    matrices = (slots_of_natural, tokens_of_slots, tokens_of_padded, spread, swap)
    return [jnp.asarray(m, BF) for m in matrices]


def nn(a, b):
    return lax.dot_general(a, b, (((1,), (0,)), ((), ())), preferred_element_type=F32)


def nt(a, b):
    return lax.dot_general(a, b, (((1,), (1,)), ((), ())), preferred_element_type=F32)


def tn(a, b):
    return lax.dot_general(a, b, (((0,), (0,)), ((), ())), preferred_element_type=F32)


def norm(x):
    centred = x - jnp.mean(x, -1, keepdims=True)
    rstd = lax.rsqrt(jnp.mean(centred * centred, -1, keepdims=True) + NORM_EPS)
    return centred * rstd, rstd


def norm_back(dn, nhat, rstd):
    return rstd * (
        dn - jnp.mean(dn, -1, keepdims=True) - nhat * jnp.mean(dn * nhat, -1, keepdims=True)
    )


def layers_kernel(
    enc_hbm, up_hbm, son_hbm, tos_hbm, ton_hbm, spread_hbm, swap_hbm,
    wqkv_hbm, wproj_hbm, wup_hbm, wdown_hbm,
    mixed_hbm, denc_hbm, oqkv_hbm, oproj_hbm, oup_hbm, odown_hbm,
    enc_ref, up_ref, son_ref, tos_ref, ton_ref, spread_ref, in_sem,
    mixed_ref, denc_ref, oqkv_ref, oproj_ref, oup_ref, odown_ref, out_sem,
    wqkv, wproj, wup, wdown, wsem,
    swap, leave, came, leave2, came2, lane_send, lane_recv, nat2, turned, send, recv, send_sem, recv_sem,
    xs, n1h, n1, r1, us, ps, att, seen, n2h, n2, r2, gp, hs, acc, eq, ep, eu, ed, dab,
    pn1, patt, pn2, phs, peq, pep, peu, ped, pair_send, pair_recv,
    part, fwd, fsum, side, plane_out, plane_in, ring_send, ring_recv, plane_send, plane_recv,
):
    i, j = lax.axis_index("lat"), lax.axis_index("lon")
    nlat, nlon = lax.axis_size("lat"), lax.axis_size("lon")

    def device(di, dj):
        return (lax.rem(i + di + nlat, nlat), lax.rem(j + dj + nlon, nlon))

    core, z, y = lax.rem(i, 2), lax.rem(j, 4), j // 8
    x = i // 2 * 2 + lax.rem(j // 4, 2)

    def along(axis, steps):
        at = {"x": x, "y": y, "z": z}
        at[axis] = lax.rem(at[axis] + steps + 4, 4)
        return (at["x"] // 2 * 2 + core, at["y"] * 8 + lax.rem(at["x"], 2) * 4 + at["z"])

    def beside(axis, steps, other, others):
        at = {"x": x, "y": y, "z": z}
        at[axis] = lax.rem(at[axis] + steps + 4, 4)
        at[other] = lax.rem(at[other] + others + 4, 4)
        return (at["x"] // 2 * 2 + core, at["y"] * 8 + lax.rem(at["x"], 2) * 4 + at["z"])

    partner = (i + 1 - 2 * core, j)

    weights = ((wqkv_hbm, wqkv), (wproj_hbm, wproj), (wup_hbm, wup), (wdown_hbm, wdown))
    inputs = {}
    for at, (name, src, dst) in enumerate(
        (
            ("enc", enc_hbm, enc_ref), ("spread", spread_hbm, spread_ref), ("up", up_hbm, up_ref),
            ("son", son_hbm, son_ref), ("tos", tos_hbm, tos_ref), ("ton", ton_hbm, ton_ref),
            ("swap", swap_hbm, swap),
        )
    ):
        inputs[name] = pltpu.make_async_copy(src, dst, in_sem.at[at])
    inputs["enc"].start()
    inputs["spread"].start()
    fetches = [
        pltpu.make_async_copy(src.at[k], dst.at[k], wsem.at[k, w]) for k in range(2) for w, (src, dst) in enumerate(weights)
    ]

    barrier = pltpu.get_barrier_semaphore()
    far = lambda xl, dy, dz: (lax.rem(i + 2, 4), lax.rem(y + dy, 4) * 8 + xl * 4 + lax.rem(z + dz, 4))
    greeted = [device(1, 0), device(-1, 0), device(1, 1), device(-1, -1)]
    greeted += [far(xl, 0, dz) for xl in range(2) for dz in range(4)]
    greeted += [far(xl, dy, 0) for xl in range(2) for dy in (1, 2, 3)]
    for other in greeted:
        pl.semaphore_signal(barrier, inc=1, device_id=other, device_id_type=MESH)

    for step in range(1, nlon):
        pl.semaphore_signal(barrier, inc=1, device_id=device(0, step), device_id_type=MESH)

    for name in ("up", "son", "tos", "ton", "swap"):
        inputs[name].start()
    for fetch in fetches:
        fetch.start()

    inputs["enc"].wait()
    inputs["spread"].wait()
    columns_first = nt(spread_ref[...], enc_ref[...].reshape(12 * 16, 32 * WLON)).astype(BF)
    leave[:, 0] = columns_first[:, 0:128].reshape(32, 16, 128)
    leave[:, 1, :, 0:64] = columns_first[:, 128:192].reshape(32, 16, 64)
    leave[:, 1, :, 64:128] = jnp.zeros((32, 16, 64), BF)
    pl.semaphore_wait(barrier, len(greeted) + nlon - 1)
    mine = pl.ds(pl.multiple_of(lax.rem(j, 8) * 128, 128), 128)

    def lane_copy(step, event):
        to = lax.rem(j + step, nlon)
        if event == 0:
            src, dst = leave.at[to], came.at[:, j // 8, :, mine]
        else:
            src, dst = leave2.at[to], came2.at[j]
        return pltpu.make_async_remote_copy(
            src_ref=src, dst_ref=dst, send_sem=lane_send.at[event], recv_sem=lane_recv.at[event],
            device_id=(i, to), device_id_type=MESH,
        )

    def lane_start(event):
        for step in range(1, nlon):
            lane_copy(step, event).start()

        if event == 0:
            src, dst = leave.at[j], came.at[:, j // 8, :, mine]
        else:
            src, dst = leave2.at[j], came2.at[j]
        pltpu.make_async_copy(src, dst, lane_recv.at[event]).start()

    def lane_finish(event):
        await_bytes((came, came2)[event], lane_recv.at[event])
        await_bytes((leave, leave2)[event].at[pl.ds(0, 31)], lane_send.at[event])

    lane_start(0)

    def remote(src, dst, sems, to):
        pltpu.make_async_remote_copy(
            src_ref=src, dst_ref=dst, send_sem=sems[0], recv_sem=sems[1], device_id=to, device_id_type=MESH
        ).start()

    def await_bytes(like, sem):
        pltpu.make_async_copy(like, like, sem).wait()

    wide = {"eq": 384, "ep": 128, "eu": 512, "ed": 128}
    whole = {"n1": (n1, pn1), "att": (att, patt), "n2": (n2, pn2), "hs": (hs, phs)}
    cut = {"eq": (eq, peq), "ep": (ep, pep), "eu": (eu, peu), "ed": (ed, ped)}

    def columns(name, hi, owner):
        width = wide[name]
        return pl.ds(pl.multiple_of((2 * hi + owner) * width, width), width)

    names = ("n1", "att", "n2", "hs", "eq", "ep", "eu", "ed")

    def give(k, name):
        sems = (pair_send.at[k, names.index(name)], pair_recv.at[k, names.index(name)])
        if name in whole:
            src, dst = whole[name]
            remote(src.at[k], dst.at[k], sems, partner)
        else:
            src, dst = cut[name]
            for hi in range(2):
                remote(src.at[k, :, columns(name, hi, 1 - core)], dst.at[k, hi], sems, partner)

    def taken(k, name, sems):
        dst = (whole[name] if name in whole else cut[name])[1]
        await_bytes(dst.at[k], sems.at[k, names.index(name)])

    def take(k, name):
        taken(k, name, pair_recv)

    orders = ("xyz", "xyz", "yxz", "yxz", "zyx", "zyx")
    where = {"x": x, "y": y, "z": z}

    def chunk(k, p, t, half):
        return part.at[k, p, lax.rem(t + 4, 4), pl.ds(2 * half, 2)]

    def f32(ref):
        return ref[...].astype(F32)

    def ring_start(k, p):
        axis = orders[p][0]
        t = where[axis]
        after, before = along(axis, 1), along(axis, -1)
        out = ring_send.at[k, p]
        remote(chunk(k, p, t + 2, 0), fwd.at[k, p, 0], (out, ring_recv.at[k, p, 0]), after)
        remote(chunk(k, p, t + 2, 1), fwd.at[k, p, 1], (out, ring_recv.at[k, p, 1]), before)
        remote(chunk(k, p, t + 1, 1), side.at[k, p, 0, pl.ds(2, 2)], (out, ring_recv.at[k, p, 2]), after)
        remote(chunk(k, p, t - 1, 0), side.at[k, p, 1, pl.ds(0, 2)], (out, ring_recv.at[k, p, 2]), before)

    def ring_mid(k, p):
        axis = orders[p][0]
        t = where[axis]
        after, before = along(axis, 1), along(axis, -1)
        sems = (ring_send.at[k, p], ring_recv.at[k, p, 2])
        await_bytes(fwd.at[k, p, 0], ring_recv.at[k, p, 0])
        fsum[k, p, 0] = (f32(fwd.at[k, p, 0]) + f32(chunk(k, p, t + 1, 0))).astype(BF)
        remote(fsum.at[k, p, 0], side.at[k, p, 0, pl.ds(0, 2)], sems, after)
        await_bytes(fwd.at[k, p, 1], ring_recv.at[k, p, 1])
        fsum[k, p, 1] = (f32(fwd.at[k, p, 1]) + f32(chunk(k, p, t - 1, 1))).astype(BF)
        remote(fsum.at[k, p, 1], side.at[k, p, 1, pl.ds(2, 2)], sems, before)

    def plane_copy(k, p, count, step):
        _, second, third = orders[p]
        d2, d3 = divmod(step, 4)
        held = pl.ds(p % 2, count)
        src = plane_out.at[k, p // 2, lax.rem(where[second] + d2, 4), lax.rem(where[third] + d3, 4), held]
        return pltpu.make_async_remote_copy(
            src_ref=src, dst_ref=plane_in.at[k, p // 2, step, held], send_sem=plane_send.at[k, p],
            recv_sem=plane_recv.at[k, p], device_id=beside(second, d2, third, d3), device_id_type=MESH,
        )

    def plane_start(k, p, count):
        planes.append((k, p, count))

        for step in range(1, 16):
            plane_copy(k, p, count, step).start()

    planes = []

    def plane_bytes(k, p, count):
        return plane_in.at[k, p // 2, pl.ds(1, 15), pl.ds(p % 2, count)]

    def plane_arrive(k, p, count):
        await_bytes(plane_bytes(k, p, count), plane_recv.at[k, p])

    def ring_end(k, p):
        await_bytes(side.at[k, p], ring_recv.at[k, p, 2])
        t = where[orders[p][0]]
        total = f32(part.at[k, p, t]) + f32(side.at[k, p, 0]) + f32(side.at[k, p, 1])
        for s2 in range(4):
            for s3 in range(4):
                if p in (0, 2):
                    rows = (total[s2, 12 * s3 : 12 * s3 + 12], total[s2, 48 + 4 * s3 : 52 + 4 * s3])
                    rows = jnp.concatenate(rows, 0)
                elif p in (4, 5):
                    rows = total[s2, 16 * s3 : 16 * s3 + 16]
                else:
                    rows = [total[s2, 16 * hb + 4 * s3 : 16 * hb + 4 * s3 + 4] for hb in range(4)]
                    rows = jnp.concatenate(rows, 0)
                plane_out[k, p // 2, s2, s3, p % 2] = rows.astype(BF)

    def ring_last(k, p):
        _, second, third = orders[p]
        total = f32(plane_out.at[k, p // 2, where[second], where[third], p % 2])
        for step in range(1, 16):
            total += f32(plane_in.at[k, p // 2, step, p % 2])
        half = p % 2 if p in (4, 5) else p // 2
        lanes = slice(256 * half, 256 * half + 256)
        if p in (0, 2):
            oqkv_ref[:, k, lanes] = total[0:12]
            oproj_ref[k, :, lanes] = total[12:16]
        elif p in (4, 5):
            oup_ref[k, :, lanes] = total
        else:
            for hb in range(4):
                at = slice(hb * C + lanes.start, hb * C + lanes.stop)
                odown_ref[k, :, at] = total[4 * hb : 4 * hb + 4]

    def both(k, name, hi, own, theirs):
        src, dst = cut[name]
        return tn(src[k, :, columns(name, hi, core)], own) + tn(dst[k, hi], theirs)

    def keep(k, p, first, second, rows, g):
        for s in range(2):
            q = p + s if p == 4 else p + 2 * s
            at = (first, second) if orders[q][0] == orders[p][0] else (second, first)
            part[k, q, at[0], at[1], rows, :] = g[:, 256 * s : 256 * s + 256]

    def grads_a(k):
        for name in ("n1", "att", "ep", "eq"):
            take(k, name)
        for hi in range(2):
            g = both(k, "eq", hi, n1[k], pn1[k]).astype(BF)
            for at in range(8):
                keep(k, 0, 2 * hi + at % 2, at // 2, slice(0, 48), g[48 * at : 48 * at + 48])
            g = both(k, "ep", hi, att[k], patt[k]).astype(BF)
            for at in range(8):
                keep(k, 0, 2 * hi + at % 2, at // 2, slice(48, 64), g[16 * at : 16 * at + 16])
        ring_start(k, 0)
        ring_start(k, 2)

    def grads_b(k):
        for name in ("n2", "eu"):
            take(k, name)
        for hi in range(2):
            g = both(k, "eu", hi, n2[k], pn2[k]).astype(BF)
            for at in range(32):
                row = (2 * hi + at // 4 % 2) * 16
                keep(k, 4, at % 4, at // 8, slice(row, row + 16), g[16 * at : 16 * at + 16])
        ring_start(k, 4)
        ring_start(k, 5)

    def grads_c(k):
        for name in ("hs", "ed"):
            take(k, name)
        for hi in range(2):
            for hb in range(4):
                cols = slice(hb * C, hb * C + C)
                g = both(k, "ed", hi, hs[k, :, cols], phs[k, :, cols]).astype(BF)
                for at in range(8):
                    row = 16 * hb
                    keep(k, 1, 2 * hi + at % 2, at // 2, slice(row, row + 16), g[16 * at : 16 * at + 16])
        ring_start(k, 1)
        ring_start(k, 3)

    def exchange(event, forward):
        for q in range(4):
            a, b = q // 2, q % 2
            di, dj = (a - 1, b - 1) if forward else (a, b)
            if (di, dj) == (0, 0):
                recv[event, 3 - q] = send[event, q]
            else:
                sems = (send_sem.at[event], recv_sem.at[event])
                remote(send.at[event, q], recv.at[event, 3 - q], sems, device(di, dj))

    def arrive(event):
        await_bytes(recv.at[event, pl.ds(0, 3)], recv_sem.at[event])

    def put(event, tokens):
        send[event] = tn(tos_ref[...], tokens).astype(BF).reshape(4, SLOT, C)

    def got(event):
        return nn(tos_ref[...], recv[event].reshape(4 * SLOT, C))

    for name in ("up", "son", "tos", "ton"):
        inputs[name].wait()
    send[0] = nn(son_ref[...], up_ref[...].reshape(T, C)).astype(BF).reshape(4, SLOT, C)
    exchange(0, True)

    lane = lax.broadcasted_iota(jnp.int32, (1, 128), 1)
    head_mask = [((lane >= 32 * s) & (lane < 32 * s + 32)).astype(BF) for s in range(4)]
    half_t = lax.broadcasted_iota(jnp.int32, (T, T), 0) < T // 2
    half_s = lax.broadcasted_iota(jnp.int32, (T, T), 1) < T // 2
    one = jnp.where((i == nlat - 1) & (half_t != half_s), 0.0, 1.0).astype(F32)
    for s in range(4):
        seen[T * s : T * s + T] = one
    inside = [(lane >= 32 * s) & (lane < 32 * s + 32) for s in range(4)]
    two = lax.broadcasted_iota(jnp.int32, (128, 128), 1) < 2
    ones_two = jnp.where(two, 1.0, 0.0).astype(BF)
    minus_two = jnp.where(lax.broadcasted_iota(jnp.int32, (T, 128), 1) < 2, -1.0, 0.0).astype(BF)

    def forward(k, x):
        xs[k] = x
        nhat, rstd = norm(x)
        n1h[k] = nhat
        r1[k] = jnp.broadcast_to(rstd, (T, 128))
        n1[k] = nhat.astype(BF)
        give(k, "n1")
        fetches[4 * k].wait()

        for s in range(3):
            cols = slice(s * C, s * C + C)
            us[k, :, cols] = nn(n1[k], wqkv[k, :, cols]).astype(BF)

        for g in range(4):
            def part(w):
                return us[k, :, pl.ds(w * C + g * 128, 128)]

            q, key, v = part(0), part(1), part(2)
            stacked = jnp.concatenate([q * m for m in head_mask], 0)
            e = jnp.exp2(nt(stacked, key) * (32**-0.5 / np.log(2.0)))
            if k == 1:
                e = e * seen[...]
            p = ((e * (1.0 / (0.25 * jnp.sum(e, -1, keepdims=True)))) * 0.25).astype(BF)
            ps[k, g] = p
            out = nn(p, v)
            total = jnp.zeros((T, 128), F32)
            for s in range(4):
                total += jnp.where(inside[s], out[T * s : T * s + T], 0.0)
            att[k, :, pl.ds(g * 128, 128)] = total.astype(BF)

        give(k, "att")
        fetches[4 * k + 1].wait()
        m = xs[k] + nn(att[k], wproj[k])
        acc[...] = m
        nhat, rstd = norm(m)
        n2h[k] = nhat
        r2[k] = jnp.broadcast_to(rstd, (T, 128))
        n2[k] = nhat.astype(BF)
        give(k, "n2")
        fetches[4 * k + 2].wait()
        fetches[4 * k + 3].wait()

        for s in range(4):
            cols = slice(s * C, s * C + C)
            z = nn(n2[k], wup[k, :, cols])
            cdf = 0.5 * (1.0 + lax.erf(z * (2.0**-0.5)))
            gp[k, :, cols] = cdf + z * (jnp.exp(-0.5 * z * z) * ((2.0 * np.pi) ** -0.5))
            h = (z * cdf).astype(BF)
            hs[k, :, cols] = h
            acc[...] += nn(h, wdown[k, cols, :])

        give(k, "hs")
        return acc[...]

    def backward(k, ct, after_up, after_proj, amid):
        acc[...] = ct
        ed[k] = ct.astype(BF)
        give(k, "ed")

        for s in range(4):
            cols = slice(s * C, s * C + C)
            dh = nt(ed[k], wdown[k, cols, :]).astype(BF).astype(F32)
            eu[k, :, cols] = (dh * gp[k, :, cols]).astype(BF)

        give(k, "eu")
        grads_c(k)
        after_up()
        dn2 = nt(eu[k], wup[k]).astype(BF).astype(F32)
        dm = acc[...] + norm_back(dn2, n2h[k], r2[k][:, 0:1])
        acc[...] = dm
        ep[k] = dm.astype(BF)
        give(k, "ep")
        grads_b(k)
        dab[...] = nt(ep[k], wproj[k]).astype(BF)
        after_proj()

        def heads(g):
            def at(w):
                return slice(w * C + g * 128, w * C + g * 128 + 128)

            q, key, v = us[k, :, at(0)], us[k, :, at(1)], us[k, :, at(2)]
            da = dab[:, at(0)]
            prod = da.astype(F32) * att[k, :, at(0)].astype(F32)
            high = prod.astype(BF)
            low = (prod - high.astype(F32)).astype(BF)
            stacked_da = jnp.concatenate([da * m for m in head_mask], 0)
            sums = nn(jnp.concatenate([high * m for m in head_mask], 0), ones_two)
            sums += nn(jnp.concatenate([low * m for m in head_mask], 0), ones_two)
            sums_high = sums.astype(BF).astype(F32)
            sums = jnp.where(lane == 0, sums_high, sums - sums_high).astype(BF)
            p = ps[k, g]
            dp = nt(jnp.concatenate([stacked_da, sums], 1), jnp.concatenate([v, minus_two], 1))
            ds = (p.astype(F32) * dp).astype(BF)
            dv = tn(p, stacked_da)
            dk = tn(ds, jnp.concatenate([q * m for m in head_mask], 0))
            out = nn(ds, key)
            dq = jnp.zeros((T, 128), F32)
            for s in range(4):
                dq += jnp.where(inside[s], out[T * s : T * s + T], 0.0)
            eq[k, :, at(0)] = (dq * (32**-0.5)).astype(BF)
            eq[k, :, at(1)] = (dk * (32**-0.5)).astype(BF)
            eq[k, :, at(2)] = dv.astype(BF)

        for half in range(2):
            for g in range(2 * half, 2 * half + 2):
                heads(g)
            amid(half)
        give(k, "eq")

    def backward_end(k):
        dn1 = nt(eq[k], wqkv[k]).astype(BF).astype(F32)
        return acc[...] + norm_back(dn1, n1h[k], r1[k][:, 0:1])

    def nothing():
        pass

    inputs["swap"].wait()
    lane_finish(0)
    for half in range(2):
        moved = nn(came[half].reshape(64, 1024), swap[:, 0 : 1024 - 512 * half]).astype(BF)
        for lr in range(8 if half == 0 else 4):
            for g in range(4):
                at = (slice(128 * half + 16 * lr, 128 * half + 16 * lr + 16), slice(128 * g, 128 * g + 128))
                nat2[at] = moved[16 * g : 16 * g + 16, 128 * lr : 128 * lr + 128]
    first = forward(0, nn(ton_ref[...], nat2[...]))
    put(1, first.astype(BF))
    exchange(1, True)
    arrive(1)
    second = forward(1, got(1))
    put(2, second.astype(BF))
    exchange(2, False)
    arrive(0)

    def mids(k, parts):
        for p in parts:
            ring_mid(k, p)

    def ends(k, parts):
        for p in parts:
            ring_end(k, p)

    def lasts(k, parts):
        for p in parts:
            ring_last(k, p)

    def amid_one(half):
        if half == 1:
            mids(1, (1, 3))

    backward(1, got(0), nothing, nothing, amid_one)
    d_second = backward_end(1)
    put(3, d_second.astype(BF))
    exchange(3, False)
    grads_a(1)
    mids(1, (4, 5))
    arrive(3)

    def up_zero():
        mids(1, (0, 2))

    def proj_zero():
        ends(1, (1, 3, 4, 5))
        plane_start(1, 4, 2)

    def amid_zero(half):
        if half == 0:
            ends(1, (0, 2))
            plane_start(1, 0, 2)
            plane_start(1, 2, 2)
            mids(0, (1, 3))
        else:
            mids(0, (4, 5))

    backward(0, got(3), up_zero, proj_zero, amid_zero)
    grads_a(0)
    d_first = backward_end(0)
    nat2[...] = tn(ton_ref[...], d_first.astype(BF)).astype(BF)
    for half in range(2):
        for lr in range(8 if half == 0 else 4):
            for g in range(4):
                at = (slice(16 * g, 16 * g + 16), slice(128 * lr, 128 * lr + 128))
                row = 128 * half + 16 * lr
                turned[half, at[0], at[1]] = nat2[row : row + 16, 128 * g : 128 * g + 128]
        moved = nn(turned[half, :, 0 : 1024 - 512 * half], swap[0 : 1024 - 512 * half]).astype(BF)
        for g in range(4):
            for lane_block in range(8):
                leave2[8 * g + lane_block, half] = moved[
                    16 * g : 16 * g + 16, 128 * lane_block : 128 * lane_block + 128
                ]
    mids(0, (0, 2))
    lane_start(1)
    ends(0, (1, 3))
    plane_start(0, 1, 1)
    plane_start(0, 3, 1)
    ends(0, (4, 5))
    plane_start(0, 4, 2)
    arrive(2)
    natural = tn(son_ref[...], recv[2].reshape(4 * SLOT, C)).astype(BF)
    mixed_ref[...] = natural.reshape(T // LEV, LEV, C)
    stores = []

    def store(src, dst):
        stores.append(pltpu.make_async_copy(src, dst, out_sem.at[len(stores)]))
        stores[-1].start()

    store(mixed_ref, mixed_hbm)
    ends(0, (0, 2))
    plane_start(0, 0, 1)
    plane_start(0, 2, 1)
    for group in (0, 2, 4):
        plane_arrive(1, group, 2)
    lasts(1, range(6))
    plane_arrive(0, 1, 1)
    plane_arrive(0, 3, 1)
    plane_arrive(0, 4, 2)
    lasts(0, (1, 3, 4, 5))
    store(oup_ref, oup_hbm)
    store(odown_ref, odown_hbm)
    lane_finish(1)
    for half in range(2):
        rows = tn(came2[:, half].reshape(512, 128), spread_ref[...]).astype(BF)
        n = 8 if half == 0 else 4
        denc_ref[8 * half : 8 * half + n] = rows[0 : 16 * n].reshape(n, 16, 32 * WLON)
    store(denc_ref, denc_hbm)
    plane_arrive(0, 0, 1)
    plane_arrive(0, 2, 1)
    lasts(0, (0, 2))
    store(oqkv_ref, oqkv_hbm)
    store(oproj_ref, oproj_hbm)
    for event in range(4):
        await_bytes(send.at[event, pl.ds(0, 3)], send_sem.at[event])
    for k in range(2):
        for name in names:
            taken(k, name, pair_send)
        for p in range(6):
            await_bytes(part.at[k, p, pl.ds(0, 3)], ring_send.at[k, p])
    for k, p, count in planes:
        await_bytes(plane_bytes(k, p, count), plane_send.at[k, p])
    for copy in stores:
        copy.wait()


def copies_kernel(*refs):
    for n in range(6):
        refs[6 + n][...] = refs[n][...]


def layers(encoded, upstream, w_qkv, w_proj, w_up, w_down):
    hbm = pl.BlockSpec(memory_space=pl.ANY)
    vmem = pl.BlockSpec(memory_space=pltpu.VMEM)
    dma = pltpu.SemaphoreType.DMA
    V = pltpu.VMEM
    shapes = (
        jax.ShapeDtypeStruct((T // LEV, LEV, C), BF),
        jax.ShapeDtypeStruct((12, 16, 32 * WLON), BF),
        jax.ShapeDtypeStruct((12, 2, C), F32),
        jax.ShapeDtypeStruct((2, 4, C), F32),
        jax.ShapeDtypeStruct((2, 16, C), F32),
        jax.ShapeDtypeStruct((2, 4, FF), F32),
    )
    results = pl.pallas_call(
        layers_kernel,
        out_shape=shapes,
        in_specs=[hbm] * 11,
        out_specs=(hbm,) * 6,
        scratch_shapes=[
            V((12, 16, 32 * WLON), BF), V((T // LEV, LEV, C), BF), V((4 * SLOT, T), BF), V((T, 4 * SLOT), BF),
            V((T, 12 * 16), BF), V((512, 32 * WLON), BF), dma((7,)),
            *[V(shape.shape, shape.dtype) for shape in shapes], dma((6,)),
            V((2, C, 3 * C), BF), V((2, C, C), BF), V((2, C, FF), BF), V((2, FF, C), BF),
            dma((2, 4)),
            V((1024, 1024), BF), V((32, 2, 16, 128), BF), V((2, 4, 16, 1024), BF),
            V((32, 2, 16, 128), BF), V((32, 2, 16, 128), BF), dma((2,)), dma((2,)),
            V((12 * 16, C), BF), V((2, 64, 1024), BF),
            V((4, 4, SLOT, C), BF), V((4, 4, SLOT, C), BF),
            dma((4,)), dma((4,)),
            V((2, T, C), F32), V((2, T, C), F32), V((2, T, C), BF), V((2, T, 128), F32),
            V((2, T, 3 * C), BF), V((2, 4, 4 * T, T), BF), V((2, T, C), BF),
            V((4 * T, T), F32),
            V((2, T, C), F32), V((2, T, C), BF), V((2, T, 128), F32),
            V((2, T, FF), F32), V((2, T, FF), BF), V((T, C), F32),
            V((2, T, 3 * C), BF), V((2, T, C), BF), V((2, T, FF), BF), V((2, T, C), BF), V((T, C), BF),
            V((2, T, C), BF), V((2, T, C), BF), V((2, T, C), BF), V((2, T, FF), BF),
            V((2, 2, T, 384), BF), V((2, 2, T, 128), BF), V((2, 2, T, 512), BF), V((2, 2, T, 128), BF),
            dma((2, 8)), dma((2, 8)),
            V((2, 6, 4, 4, 64, 256), BF), V((2, 6, 2, 2, 64, 256), BF), V((2, 6, 2, 2, 64, 256), BF),
            V((2, 6, 2, 4, 64, 256), BF), V((2, 3, 4, 4, 2, 16, 256), BF), V((2, 3, 16, 2, 16, 256), BF),
            dma((2, 6)), dma((2, 6, 3)), dma((2, 6)), dma((2, 6)),
        ],
        compiler_params=pltpu.CompilerParams(
            collective_id=0, has_side_effects=True, vmem_limit_bytes=60 * 2**20
        ),
    )(encoded, upstream, *permutations(), w_qkv, w_proj, w_up, w_down)
    return pl.pallas_call(
        copies_kernel,
        out_shape=shapes,
        in_specs=[vmem] * 6,
        out_specs=(vmem,) * 6,
    )(*results)


def on_device(encoded, upstream, w_qkv, w_proj, w_up, w_down):
    mixed, dencoded, qkv, proj, up, down = layers(
        encoded.reshape(12, 16, 32 * WLON),
        upstream.transpose(1, 2, 0, 3).reshape(T // LEV, LEV, C),
        w_qkv, w_proj, w_up, w_down,
    )
    return (
        mixed.reshape(WLAT, WLON, LEV, C).transpose(2, 0, 1, 3),
        dencoded.reshape(encoded.shape),
        qkv.transpose(1, 2, 0),
        proj.swapaxes(1, 2),
        up.swapaxes(1, 2),
        down.swapaxes(1, 2),
    )


def solution(mesh):
    return jax.shard_map(
        on_device,
        mesh=mesh,
        in_specs=(P(None, "lat", "lon", None), P(None, "lat", "lon", None), P(), P(), P(), P()),
        out_specs=(
            P(None, "lat", "lon", None),
            P(None, "lat", "lon", None),
            P(None, None, ("lat", "lon")),
            P(None, None, ("lat", "lon")),
            P(None, None, ("lat", "lon")),
            P(None, None, ("lat", "lon")),
        ),
        check_vma=False,
    )
```

```python
import functools

import jax
import jax.numpy as jnp
import numpy as np
from jax import lax
from jax.experimental import pallas as pl
from jax.experimental.pallas import tpu as pltpu
from jax.sharding import PartitionSpec as P

HEADS = 16
WLAT = 6
WLON = 12
LEV = 2
C = 512
FF = 2048
T = LEV * WLAT * WLON
QUAD = T // 4
SLOT = 48
NORM_EPS = 1e-05
MESH = pl.DeviceIdType.MESH
BF = jnp.bfloat16
F32 = jnp.float32


def quadrant_order():
    return [
        (l, 3 * a + r, 6 * b + c)
        for a in range(2)
        for b in range(2)
        for l in range(LEV)
        for r in range(3)
        for c in range(6)
    ]


def permutations():
    slots_of_natural = np.zeros((4 * SLOT, T), np.float32)
    tokens_of_slots = np.zeros((T, 4 * SLOT), np.float32)
    tokens_of_padded = np.zeros((T, 12 * 16), np.float32)
    for t, (l, r, c) in enumerate(quadrant_order()):
        slot = t // QUAD * SLOT + t % QUAD
        slots_of_natural[slot, (r * WLON + c) * LEV + l] = 1
        tokens_of_slots[t, slot] = 1
        tokens_of_padded[t, (l * WLAT + r) * 16 + c] = 1
    spread = np.zeros((32 * 16, 32 * WLON), np.float32)
    for col in range(32 * WLON):
        spread[col // WLON * 16 + col % WLON, col] = 1
    swap = np.eye(1024, dtype=np.float32).reshape(8, 8, 16, 1024).swapaxes(0, 1).reshape(1024, 1024)
    matrices = (slots_of_natural, tokens_of_slots, tokens_of_padded, spread, swap)
    return [jnp.asarray(m, BF) for m in matrices]


def nn(a, b):
    return lax.dot_general(a, b, (((1,), (0,)), ((), ())), preferred_element_type=F32)


def nt(a, b):
    return lax.dot_general(a, b, (((1,), (1,)), ((), ())), preferred_element_type=F32)


def tn(a, b):
    return lax.dot_general(a, b, (((0,), (0,)), ((), ())), preferred_element_type=F32)


def norm(x):
    centred = x - jnp.mean(x, -1, keepdims=True)
    rstd = lax.rsqrt(jnp.mean(centred * centred, -1, keepdims=True) + NORM_EPS)
    return centred * rstd, rstd


def norm_back(dn, nhat, rstd):
    return rstd * (
        dn - jnp.mean(dn, -1, keepdims=True) - nhat * jnp.mean(dn * nhat, -1, keepdims=True)
    )


def layers_kernel(
    enc_hbm, up_hbm, son_hbm, tos_hbm, ton_hbm, spread_hbm, swap_hbm,
    wqkv_hbm, wproj_hbm, wup_hbm, wdown_hbm,
    mixed_hbm, denc_hbm, oqkv_hbm, oproj_hbm, oup_hbm, odown_hbm,
    enc_ref, up_ref, son_ref, tos_ref, ton_ref, spread_ref, in_sem,
    mixed_ref, denc_ref, oqkv_ref, oproj_ref, oup_ref, odown_ref, out_sem,
    wqkv, wproj, wup, wdown, wsem,
    swap, leave, came, leave2, came2, lane_send, lane_recv, nat2, turned, send, recv, send_sem, recv_sem,
    xs, n1h, n1, r1, us, ps, att, seen, n2h, n2, r2, gp, hs, acc, eq, ep, eu, ed, dab,
    pn1, patt, pn2, phs, peq, pep, peu, ped, pair_send, pair_recv,
    part, fwd, fsum, side, plane_out, plane_in, ring_send, ring_recv, plane_send, plane_recv,
):
    i, j = lax.axis_index("lat"), lax.axis_index("lon")
    nlat, nlon = lax.axis_size("lat"), lax.axis_size("lon")

    def device(di, dj):
        return (lax.rem(i + di + nlat, nlat), lax.rem(j + dj + nlon, nlon))

    core, z, y = lax.rem(i, 2), lax.rem(j, 4), j // 8
    x = i // 2 * 2 + lax.rem(j // 4, 2)

    def along(axis, steps):
        at = {"x": x, "y": y, "z": z}
        at[axis] = lax.rem(at[axis] + steps + 4, 4)
        return (at["x"] // 2 * 2 + core, at["y"] * 8 + lax.rem(at["x"], 2) * 4 + at["z"])

    def beside(axis, steps, other, others):
        at = {"x": x, "y": y, "z": z}
        at[axis] = lax.rem(at[axis] + steps + 4, 4)
        at[other] = lax.rem(at[other] + others + 4, 4)
        return (at["x"] // 2 * 2 + core, at["y"] * 8 + lax.rem(at["x"], 2) * 4 + at["z"])

    partner = (i + 1 - 2 * core, j)

    weights = ((wqkv_hbm, wqkv), (wproj_hbm, wproj), (wup_hbm, wup), (wdown_hbm, wdown))
    inputs = {}
    for at, (name, src, dst) in enumerate(
        (
            ("enc", enc_hbm, enc_ref), ("spread", spread_hbm, spread_ref), ("up", up_hbm, up_ref),
            ("son", son_hbm, son_ref), ("tos", tos_hbm, tos_ref), ("ton", ton_hbm, ton_ref),
            ("swap", swap_hbm, swap),
        )
    ):
        inputs[name] = pltpu.make_async_copy(src, dst, in_sem.at[at])
    inputs["enc"].start()
    inputs["spread"].start()
    fetches = [
        pltpu.make_async_copy(src.at[k], dst.at[k], wsem.at[k, w]) for k in range(2) for w, (src, dst) in enumerate(weights)
    ]

    barrier = pltpu.get_barrier_semaphore()
    far = lambda xl, dy, dz: (lax.rem(i + 2, 4), lax.rem(y + dy, 4) * 8 + xl * 4 + lax.rem(z + dz, 4))
    greeted = [device(1, 0), device(-1, 0), device(1, 1), device(-1, -1)]
    greeted += [far(xl, 0, dz) for xl in range(2) for dz in range(4)]
    greeted += [far(xl, dy, 0) for xl in range(2) for dy in (1, 2, 3)]
    for other in greeted:
        pl.semaphore_signal(barrier, inc=1, device_id=other, device_id_type=MESH)

    for step in range(1, nlon):
        pl.semaphore_signal(barrier, inc=1, device_id=device(0, step), device_id_type=MESH)

    for name in ("up", "son", "tos", "ton", "swap"):
        inputs[name].start()
    for fetch in fetches:
        fetch.start()

    inputs["enc"].wait()
    inputs["spread"].wait()
    columns_first = nt(spread_ref[...], enc_ref[...].reshape(12 * 16, 32 * WLON)).astype(BF)
    leave[:, 0] = columns_first[:, 0:128].reshape(32, 16, 128)
    leave[:, 1, :, 0:64] = columns_first[:, 128:192].reshape(32, 16, 64)
    leave[:, 1, :, 64:128] = jnp.zeros((32, 16, 64), BF)
    pl.semaphore_wait(barrier, len(greeted) + nlon - 1)
    mine = pl.ds(pl.multiple_of(lax.rem(j, 8) * 128, 128), 128)

    def lane_copy(step, event):
        to = lax.rem(j + step, nlon)
        if event == 0:
            src, dst = leave.at[to], came.at[:, j // 8, :, mine]
        else:
            src, dst = leave2.at[to], came2.at[j]
        return pltpu.make_async_remote_copy(
            src_ref=src, dst_ref=dst, send_sem=lane_send.at[event], recv_sem=lane_recv.at[event],
            device_id=(i, to), device_id_type=MESH,
        )

    def lane_start(event):
        for step in range(1, nlon):
            lane_copy(step, event).start()

        if event == 0:
            src, dst = leave.at[j], came.at[:, j // 8, :, mine]
        else:
            src, dst = leave2.at[j], came2.at[j]
        pltpu.make_async_copy(src, dst, lane_recv.at[event]).start()

    def lane_finish(event):
        await_bytes((came, came2)[event], lane_recv.at[event])
        await_bytes((leave, leave2)[event].at[pl.ds(0, 31)], lane_send.at[event])

    lane_start(0)

    def remote(src, dst, sems, to):
        pltpu.make_async_remote_copy(
            src_ref=src, dst_ref=dst, send_sem=sems[0], recv_sem=sems[1], device_id=to, device_id_type=MESH
        ).start()

    def await_bytes(like, sem):
        pltpu.make_async_copy(like, like, sem).wait()

    wide = {"eq": 384, "ep": 128, "eu": 512, "ed": 128}
    whole = {"n1": (n1, pn1), "att": (att, patt), "n2": (n2, pn2), "hs": (hs, phs)}
    cut = {"eq": (eq, peq), "ep": (ep, pep), "eu": (eu, peu), "ed": (ed, ped)}

    def columns(name, hi, owner):
        width = wide[name]
        return pl.ds(pl.multiple_of((2 * hi + owner) * width, width), width)

    names = ("n1", "att", "n2", "hs", "eq", "ep", "eu", "ed")

    def give(k, name):
        sems = (pair_send.at[k, names.index(name)], pair_recv.at[k, names.index(name)])
        if name in whole:
            src, dst = whole[name]
            remote(src.at[k], dst.at[k], sems, partner)
        else:
            src, dst = cut[name]
            for hi in range(2):
                remote(src.at[k, :, columns(name, hi, 1 - core)], dst.at[k, hi], sems, partner)

    def taken(k, name, sems):
        dst = (whole[name] if name in whole else cut[name])[1]
        await_bytes(dst.at[k], sems.at[k, names.index(name)])

    def take(k, name):
        taken(k, name, pair_recv)

    orders = ("xyz", "xyz", "yxz", "yxz", "zyx", "zyx")
    where = {"x": x, "y": y, "z": z}

    def chunk(k, p, t, half):
        return part.at[k, p, lax.rem(t + 4, 4), pl.ds(2 * half, 2)]

    def f32(ref):
        return ref[...].astype(F32)

    def ring_start(k, p):
        axis = orders[p][0]
        t = where[axis]
        after, before = along(axis, 1), along(axis, -1)
        out = ring_send.at[k, p]
        remote(chunk(k, p, t + 2, 0), fwd.at[k, p, 0], (out, ring_recv.at[k, p, 0]), after)
        remote(chunk(k, p, t + 2, 1), fwd.at[k, p, 1], (out, ring_recv.at[k, p, 1]), before)
        remote(chunk(k, p, t + 1, 1), side.at[k, p, 0, pl.ds(2, 2)], (out, ring_recv.at[k, p, 2]), after)
        remote(chunk(k, p, t - 1, 0), side.at[k, p, 1, pl.ds(0, 2)], (out, ring_recv.at[k, p, 2]), before)

    def ring_mid(k, p):
        axis = orders[p][0]
        t = where[axis]
        after, before = along(axis, 1), along(axis, -1)
        sems = (ring_send.at[k, p], ring_recv.at[k, p, 2])
        await_bytes(fwd.at[k, p, 0], ring_recv.at[k, p, 0])
        fsum[k, p, 0] = (f32(fwd.at[k, p, 0]) + f32(chunk(k, p, t + 1, 0))).astype(BF)
        remote(fsum.at[k, p, 0], side.at[k, p, 0, pl.ds(0, 2)], sems, after)
        await_bytes(fwd.at[k, p, 1], ring_recv.at[k, p, 1])
        fsum[k, p, 1] = (f32(fwd.at[k, p, 1]) + f32(chunk(k, p, t - 1, 1))).astype(BF)
        remote(fsum.at[k, p, 1], side.at[k, p, 1, pl.ds(2, 2)], sems, before)

    def plane_copy(k, p, count, step):
        _, second, third = orders[p]
        d2, d3 = divmod(step, 4)
        held = pl.ds(p % 2, count)
        src = plane_out.at[k, p // 2, lax.rem(where[second] + d2, 4), lax.rem(where[third] + d3, 4), held]
        return pltpu.make_async_remote_copy(
            src_ref=src, dst_ref=plane_in.at[k, p // 2, step, held], send_sem=plane_send.at[k, p],
            recv_sem=plane_recv.at[k, p], device_id=beside(second, d2, third, d3), device_id_type=MESH,
        )

    def plane_start(k, p, count):
        planes.append((k, p, count))

        for step in range(1, 16):
            plane_copy(k, p, count, step).start()

    planes = []

    def plane_bytes(k, p, count):
        return plane_in.at[k, p // 2, pl.ds(1, 15), pl.ds(p % 2, count)]

    def plane_arrive(k, p, count):
        await_bytes(plane_bytes(k, p, count), plane_recv.at[k, p])

    def ring_end(k, p):
        await_bytes(side.at[k, p], ring_recv.at[k, p, 2])
        t = where[orders[p][0]]
        total = f32(part.at[k, p, t]) + f32(side.at[k, p, 0]) + f32(side.at[k, p, 1])
        for s2 in range(4):
            for s3 in range(4):
                if p in (0, 2):
                    rows = (total[s2, 12 * s3 : 12 * s3 + 12], total[s2, 48 + 4 * s3 : 52 + 4 * s3])
                    rows = jnp.concatenate(rows, 0)
                elif p in (4, 5):
                    rows = total[s2, 16 * s3 : 16 * s3 + 16]
                else:
                    rows = [total[s2, 16 * hb + 4 * s3 : 16 * hb + 4 * s3 + 4] for hb in range(4)]
                    rows = jnp.concatenate(rows, 0)
                plane_out[k, p // 2, s2, s3, p % 2] = rows.astype(BF)

    def ring_last(k, p):
        _, second, third = orders[p]
        total = f32(plane_out.at[k, p // 2, where[second], where[third], p % 2])
        for step in range(1, 16):
            total += f32(plane_in.at[k, p // 2, step, p % 2])
        half = p % 2 if p in (4, 5) else p // 2
        lanes = slice(256 * half, 256 * half + 256)
        if p in (0, 2):
            oqkv_ref[:, k, lanes] = total[0:12]
            oproj_ref[k, :, lanes] = total[12:16]
        elif p in (4, 5):
            oup_ref[k, :, lanes] = total
        else:
            for hb in range(4):
                at = slice(hb * C + lanes.start, hb * C + lanes.stop)
                odown_ref[k, :, at] = total[4 * hb : 4 * hb + 4]

    def both(k, name, hi, own, theirs):
        src, dst = cut[name]
        return tn(src[k, :, columns(name, hi, core)], own) + tn(dst[k, hi], theirs)

    def keep(k, p, first, second, rows, g):
        for s in range(2):
            q = p + s if p == 4 else p + 2 * s
            at = (first, second) if orders[q][0] == orders[p][0] else (second, first)
            part[k, q, at[0], at[1], rows, :] = g[:, 256 * s : 256 * s + 256]

    def grads_a(k):
        for name in ("att", "ep", "n1"):
            take(k, name)
        for hi in range(2):
            g = both(k, "ep", hi, att[k], patt[k]).astype(BF)
            for at in range(8):
                keep(k, 0, 2 * hi + at % 2, at // 2, slice(48, 64), g[16 * at : 16 * at + 16])
        take(k, "eq")
        for hi in range(2):
            g = both(k, "eq", hi, n1[k], pn1[k]).astype(BF)
            for at in range(8):
                keep(k, 0, 2 * hi + at % 2, at // 2, slice(0, 48), g[48 * at : 48 * at + 48])
        ring_start(k, 0)
        ring_start(k, 2)

    def grads_b(k):
        for name in ("n2", "eu"):
            take(k, name)
        for hi in range(2):
            g = both(k, "eu", hi, n2[k], pn2[k]).astype(BF)
            for at in range(32):
                row = (2 * hi + at // 4 % 2) * 16
                keep(k, 4, at % 4, at // 8, slice(row, row + 16), g[16 * at : 16 * at + 16])
        ring_start(k, 4)
        ring_start(k, 5)

    def grads_c(k):
        for name in ("hs", "ed"):
            take(k, name)
        for hi in range(2):
            for hb in range(4):
                cols = slice(hb * C, hb * C + C)
                g = both(k, "ed", hi, hs[k, :, cols], phs[k, :, cols]).astype(BF)
                for at in range(8):
                    row = 16 * hb
                    keep(k, 1, 2 * hi + at % 2, at // 2, slice(row, row + 16), g[16 * at : 16 * at + 16])
        ring_start(k, 1)
        ring_start(k, 3)

    def exchange(event, forward):
        for q in range(4):
            a, b = q // 2, q % 2
            di, dj = (a - 1, b - 1) if forward else (a, b)
            if (di, dj) == (0, 0):
                recv[event, 3 - q] = send[event, q]
            else:
                sems = (send_sem.at[event], recv_sem.at[event])
                remote(send.at[event, q], recv.at[event, 3 - q], sems, device(di, dj))

    def arrive(event):
        await_bytes(recv.at[event, pl.ds(0, 3)], recv_sem.at[event])

    def put(event, tokens):
        send[event] = tn(tos_ref[...], tokens).astype(BF).reshape(4, SLOT, C)

    def got(event):
        return nn(tos_ref[...], recv[event].reshape(4 * SLOT, C))

    for name in ("up", "son", "tos", "ton"):
        inputs[name].wait()
    send[0] = nn(son_ref[...], up_ref[...].reshape(T, C)).astype(BF).reshape(4, SLOT, C)
    exchange(0, True)

    lane = lax.broadcasted_iota(jnp.int32, (1, 128), 1)
    head_mask = [((lane >= 32 * s) & (lane < 32 * s + 32)).astype(BF) for s in range(4)]
    half_t = lax.broadcasted_iota(jnp.int32, (T, T), 0) < T // 2
    half_s = lax.broadcasted_iota(jnp.int32, (T, T), 1) < T // 2
    one = jnp.where((i == nlat - 1) & (half_t != half_s), 0.0, 1.0).astype(F32)
    for s in range(4):
        seen[T * s : T * s + T] = one
    inside = [(lane >= 32 * s) & (lane < 32 * s + 32) for s in range(4)]
    two = lax.broadcasted_iota(jnp.int32, (128, 128), 1) < 2
    ones_two = jnp.where(two, 1.0, 0.0).astype(BF)
    minus_two = jnp.where(lax.broadcasted_iota(jnp.int32, (T, 128), 1) < 2, -1.0, 0.0).astype(BF)

    def forward(k, x):
        xs[k] = x
        nhat, rstd = norm(x)
        n1h[k] = nhat
        r1[k] = jnp.broadcast_to(rstd, (T, 128))
        n1[k] = nhat.astype(BF)
        give(k, "n1")
        fetches[4 * k].wait()

        for s in range(3):
            cols = slice(s * C, s * C + C)
            us[k, :, cols] = nn(n1[k], wqkv[k, :, cols]).astype(BF)

        for g in range(4):
            def part(w):
                return us[k, :, pl.ds(w * C + g * 128, 128)]

            q, key, v = part(0), part(1), part(2)
            stacked = jnp.concatenate([q * m for m in head_mask], 0)
            e = jnp.exp2(nt(stacked, key) * (32**-0.5 / np.log(2.0)))
            if k == 1:
                e = e * seen[...]
            p = ((e * (1.0 / (0.25 * jnp.sum(e, -1, keepdims=True)))) * 0.25).astype(BF)
            ps[k, g] = p
            out = nn(p, v)
            total = jnp.zeros((T, 128), F32)
            for s in range(4):
                total += jnp.where(inside[s], out[T * s : T * s + T], 0.0)
            att[k, :, pl.ds(g * 128, 128)] = total.astype(BF)

        give(k, "att")
        fetches[4 * k + 1].wait()
        m = xs[k] + nn(att[k], wproj[k])
        acc[...] = m
        nhat, rstd = norm(m)
        n2h[k] = nhat
        r2[k] = jnp.broadcast_to(rstd, (T, 128))
        n2[k] = nhat.astype(BF)
        give(k, "n2")
        fetches[4 * k + 2].wait()
        fetches[4 * k + 3].wait()

        for s in range(4):
            cols = slice(s * C, s * C + C)
            z = nn(n2[k], wup[k, :, cols])
            cdf = 0.5 * (1.0 + lax.erf(z * (2.0**-0.5)))
            gp[k, :, cols] = cdf + z * (jnp.exp(-0.5 * z * z) * ((2.0 * np.pi) ** -0.5))
            h = (z * cdf).astype(BF)
            hs[k, :, cols] = h
            acc[...] += nn(h, wdown[k, cols, :])

        give(k, "hs")
        return acc[...]

    def backward(k, ct, after_up, after_proj, amid):
        acc[...] = ct
        ed[k] = ct.astype(BF)
        give(k, "ed")

        for s in range(4):
            cols = slice(s * C, s * C + C)
            dh = nt(ed[k], wdown[k, cols, :]).astype(BF).astype(F32)
            eu[k, :, cols] = (dh * gp[k, :, cols]).astype(BF)

        give(k, "eu")
        grads_c(k)
        after_up()
        dn2 = nt(eu[k], wup[k]).astype(BF).astype(F32)
        dm = acc[...] + norm_back(dn2, n2h[k], r2[k][:, 0:1])
        acc[...] = dm
        ep[k] = dm.astype(BF)
        give(k, "ep")
        grads_b(k)
        dab[...] = nt(ep[k], wproj[k]).astype(BF)
        after_proj()

        def heads(g):
            def at(w):
                return slice(w * C + g * 128, w * C + g * 128 + 128)

            q, key, v = us[k, :, at(0)], us[k, :, at(1)], us[k, :, at(2)]
            da = dab[:, at(0)]
            prod = da.astype(F32) * att[k, :, at(0)].astype(F32)
            high = prod.astype(BF)
            low = (prod - high.astype(F32)).astype(BF)
            stacked_da = jnp.concatenate([da * m for m in head_mask], 0)
            sums = nn(jnp.concatenate([high * m for m in head_mask], 0), ones_two)
            sums += nn(jnp.concatenate([low * m for m in head_mask], 0), ones_two)
            sums_high = sums.astype(BF).astype(F32)
            sums = jnp.where(lane == 0, sums_high, sums - sums_high).astype(BF)
            p = ps[k, g]
            dp = nt(jnp.concatenate([stacked_da, sums], 1), jnp.concatenate([v, minus_two], 1))
            ds = (p.astype(F32) * dp).astype(BF)
            dv = tn(p, stacked_da)
            dk = tn(ds, jnp.concatenate([q * m for m in head_mask], 0))
            out = nn(ds, key)
            dq = jnp.zeros((T, 128), F32)
            for s in range(4):
                dq += jnp.where(inside[s], out[T * s : T * s + T], 0.0)
            eq[k, :, at(0)] = (dq * (32**-0.5)).astype(BF)
            eq[k, :, at(1)] = (dk * (32**-0.5)).astype(BF)
            eq[k, :, at(2)] = dv.astype(BF)

        for half in range(2):
            for g in range(2 * half, 2 * half + 2):
                heads(g)
            if half == 1:
                give(k, "eq")
            amid(half)

    def backward_end(k):
        dn1 = nt(eq[k], wqkv[k]).astype(BF).astype(F32)
        return acc[...] + norm_back(dn1, n1h[k], r1[k][:, 0:1])

    def nothing():
        pass

    inputs["swap"].wait()
    lane_finish(0)
    for half in range(2):
        moved = nn(came[half].reshape(64, 1024), swap[:, 0 : 1024 - 512 * half]).astype(BF)
        for lr in range(8 if half == 0 else 4):
            for g in range(4):
                at = (slice(128 * half + 16 * lr, 128 * half + 16 * lr + 16), slice(128 * g, 128 * g + 128))
                nat2[at] = moved[16 * g : 16 * g + 16, 128 * lr : 128 * lr + 128]
    first = forward(0, nn(ton_ref[...], nat2[...]))
    put(1, first.astype(BF))
    exchange(1, True)
    arrive(1)
    second = forward(1, got(1))
    put(2, second.astype(BF))
    exchange(2, False)
    arrive(0)

    def mids(k, parts):
        for p in parts:
            ring_mid(k, p)

    def ends(k, parts):
        for p in parts:
            ring_end(k, p)

    def lasts(k, parts):
        for p in parts:
            ring_last(k, p)

    def amid_one(half):
        if half == 1:
            mids(1, (1, 3))

    backward(1, got(0), nothing, nothing, amid_one)
    d_second = backward_end(1)
    put(3, d_second.astype(BF))
    exchange(3, False)
    grads_a(1)
    mids(1, (4, 5))
    arrive(3)

    def up_zero():
        mids(1, (0, 2))

    def proj_zero():
        ends(1, (1, 3, 4, 5))
        plane_start(1, 4, 2)

    def amid_zero(half):
        if half == 0:
            ends(1, (0, 2))
            plane_start(1, 0, 2)
            plane_start(1, 2, 2)
            mids(0, (1, 3))
        else:
            mids(0, (4, 5))

    backward(0, got(3), up_zero, proj_zero, amid_zero)
    d_first = backward_end(0).astype(BF)
    grads_a(0)
    nat2[...] = tn(ton_ref[...], d_first).astype(BF)
    for half in range(2):
        for lr in range(8 if half == 0 else 4):
            for g in range(4):
                at = (slice(16 * g, 16 * g + 16), slice(128 * lr, 128 * lr + 128))
                row = 128 * half + 16 * lr
                turned[half, at[0], at[1]] = nat2[row : row + 16, 128 * g : 128 * g + 128]
        moved = nn(turned[half, :, 0 : 1024 - 512 * half], swap[0 : 1024 - 512 * half]).astype(BF)
        for g in range(4):
            for lane_block in range(8):
                leave2[8 * g + lane_block, half] = moved[
                    16 * g : 16 * g + 16, 128 * lane_block : 128 * lane_block + 128
                ]
    mids(0, (0, 2))
    lane_start(1)
    ends(0, (1, 3))
    plane_start(0, 1, 1)
    plane_start(0, 3, 1)
    ends(0, (4, 5))
    plane_start(0, 4, 2)
    arrive(2)
    natural = tn(son_ref[...], recv[2].reshape(4 * SLOT, C)).astype(BF)
    mixed_ref[...] = natural.reshape(T // LEV, LEV, C)
    stores = []

    def store(src, dst):
        stores.append(pltpu.make_async_copy(src, dst, out_sem.at[len(stores)]))
        stores[-1].start()

    store(mixed_ref, mixed_hbm)
    ends(0, (0, 2))
    plane_start(0, 0, 1)
    plane_start(0, 2, 1)
    for group in (0, 2, 4):
        plane_arrive(1, group, 2)
    lasts(1, range(6))
    plane_arrive(0, 1, 1)
    plane_arrive(0, 3, 1)
    plane_arrive(0, 4, 2)
    lasts(0, (1, 3, 4, 5))
    store(oup_ref, oup_hbm)
    store(odown_ref, odown_hbm)
    lane_finish(1)
    for half in range(2):
        rows = tn(came2[:, half].reshape(512, 128), spread_ref[...]).astype(BF)
        n = 8 if half == 0 else 4
        denc_ref[8 * half : 8 * half + n] = rows[0 : 16 * n].reshape(n, 16, 32 * WLON)
    store(denc_ref, denc_hbm)
    plane_arrive(0, 0, 1)
    plane_arrive(0, 2, 1)
    lasts(0, (0, 2))
    store(oqkv_ref, oqkv_hbm)
    store(oproj_ref, oproj_hbm)
    for event in range(4):
        await_bytes(send.at[event, pl.ds(0, 3)], send_sem.at[event])
    for k in range(2):
        for name in names:
            taken(k, name, pair_send)
        for p in range(6):
            await_bytes(part.at[k, p, pl.ds(0, 3)], ring_send.at[k, p])
    for k, p, count in planes:
        await_bytes(plane_bytes(k, p, count), plane_send.at[k, p])
    for copy in stores:
        copy.wait()


def copies_kernel(*refs):
    for n in range(6):
        refs[6 + n][...] = refs[n][...]


def layers(encoded, upstream, w_qkv, w_proj, w_up, w_down):
    hbm = pl.BlockSpec(memory_space=pl.ANY)
    vmem = pl.BlockSpec(memory_space=pltpu.VMEM)
    dma = pltpu.SemaphoreType.DMA
    V = pltpu.VMEM
    shapes = (
        jax.ShapeDtypeStruct((T // LEV, LEV, C), BF),
        jax.ShapeDtypeStruct((12, 16, 32 * WLON), BF),
        jax.ShapeDtypeStruct((12, 2, C), F32),
        jax.ShapeDtypeStruct((2, 4, C), F32),
        jax.ShapeDtypeStruct((2, 16, C), F32),
        jax.ShapeDtypeStruct((2, 4, FF), F32),
    )
    results = pl.pallas_call(
        layers_kernel,
        out_shape=shapes,
        in_specs=[hbm] * 11,
        out_specs=(hbm,) * 6,
        scratch_shapes=[
            V((12, 16, 32 * WLON), BF), V((T // LEV, LEV, C), BF), V((4 * SLOT, T), BF), V((T, 4 * SLOT), BF),
            V((T, 12 * 16), BF), V((512, 32 * WLON), BF), dma((7,)),
            *[V(shape.shape, shape.dtype) for shape in shapes], dma((6,)),
            V((2, C, 3 * C), BF), V((2, C, C), BF), V((2, C, FF), BF), V((2, FF, C), BF),
            dma((2, 4)),
            V((1024, 1024), BF), V((32, 2, 16, 128), BF), V((2, 4, 16, 1024), BF),
            V((32, 2, 16, 128), BF), V((32, 2, 16, 128), BF), dma((2,)), dma((2,)),
            V((12 * 16, C), BF), V((2, 64, 1024), BF),
            V((4, 4, SLOT, C), BF), V((4, 4, SLOT, C), BF),
            dma((4,)), dma((4,)),
            V((2, T, C), F32), V((2, T, C), F32), V((2, T, C), BF), V((2, T, 128), F32),
            V((2, T, 3 * C), BF), V((2, 4, 4 * T, T), BF), V((2, T, C), BF),
            V((4 * T, T), F32),
            V((2, T, C), F32), V((2, T, C), BF), V((2, T, 128), F32),
            V((2, T, FF), F32), V((2, T, FF), BF), V((T, C), F32),
            V((2, T, 3 * C), BF), V((2, T, C), BF), V((2, T, FF), BF), V((2, T, C), BF), V((T, C), BF),
            V((2, T, C), BF), V((2, T, C), BF), V((2, T, C), BF), V((2, T, FF), BF),
            V((2, 2, T, 384), BF), V((2, 2, T, 128), BF), V((2, 2, T, 512), BF), V((2, 2, T, 128), BF),
            dma((2, 8)), dma((2, 8)),
            V((2, 6, 4, 4, 64, 256), BF), V((2, 6, 2, 2, 64, 256), BF), V((2, 6, 2, 2, 64, 256), BF),
            V((2, 6, 2, 4, 64, 256), BF), V((2, 3, 4, 4, 2, 16, 256), BF), V((2, 3, 16, 2, 16, 256), BF),
            dma((2, 6)), dma((2, 6, 3)), dma((2, 6)), dma((2, 6)),
        ],
        compiler_params=pltpu.CompilerParams(
            collective_id=0, has_side_effects=True, vmem_limit_bytes=60 * 2**20
        ),
    )(encoded, upstream, *permutations(), w_qkv, w_proj, w_up, w_down)
    return pl.pallas_call(
        copies_kernel,
        out_shape=shapes,
        in_specs=[vmem] * 6,
        out_specs=(vmem,) * 6,
    )(*results)


def on_device(encoded, upstream, w_qkv, w_proj, w_up, w_down):
    mixed, dencoded, qkv, proj, up, down = layers(
        encoded.reshape(12, 16, 32 * WLON),
        upstream.transpose(1, 2, 0, 3).reshape(T // LEV, LEV, C),
        w_qkv, w_proj, w_up, w_down,
    )
    return (
        mixed.reshape(WLAT, WLON, LEV, C).transpose(2, 0, 1, 3),
        dencoded.reshape(encoded.shape),
        qkv.transpose(1, 2, 0),
        proj.swapaxes(1, 2),
        up.swapaxes(1, 2),
        down.swapaxes(1, 2),
    )


def solution(mesh):
    return jax.shard_map(
        on_device,
        mesh=mesh,
        in_specs=(P(None, "lat", "lon", None), P(None, "lat", "lon", None), P(), P(), P(), P()),
        out_specs=(
            P(None, "lat", "lon", None),
            P(None, "lat", "lon", None),
            P(None, None, ("lat", "lon")),
            P(None, None, ("lat", "lon")),
            P(None, None, ("lat", "lon")),
            P(None, None, ("lat", "lon")),
        ),
        check_vma=False,
    )
```
